32 devices in a mesh: dp: 8 (over y, x, core), mp: 4 (over z).
Axes of the slice: x: 2, y: 2, z: 4, core: 2. Of those that a mesh axis runs over, the one named last changes fastest.
Arguments:
- activations: bfloat16 [16384, 1024], P('dp'), may hold values from -6 to 6
- noise_embed: bfloat16 [128, 256], P('dp'), may hold values from -6 to 6
- lengths: int32 [128], P('dp'), may hold values from 0 to 1024, as said below
- time_weight: bfloat16 [256, 1024], replicated, may hold values from -0.375 to 0.375
- time_bias: float32 [1024], replicated, may hold values from -4 to 4
- attn_gain: float32 [1024], replicated, may hold values from 0.5 to 1.5
- qkv_weight: bfloat16 [1024, 3, 1024], P(None, None, 'mp'), may hold values from -0.25 to 0.25
- qkv_bias: float32 [3, 1024], P(None, 'mp'), may hold values from -4 to 4
- out_weight: bfloat16 [1024, 1024], P('mp'), may hold values from -0.75 to 0.75
- out_bias: float32 [1024], replicated, may hold values from -4 to 4
- mlp_gain: float32 [1024], replicated, may hold values from 0.5 to 1.5
- up_weight: bfloat16 [1024, 4096], P(None, 'mp'), may hold values from -0.1875 to 0.1875
- up_bias: float32 [4096], P('mp'), may hold values from -4 to 4
- down_weight: bfloat16 [4096, 1024], P('mp'), may hold values from -0.125 to 0.125
- down_bias: float32 [1024], replicated, may hold values from -4 to 4
- cotangent: bfloat16 [16384, 1024], P('dp'), may hold values from -6 to 6
Outputs:
- layer_output: bfloat16 [16384, 1024], P('dp')
- grad_input: float32 [16384, 1024], P('dp')
- grad_time_weight: float32 [256, 1024], replicated
- grad_time_bias: float32 [1024], replicated
- grad_attn_gain: float32 [1024], replicated
- grad_qkv_weight: float32 [1024, 3, 1024], P(None, None, 'mp')
- grad_qkv_bias: float32 [3, 1024], P(None, 'mp')
- grad_out_weight: float32 [1024, 1024], P('mp')
- grad_out_bias: float32 [1024], replicated
- grad_mlp_gain: float32 [1024], replicated
- grad_up_weight: float32 [1024, 4096], P(None, 'mp')
- grad_up_bias: float32 [4096], P('mp')
- grad_down_weight: float32 [4096, 1024], P('mp')
- grad_down_bias: float32 [1024], replicated
The draws below stay inside these ranges and needn't reach their ends.
Inputs may be any that keep to these rules, and one draw needn't show every extreme that they name: In each bucket the sequences lie packed in slot order from the bucket's first row, their lengths summing to at most 1024; rows after them are padding; empty slots have length 0 and come last; some bucket holds one sequence of exactly 1024 rows.
All inputs are finite; a program needn't handle non-finite values.
Results may differ from the reference program's by a relative error of at most 0.019.
Values may be sent and summed in bfloat16 or wider, within the bound.
A program may use at most 256 MiB of HBM per device.

```python
import math
import jax
import jax.numpy as jnp
from jax import lax

D = 1024
HEADS = 16
HEAD = 64
FF = 4096
TIME = 256
BUCKET = 1024
SLOTS = 8
SEQS = 128
TOKENS = 16384
N_MP = 4


def draw_lengths(key, part):
    key = jax.random.fold_in(key, 11)
    subkeys = jax.random.split(key, 3)
    bucket_total = SEQS // SLOTS
    unit_len = max(BUCKET // 64, 1)
    powers = jax.random.randint(subkeys[0], (bucket_total, SLOTS), 0, 5)
    wanted = unit_len * jnp.left_shift(jnp.ones_like(powers), powers) + jax.random.randint(subkeys[1], (bucket_total, SLOTS), 0, unit_len)
    before = jnp.cumsum(wanted, axis=1) - wanted
    fitted = jnp.clip(BUCKET - before, 0, wanted)
    chosen = jax.random.randint(subkeys[2], (), 0, bucket_total)
    whole_row = jnp.where(jnp.arange(SLOTS) == 0, BUCKET, 0)
    fitted = jnp.where((jnp.arange(bucket_total) == chosen)[:, None], whole_row[None, :], fitted)
    return fitted.reshape(SEQS).astype(jnp.int32)


def shard_levels(own_key, extent, pieces, low, largest):
    loudness, own = 1.0, jax.random.fold_in(own_key, 6)
    for position, shards_of in pieces:
        steps = jnp.exp(jax.random.uniform(jax.random.fold_in(own, position), (shards_of,), jnp.float32, low / len(pieces), largest / len(pieces)))
        loudness = loudness * jnp.repeat(steps, extent[position] // shards_of).reshape([-1 if axis == position else 1 for axis in range(len(extent))])
    return loudness


def normal_values(own_key, shape, deviation, most, cuts=(), dtype=jnp.bfloat16):
    drawn = jax.random.normal(own_key, shape, jnp.float32) * deviation
    if len(cuts) > 0:
        drawn = shard_levels(own_key, shape, cuts, -0.22, 0.18) * drawn
    return jnp.clip(drawn, min=-most, max=most).astype(dtype)


def setup_inputs(seed: int = 0) -> dict:
    seeds = jax.random.split(jax.random.key(seed), 17)
    return {
        "activations": normal_values(seeds[0], (TOKENS, D), 1.0, 6.0, ((0, 8),)),
        "noise_embed": normal_values(seeds[1], (SEQS, TIME), 1.0, 6.0, ((0, 8),)),
        "lengths": draw_lengths(jax.random.fold_in(seeds[16], 71), 0),
        "time_weight": normal_values(seeds[3], (TIME, D), TIME ** -0.5, 0.375),
        "time_bias": normal_values(seeds[4], (D,), 0.3, 4.0, (), jnp.float32),
        "attn_gain": jnp.clip(1.0 + 0.1 * jax.random.normal(seeds[5], (D,), jnp.float32), 0.5, 1.5),
        "qkv_weight": normal_values(seeds[6], (D, 3, D), (D // 2) ** -0.5, 0.25, ((2, 4),)),
        "qkv_bias": normal_values(seeds[7], (3, D), 0.3, 4.0, ((1, 4),), jnp.float32),
        "out_weight": normal_values(seeds[8], (D, D), (D // 16) ** -0.5, 0.75, ((0, 4),)),
        "out_bias": normal_values(seeds[9], (D,), 0.3, 4.0, (), jnp.float32),
        "mlp_gain": jnp.clip(1.0 + 0.1 * jax.random.normal(seeds[10], (D,), jnp.float32), 0.5, 1.5),
        "up_weight": normal_values(seeds[11], (D, FF), D ** -0.5, 0.1875, ((1, 4),)),
        "up_bias": normal_values(seeds[12], (FF,), 0.3, 4.0, ((0, 4),), jnp.float32),
        "down_weight": normal_values(seeds[13], (FF, D), (FF // 2) ** -0.5, 0.125, ((0, 4),)),
        "down_bias": normal_values(seeds[14], (D,), 0.3, 4.0, (), jnp.float32),
        "cotangent": normal_values(seeds[15], (TOKENS, D), 1.0, 6.0, ((0, 8),)),
    }


highest = lax.Precision.HIGHEST

@jax.custom_vjp
def low(v):
    return lax.optimization_barrier(v.astype(jnp.bfloat16)).astype(jnp.float32)

@jax.custom_vjp
def low_back(v):
    return v

def low_keep(v):
    return (low(v), None)

def low_pass(kept, grad):
    return (grad,)

def back_keep(v):
    return (v, None)

def back_low(kept, grad):
    return (low(grad),)
low.defvjp(low_keep, low_pass)
low_back.defvjp(back_keep, back_low)

def layout(lens_b):
    seq_ends = jnp.cumsum(lens_b).astype(jnp.int32)
    starts = seq_ends - lens_b.astype(jnp.int32)
    places = jnp.arange(BUCKET).astype(jnp.int32)
    inside = (places[:, None] >= starts[None, :]) & (places[:, None] < seq_ends[None, :])
    member = inside.astype(jnp.float32)
    live_rows = lax.optimization_barrier(jnp.sum(member, axis=1))
    where_at = (places - lax.optimization_barrier(jnp.sum(jnp.where(inside, starts[None, :], 0), axis=1))).astype(jnp.float32)
    segment = lax.optimization_barrier(jnp.sum((places[:, None] >= seq_ends[None, :]).astype(jnp.int32), axis=1))
    allowed = (segment[:, None] == segment[None, :]) & (live_rows[None, :] > 0.5) | (places[:, None] == places[None, :])
    return (member, live_rows, where_at, allowed)

def layer_norm(field, norm_gain):
    centered = field - lax.optimization_barrier(jnp.mean(field, axis=-1, keepdims=True))
    return centered * lax.rsqrt(lax.optimization_barrier(jnp.mean(centered * centered, axis=-1, keepdims=True)) + 1e-05) * norm_gain

def rotate(field, cosine, sine_of):
    half_dim = field.shape[-1] // 2
    first_half = field[..., :half_dim]
    second_half = field[..., half_dim:]
    return jnp.concatenate([first_half * cosine - second_half * sine_of, second_half * cosine + first_half * sine_of], axis=-1)

def smooth_gelu(field):
    return 0.5 * field * (1.0 + jnp.tanh(0.7978845608028654 * (field + 0.044715 * field * field * field)))

def bucket_forward(params, bucket_item):
    time_weight, time_bias, attn_gain, qkv_weight, qkv_bias, out_weight, out_bias, mlp_gain, up_weight, up_bias, down_weight, down_bias = params
    rows_in, noise_rows, lens_b = bucket_item
    member, live_rows, where_at, allowed = layout(lens_b)
    frequency = jnp.exp(jnp.arange(HEAD // 2).astype(jnp.float32) * (-2.0 * math.log(10000.0) / HEAD))
    angles = where_at[:, None] * frequency[None, :]
    cosine = jnp.cos(angles)[:, None, :]
    sine_of = jnp.sin(angles)[:, None, :]
    time_rows = jnp.dot(noise_rows, time_weight, precision=highest) + time_bias
    stream_in = rows_in + jnp.dot(member, time_rows, precision=highest)
    normed = low(layer_norm(stream_in, attn_gain))
    width_here = D // N_MP
    heads_here = HEADS // N_MP
    attn_total = jnp.zeros_like(stream_in)
    for group_idx in range(N_MP):
        columns = slice(group_idx * width_here, (group_idx + 1) * width_here)
        shared = low_back(normed)
        projected = low_back(jnp.einsum('td,dcw->ctw', shared, qkv_weight[:, :, columns], precision=highest) + qkv_bias[:, None, columns])
        shaped = projected.reshape(3, BUCKET, heads_here, HEAD)
        queries = low(rotate(shaped[0], cosine, sine_of))
        key_rows = low(rotate(shaped[1], cosine, sine_of))
        values = low(shaped[2])
        raw_scores = low_back(jnp.einsum('qhk,shk->hqs', queries, key_rows, precision=highest)) * 0.125
        masked = jnp.where(allowed[None], raw_scores, -1e+30)
        shifted = masked - lax.optimization_barrier(jnp.max(masked, axis=-1, keepdims=True))
        powers = jnp.exp(shifted)
        weights = low(powers / lax.optimization_barrier(jnp.sum(powers, axis=-1, keepdims=True)))
        attended = jnp.einsum('hqs,shk->qhk', weights, values, precision=highest).reshape(BUCKET, width_here)
        merged = low(low_back(attended))
        attn_total = attn_total + low(low_back(jnp.dot(merged, out_weight[columns, :], precision=highest)))
    middle = stream_in + attn_total + out_bias
    normed_mlp = low(layer_norm(middle, mlp_gain))
    hidden_width = FF // N_MP
    mlp_total = jnp.zeros_like(middle)
    for group_idx in range(N_MP):
        columns = slice(group_idx * hidden_width, (group_idx + 1) * hidden_width)
        shared = low_back(normed_mlp)
        pre_act = low_back(jnp.dot(shared, up_weight[:, columns], precision=highest) + up_bias[columns])
        activated = low(smooth_gelu(pre_act))
        mlp_total = mlp_total + low(low_back(jnp.dot(activated, down_weight[columns, :], precision=highest)))
    return live_rows[:, None] * (middle + mlp_total + down_bias)

def reference(activations, noise_embed, lengths, time_weight, time_bias, attn_gain, qkv_weight, qkv_bias, out_weight, out_bias, mlp_gain, up_weight, up_bias, down_weight, down_bias, cotangent):
    params = tuple((tensor.astype(jnp.float32) for tensor in (time_weight, time_bias, attn_gain, qkv_weight, qkv_bias, out_weight, out_bias, mlp_gain, up_weight, up_bias, down_weight, down_bias)))
    bucket_total = TOKENS // BUCKET
    noise_rows = noise_embed.astype(jnp.float32).reshape(bucket_total, SLOTS, TIME)
    lens_all = lengths.reshape(bucket_total, SLOTS)
    rows_in = activations.astype(jnp.float32).reshape(bucket_total, BUCKET, D)
    bucket_step = jax.checkpoint(bucket_forward)

    def whole_layer(weights_in, rows_all):

        def scan_step(scan_carry, bucket_item):
            return (scan_carry, bucket_step(weights_in, bucket_item))
        unused, outputs = lax.scan(scan_step, jnp.zeros((), jnp.float32), (rows_all, noise_rows, lens_all))
        return outputs
    outputs, pullback = jax.vjp(whole_layer, params, rows_in)
    grad_params, grad_rows = pullback(cotangent.astype(jnp.float32).reshape(bucket_total, BUCKET, D))
    return (outputs.reshape(TOKENS, D).astype(jnp.bfloat16), grad_rows.reshape(TOKENS, D), grad_params[0], grad_params[1], grad_params[2], grad_params[3], grad_params[4], grad_params[5], grad_params[6], grad_params[7], grad_params[8], grad_params[9], grad_params[10], grad_params[11])
```

```python
import functools
import math

import jax
import jax.numpy as jnp
import numpy as np
from jax import lax
from jax.experimental import pallas as pl
from jax.experimental.pallas import tpu as pltpu
from jax.sharding import PartitionSpec as P

HEAD = 64
BUCKET = 1024
SLOTS = 8
MIB = 1 << 20
MESH = pl.DeviceIdType.MESH
VMEM = pltpu.VMEM
bf16 = jnp.bfloat16
f32 = jnp.float32


def contract(a, b, ca, cb):
    return lax.dot_general(a, b, (((ca,), (cb,)), ((), ())), preferred_element_type=f32)


def tile(i, n):
    return pl.ds(pl.multiple_of(i * n, n), n)


def loop(n, body):
    def step(i, carry):
        body(i)
        return carry

    lax.fori_loop(0, n, step, 0)


def row_stats(v):
    centered = v - jnp.mean(v, axis=-1, keepdims=True)
    return centered, lax.rsqrt(jnp.mean(centered * centered, axis=-1, keepdims=True) + 1e-05)


def norm_back(v, gain, err):
    centered, scale = row_stats(v)
    xhat = centered * scale
    u = err * gain
    grad = (
        u - jnp.mean(u, axis=-1, keepdims=True) - xhat * jnp.mean(u * xhat, axis=-1, keepdims=True)
    ) * scale
    return grad, jnp.sum(err * xhat, axis=0, keepdims=True)


def toggled(v, bit):
    return v + bit - 2 * bit * lax.rem(v // bit, 2)


def peer(z, m):
    low = lax.rem(lax.rem(z, 2) + m % 2, 2)
    return low + 2 * lax.rem(z // 2 + m // 2, 2)


def greet(targets):
    barrier = pltpu.get_barrier_semaphore()
    for d, z in targets:
        pl.semaphore_signal(barrier, inc=1, device_id={"dp": d, "mp": z}, device_id_type=MESH)
    pl.semaphore_wait(barrier, len(targets))


def remote(src, dst, ss, rs, d, z):
    return pltpu.make_async_remote_copy(
        src_ref=src,
        dst_ref=dst,
        send_sem=ss,
        recv_sem=rs,
        device_id={"dp": d, "mp": z},
        device_id_type=MESH,
    )


class Spread:
    def __init__(self, src, out, near_sem, send_sem, recv_sem):
        me, z = lax.axis_index("dp"), lax.axis_index("mp")
        self.core = core = lax.rem(me, 2)
        self.kind = kind = z // 2
        self.place = z + core * (3 - 2 * z)
        self.start_place = z + kind * (3 - 2 * z)
        self.out, self.send, self.recv = out, send_sem, recv_sem
        self.me, self.z, self.ahead = me, z, z + 1 - 2 * core
        keeper = me - core + kind
        dst = self.piece(self.start_place, core, kind)
        rs = recv_sem.at[2 * self.start_place + core]
        self.near = pltpu.make_async_copy(src, dst, near_sem.at[0])
        self.first = [
            remote(src, dst, send_sem.at[0], rs, keeper, z + 1 - 2 * kind),
            remote(src, dst, send_sem.at[1], rs, keeper, z - 1 + 2 * kind),
            remote(src, dst, send_sem.at[2], rs, toggled(me, 1), z),
        ]

    def piece(self, m, h, kind):
        rows = self.out.shape[0] // 4
        at = 2 * (m + kind * (1 - 2 * m)) + h
        return self.out.at[pl.ds(pl.multiple_of(at * rows, rows), rows), :]

    def hop(self, m, h, i):
        ref = self.piece(m, h, self.core)
        return remote(ref, ref, self.send.at[i], self.recv.at[2 * m + h], self.me, self.ahead)

    def begin(self):
        self.first[0].start()

        @pl.when(self.start_place == 1)
        def _():
            self.first[1].start()

        @pl.when(self.core == self.kind)
        def _():
            self.near.start()

        @pl.when(self.core != self.kind)
        def _():
            self.first[2].start()

    def forward(self, place, m, i):
        @pl.when(self.place == place)
        def _():
            for h in range(2):
                self.hop(m, h, i + h).wait_recv()
                self.hop(m, h, i + h).start()

    def pass_first(self):
        self.forward(1, 0, 3)
        self.forward(2, 1, 3)

    def pass_second(self):
        self.forward(2, 0, 5)

    def finish(self):
        @pl.when(self.core == self.kind)
        def _():
            self.near.wait()
            self.hop(self.place, 1 - self.core, 3).wait_recv()

        @pl.when(self.core != self.kind)
        def _():
            self.first[2].wait_send()

        @pl.when(self.place == 0)
        def _():
            for h in range(2):
                self.hop(1, h, 3).wait_recv()

        @pl.when(self.place == 3)
        def _():
            for m in range(2):
                for h in range(2):
                    self.hop(m, h, 3).wait_recv()

        self.first[0].wait_send()

        @pl.when(self.start_place == 1)
        def _():
            self.first[1].wait_send()

        for place, m, i in ((1, 0, 3), (2, 1, 3), (2, 0, 5)):

            @pl.when(self.place == place)
            def _(m=m, i=i):
                for h in range(2):
                    self.hop(m, h, i + h).wait_send()


class PlaneSum:
    def __init__(self, src, keep, got, last, load_sem, send_sem, recv_sem):
        me, z = lax.axis_index("dp"), lax.axis_index("mp")
        self.x, self.y = lax.rem(me // 2, 2), lax.rem(me // 4, 2)
        self.z, self.across, self.along = z, toggled(me, 2), toggled(me, 4)
        self.src, self.keep, self.got, self.last = src, keep, got, last
        self.load_sem, self.send_sem, self.recv_sem = load_sem, send_sem, recv_sem

    def part(self, u, order, mine):
        x = self.x if mine else 1 - self.x
        y = self.y if mine else 1 - self.y
        return self.src.at[u, :, :, x, 0] if order == 0 else self.src.at[u, :, y, :, 1]

    def load(self, u, order):
        return pltpu.make_async_copy(
            self.part(u, order, True), self.keep.at[order, u], self.load_sem.at[order, u]
        )

    def hop(self, u, order, stage):
        if stage == 0:
            src, dst = self.part(u, order, False), self.got.at[order, u]
        else:
            there = 1 - (self.y if order == 0 else self.x)
            src, dst = self.keep.at[order, u, :, there], self.last.at[order, u]
        to = self.across if order == stage else self.along
        return remote(
            src, dst, self.send_sem.at[order, stage, u], self.recv_sem.at[order, stage, u], to, self.z
        )

    def begin(self, u):
        for order in range(2):
            self.load(u, order).start()
            self.hop(u, order, 0).start()

    def middle(self, u):
        for order in range(2):
            self.load(u, order).wait()
            self.hop(u, order, 0).wait_recv()
            total = self.keep[order, u].astype(f32) + self.got[order, u].astype(f32)
            self.keep[order, u] = total.astype(bf16)
            self.hop(u, order, 1).start()

    def end(self, u, put):
        for order in range(2):
            self.hop(u, order, 1).wait_recv()
            here = self.y if order == 0 else self.x
            total = self.keep[order, u, :, here].astype(f32) + self.last[order, u].astype(f32)
            put(u, order, total.astype(bf16))

    def drain(self, u):
        for order in range(2):
            for stage in range(2):
                self.hop(u, order, stage).wait_send()


class LineSum:
    def __init__(self, own, got, send_sem, recv_sem):
        self.me, self.z = lax.axis_index("dp"), lax.axis_index("mp")
        self.own, self.got, self.send_sem, self.recv_sem = own, got, send_sem, recv_sem

    def hop(self, way, t):
        entry = t if way == 0 else 3 - t
        return remote(
            self.own.at[entry], self.got.at[way, t - 1], self.send_sem.at[way, t - 1],
            self.recv_sem.at[way, t - 1], self.me, self.z + 1 - 2 * way,
        )

    def step(self, s):
        for way in range(2):

            @pl.when(self.z == (s if way == 0 else 3 - s))
            def _(way=way):
                for t in range(3, s, -1):
                    if s > 0:
                        self.hop(way, t).wait_recv()
                        entry = t if way == 0 else 3 - t
                        total = self.own[entry].astype(f32) + self.got[way, t - 1].astype(f32)
                        self.own[entry] = total.astype(bf16)
                    self.hop(way, t).start()

    def finish(self, put):
        for way in range(2):
            for t in range(1, 4):

                @pl.when(self.z == (t if way == 0 else 3 - t))
                def _(way=way, t=t):
                    self.hop(way, t).wait_recv()
                    entry = t if way == 0 else 3 - t
                    total = self.own[entry].astype(f32) + self.got[way, t - 1].astype(f32)
                    self.own[entry] = total.astype(bf16)

        put(self.own[self.z])
        for way in range(2):
            for s in range(3):

                @pl.when(self.z == (s if way == 0 else 3 - s))
                def _(way=way, s=s):
                    for t in range(3, s, -1):
                        self.hop(way, t).wait_send()


class PlaneGather:
    def __init__(self, final, parts, rows, own_sem, send_sem, recv_sem):
        me, self.z = lax.axis_index("dp"), lax.axis_index("mp")
        self.core, self.col = lax.rem(me, 2), lax.rem(me // 2, 4)
        self.other, self.across, self.along = toggled(me, 1), toggled(me, 2), toggled(me, 4)
        self.parts, self.rows = parts, rows
        self.send_sem, self.recv_sem = send_sem, recv_sem
        self.cols = (
            self.col, toggled(self.col, 1), toggled(self.col, 2), toggled(toggled(self.col, 1), 2),
        )
        src = final.at[pl.ds(rows[0], rows[1]), :]
        self.near = pltpu.make_async_copy(src, self.slot(self.core, self.col), own_sem)
        self.hops = [
            self.hop(self.slot(self.core, self.col), 4, self.across, src),
            self.hop(self.slot(self.core, self.col), 5, self.along, src),
            self.hop(self.slot(self.core, self.col), 0, self.other, src),
        ]

    def slot(self, c, s, h=None):
        at, n = self.rows
        if h is not None:
            at, n = at + h * (n // 2), n // 2
        return self.parts.at[c, s, pl.ds(at, n), :]

    def hop(self, dst, i, to, src=None):
        src = dst if src is None else src
        return remote(src, dst, self.send_sem.at[i], self.recv_sem.at[i], to, self.z)

    def begin(self):
        for c in self.hops:
            c.start()
        self.near.start()

    def pass_on(self):
        for j, (i, ahead, h, k) in enumerate(((4, self.along, 0, 6), (5, self.across, 1, 7))):
            s = self.cols[1 + j]
            self.hop(self.slot(self.core, s), i, self.other).wait_recv()
            more = [
                self.hop(self.slot(self.core, s, h), k, ahead),
                self.hop(self.slot(self.core, s), 1 + j, self.other),
            ]
            for c in more:
                c.start()
            self.hops += more

    def finish(self):
        s = self.cols[3]
        for h in range(2):
            self.hop(self.slot(self.core, s, h), 6 + h, self.other).wait_recv()
        last = self.hop(self.slot(self.core, s), 3, self.other)
        last.start()
        self.near.wait()
        for i in range(4):
            self.hop(self.slot(1 - self.core, self.cols[i]), i, self.other).wait_recv()
        for c in self.hops + [last]:
            c.wait_send()


class SmallSum:
    def __init__(self, mine, pair, line, across, along, out, send_sem, recv_sem):
        me, self.z = lax.axis_index("dp"), lax.axis_index("mp")
        self.me, self.core = me, lax.rem(me, 2)
        self.x, self.y = lax.rem(me // 2, 2), lax.rem(me // 4, 2)
        self.mine, self.pair, self.line, self.a, self.b, self.out = mine, pair, line, across, along, out
        self.send_sem, self.recv_sem = send_sem, recv_sem
        n = pair.shape[1]
        self.n = n
        self.lanes = pl.ds(pl.multiple_of(self.core * n, n), n)
        there = pl.ds(pl.multiple_of((1 - self.core) * n, n), n)

        def move(src, dst, i, d, z):
            return remote(src, dst, send_sem.at[i], recv_sem.at[i], d, z)

        other = toggled(me, 1)
        self.swap = move(mine.at[:, there], pair, 0, other, self.z)
        slot = line.at[self.z]
        self.hops = [move(slot, slot, m, me, peer(self.z, m)) for m in (1, 2, 3)]
        self.hop_x = move(across.at[self.x], across.at[self.x], 4, toggled(me, 2), self.z)
        self.hop_y = move(along.at[self.y], along.at[self.y], 5, toggled(me, 4), self.z)
        done = out.at[:, self.lanes]
        self.last = move(done, done, 6, other, self.z)

    def begin(self):
        self.swap.start()

    def step_line(self, noise):
        n, width = self.n, noise.shape[1]
        self.swap.wait()
        self.line[self.z, :, 0:n] = self.mine[:, self.lanes] + self.pair[...]
        self.line[self.z, 16:24, n : n + width] = noise
        self.line[self.z, 0:16, n : n + width] = jnp.zeros((16, width), f32)
        for c in self.hops:
            c.start()

    def step_across(self):
        for c in self.hops:
            c.wait()
        v = [self.line[i] for i in range(4)]
        self.a[self.x, 0:16, :] = ((v[0] + v[1]) + (v[2] + v[3]))[0:16]
        for i in range(4):
            self.a[self.x, 16 + 8 * i : 24 + 8 * i, :] = v[i][16:24]
        self.hop_x.start()

    def step_along(self):
        self.hop_x.wait()
        self.b[self.y, 0:16, :] = self.a[0, 0:16, :] + self.a[1, 0:16, :]
        for i in range(2):
            self.b[self.y, 16 + 32 * i : 48 + 32 * i, :] = self.a[i, 16:48, :]
        self.hop_y.start()

    def step_out(self):
        self.hop_y.wait()
        n, n_time = self.n, self.out.shape[0] - 16
        self.out[n_time : n_time + 16, self.lanes] = self.b[0, 0:16, 0:n] + self.b[1, 0:16, 0:n]
        rows = jnp.concatenate([self.b[0, 16:80, :], self.b[1, 16:80, :]])
        grads, noise = rows[:, 0:n], rows[:, n : n + n_time].astype(bf16)
        high = grads.astype(bf16)
        rest = grads - high.astype(f32)
        middle = rest.astype(bf16)
        low = (rest - middle.astype(f32)).astype(bf16)
        total = contract(noise, high, 0, 0) + contract(noise, middle, 0, 0)
        self.out[0:n_time, self.lanes] = total + contract(noise, low, 0, 0)
        self.last.start()

    def finish(self):
        self.last.wait()


def one_hot(seg, copies):
    lanes = lax.broadcasted_iota(jnp.int32, (1, 128), 1)
    lanes = jnp.where(lanes < 16 * copies, lax.rem(lanes, 16), -1).astype(f32)
    return jnp.where(seg == lanes, 1.0, 0.0).astype(bf16)


def rotate_rows(v, cosine, sine):
    a, b = v[: HEAD // 2], v[HEAD // 2 :]
    return jnp.concatenate([a * cosine - b * sine, b * cosine + a * sine], axis=0)


def forward_kernel(
    act_any, cot_any, lens, noise, time_weight, time_bias, attn_gain, out_bias, mlp_gain, down_bias,
    qkv_bias, up_bias, freq, qkv_any, ow_any, uw_any, dn_any,
    out_any, gmid_any, gm_any, stream_any, normed_any, q_any, k_any, v_any, merged_any, lse_any,
    dwm_any, wqo_any, small, bias_rows, seg_col, trig, meta,
    w, x, gfin, bias, biases, stream, normed, qt, kt, vt, merged, lse, send, recv, mid, nm, act, gp, gm,
    stage, lo, gmid, raw_qkv, acc,
    load_sem, bring_send, bring_recv, bias_send, bias_recv, w_send, w_recv,
    out_sem, stage_sem, send_sem, recv_sem,
):
    me, z = lax.axis_index("dp"), lax.axis_index("mp")
    core, col = lax.rem(me, 2), lax.rem(me // 2, 4)
    other, across, along = toggled(me, 1), toggled(me, 2), toggled(me, 4)
    here = act_any.shape[0] // BUCKET
    units = biases.shape[0]
    half = BUCKET // 2
    own, far = tile(core, half), tile(1 - core, half)
    mine = core == z // here
    up_at, dn_at, out_at = units * 512, units * 1024, units * 384

    def block(start, n):
        return pl.ds(pl.multiple_of(start, n), n)

    loads = [
        pltpu.make_async_copy(s, d, load_sem.at[i])
        for i, (s, d) in enumerate(
            (
                (qkv_any.at[:, :, block(core * 128, 128)], raw_qkv),
                (ow_any.at[block(core * 128, 128), :], w.at[block(out_at + z * 128, 128), :]),
                (uw_any.at[:, block(core * 512, 512)], nm.at[:, pl.ds(0, 512)]),
                (dn_any.at[block(core * 512, 512), :], w.at[block(dn_at + z * 512, 512), :]),
            )
        )
    ]
    for c in loads:
        c.start()
    greet([(other, z), (across, z), (along, z)] + [(me, peer(z, m)) for m in (1, 2, 3)])

    bucket_at = lax.rem(z, here)
    bucket = pl.ds(pl.multiple_of(bucket_at * BUCKET, BUCKET), BUCKET)
    brought = (
        (meta, meta),
        (act_any.at[bucket, :], x),
        (cot_any.at[bucket, :], gfin),
    )

    def bring(i, begin):
        src, dst = brought[i]
        near = None if i == 0 else pltpu.make_async_copy(src, dst, load_sem.at[4 + i])
        sent = remote(src, dst, bring_send.at[i], bring_recv.at[i], other, z)

        @pl.when(mine)
        def _():
            if begin:
                sent.start()
                if near is not None:
                    near.start()
            else:
                if near is not None:
                    near.wait()
                sent.wait_send()

        if not begin:

            @pl.when(jnp.logical_not(mine))
            def _():
                sent.wait_recv()

    bring(1, True)
    for c in range(2):

        @pl.when(core == c)
        def _(c=c):
            bias[0:3, :] = qkv_bias[:, c * 128 : (c + 1) * 128]
            bias[3:4, :] = jnp.zeros((1, 128), f32)
            bias[4:8, :] = up_bias[c * 4 : (c + 1) * 4, :]

    biases[z] = bias[...]
    bias_hops = [
        remote(bias, biases.at[z], bias_send.at[m - 1], bias_recv.at[m - 1], me, peer(z, m))
        for m in (1, 2, 3)
    ]

    def row_of(k, u, s):
        if k == 0:
            return u * 384 + 128 * s + (s // 3) * (out_at - 384 + 128 * u - 384 * u)
        return (up_at if k == 1 else dn_at) + u * 512 + 128 * s

    def hop(k, m, way):
        i = 3 * k + m - 1
        u = peer(z, m)
        if way == 0:
            at, n, d, zz = row_of(k, z, col), 128, me, u
        elif way == 1:
            at, n, d, zz = row_of(k, u, col), 128, across, z
        elif way == 2:
            at, n, d, zz = row_of(k, u, col), 128, along, z
        elif way == 3:
            at, n, d, zz = row_of(k, u, toggled(col, 1)), 64, along, z
        else:
            at, n, d, zz = row_of(k, u, toggled(col, 2)) + 64, 64, across, z
        rows = w.at[block(at, n), :]
        return remote(rows, rows, w_send.at[i, way], w_recv.at[i, way], d, zz)

    def arrived(k, m, way):
        i = 3 * k + m - 1
        u = peer(z, m)
        s = (col, toggled(col, 1), toggled(col, 2), toggled(toggled(col, 1), 2), toggled(toggled(col, 1), 2))[way]
        at = row_of(k, u, s) + (64 if way == 4 else 0)
        rows = w.at[block(at, 128 if way < 3 else 64), :]
        remote(rows, rows, w_send.at[i, way], w_recv.at[i, way], other, z).wait_recv()

    def send_z(k, *ms):
        for m in ms:
            hop(k, m, 0).start()

    def pass_a(k, m):
        arrived(k, m, 0)
        hop(k, m, 1).start()
        hop(k, m, 2).start()

    def pass_b(k, m):
        arrived(k, m, 1)
        hop(k, m, 3).start()
        arrived(k, m, 2)
        hop(k, m, 4).start()

    def pass_c(k, m):
        arrived(k, m, 3)
        arrived(k, m, 4)

    loads[0].wait()
    for i in range(3):
        w[block(z * 384 + i * 128, 128), :] = raw_qkv[i].T
    loads[1].wait()
    send_z(0, 1)

    @pl.when(mine)
    def _():
        places = lax.broadcasted_iota(jnp.int32, (1, BUCKET), 1)
        past, start, end = jnp.zeros_like(places), jnp.zeros_like(places), 0
        for i in range(SLOTS):
            end = end + lens[bucket_at * SLOTS + i]
            beyond = places >= end
            past = past + beyond.astype(jnp.int32)
            start = jnp.where(beyond, end, start)
        live = places < end
        meta[8:9, :] = jnp.where(live, past, 2000 + places).astype(f32)
        meta[9:10, :] = (places - jnp.where(live, start, 0)).astype(f32)
        rows = jnp.dot(noise[...], time_weight[...], preferred_element_type=f32) + time_bias[...]
        first = bucket_at == 0
        meta[0:8, :] = jnp.where(first, rows[0:SLOTS], rows[SLOTS : 2 * SLOTS])
        loud = noise[...].astype(f32)
        meta[16:24, 0 : loud.shape[1]] = jnp.where(first, loud[0:SLOTS], loud[SLOTS : 2 * SLOTS])

    bring(0, True)
    bring(2, True)
    for c in bias_hops:
        c.start()
    loads[2].wait()
    for i in range(4):
        w[block(up_at + z * 512 + i * 128, 128), :] = nm[:, i * 128 : (i + 1) * 128].T
    loads[3].wait()
    send_z(1, 1)

    saves = []

    def save(src, dst):
        c = pltpu.make_async_copy(src, dst, out_sem.at[len(saves)])
        c.start()
        saves.append(c)

    def swap(src, dst, i):
        c = remote(src, dst, send_sem.at[i], recv_sem.at[i], other, z)
        c.start()
        return c

    bring(0, False)
    seg_col[...] = jnp.broadcast_to(meta[8:9, :], (128, BUCKET)).T
    angles = freq[:, 0:1] * meta[9:10, :]
    trig[0:32, :] = jnp.cos(angles)
    trig[32:64, :] = jnp.sin(angles)
    t_rows = meta[0:8, :]
    high = t_rows.astype(bf16).astype(f32)
    middle_part = (t_rows - high).astype(bf16).astype(f32)
    lowest = t_rows - high - middle_part
    gap = jnp.zeros((8, t_rows.shape[1]), f32)
    time_rows = jnp.concatenate(
        [high, gap, middle_part, gap, lowest, gap, jnp.zeros((80, t_rows.shape[1]), f32)]
    ).astype(bf16)
    bring(1, False)

    def enter(i):
        rs = tile(i, 256)
        added = jnp.dot(one_hot(seg_col[rs, :], 3), time_rows, preferred_element_type=f32)
        stream[rs, :] = x[rs, :].astype(f32) + added

    loop(4, enter)

    def norm(i):
        rs = tile(i, 128)
        centered, scale = row_stats(stream[rs, :])
        normed[rs, :] = (centered * scale * attn_gain[...]).astype(bf16)

    loop(8, norm)
    save(normed, normed_any)
    save(stream.at[own, :], stream_any)
    stream_saved = saves[-1]

    def bias_column(u, s):
        return jnp.broadcast_to(biases[u, s : s + 1, :], (128, 128)).T[:, 0:1]

    def unit(u):
        column = jnp.concatenate([bias_column(u, s) for s in range(3)], axis=0)
        proj = contract(w[block(u * 384, 384), :], normed[...], 1, 1) + column
        cs, sn = trig[0:32, :], trig[32:64, :]
        us = tile(u, 128)
        qt[us, :] = jnp.concatenate(
            [rotate_rows(proj[h * HEAD : (h + 1) * HEAD], cs, sn) for h in range(2)], axis=0
        ).astype(bf16)
        kt[us, :] = jnp.concatenate(
            [rotate_rows(proj[128 + h * HEAD : 128 + (h + 1) * HEAD], cs, sn) for h in range(2)],
            axis=0,
        ).astype(bf16)
        vt[us, :] = proj[256:384].astype(bf16)

        def head(j):
            h = 2 * u + j
            hs = tile(h, HEAD)
            keys = (kt[hs, :].astype(f32) * 0.125).T.astype(bf16)
            values = vt[hs, :]
            for t in range(2):
                cs_t = pl.ds(t * 512, 512)
                s = jnp.dot(keys, qt[hs, cs_t], preferred_element_type=f32)
                same = jnp.tile(seg_col[...], (1, 4)) == meta[8:9, cs_t]
                s = jnp.where(same, s, -1e30)
                top = jnp.max(s, axis=0, keepdims=True)
                p = jnp.exp(s - top)
                total = jnp.sum(p, axis=0, keepdims=True)
                o = jnp.dot(values, p.astype(bf16), preferred_element_type=f32)
                merged[hs, cs_t] = (o / total).astype(bf16)
                lse[h, :, cs_t] = top + jnp.log(total)

        loop(2, head)

    pass_a(0, 1)
    send_z(0, 2, 3)
    unit(z)
    pass_a(1, 1)
    pass_b(0, 1)
    for c in bias_hops:
        c.wait()
    pass_c(0, 1)
    unit(peer(z, 1))
    pass_a(0, 2)
    pass_a(0, 3)
    pass_b(1, 1)
    send_z(2, 1)
    send_z(1, 2)
    pass_b(0, 2)
    pass_c(0, 2)
    unit(peer(z, 2))
    pass_b(0, 3)
    pass_a(2, 1)
    pass_a(1, 2)
    send_z(2, 2)
    send_z(1, 3)
    pass_c(1, 1)
    pass_c(0, 3)
    unit(peer(z, 3))
    pass_b(2, 1)
    save(qt, q_any)
    save(kt, k_any)
    save(vt, v_any)
    save(merged, merged_any)
    save(lse, lse_any)
    save(w.at[pl.ds(0, up_at), :], wqo_any)

    w_out = w.at[pl.ds(out_at, units * 128), :]
    w_up = w.at[pl.ds(up_at, units * 512), :]
    w_dn = w.at[pl.ds(dn_at, units * 512), :]
    send[0] = contract(merged[:, far], w_out[...], 0, 0).astype(bf16)
    swap0 = swap(send.at[0], recv.at[0], 0)
    mid[...] = contract(merged[:, own], w_out[...], 0, 0)
    bring(2, False)

    def mask(i):
        rs = tile(i, 256)
        live = jnp.where(seg_col[rs, :][:, 0:1] < 1000.0, 1.0, 0.0)
        gfin[rs, :] = (gfin[rs, :].astype(f32) * live).astype(bf16)

    loop(4, mask)
    swap0.wait()

    def middle(i):
        rs = tile(i, 128)
        ro = pl.ds(pl.multiple_of(core * half + i * 128, 128), 128)
        v = stream[ro, :] + (mid[rs, :] + recv[0, rs, :].astype(f32)) + out_bias[...]
        mid[rs, :] = v
        centered, scale = row_stats(v)
        nm[ro, :] = (centered * scale * mlp_gain[...]).astype(bf16)

    loop(4, middle)
    swap1 = swap(nm.at[own, :], nm.at[own, :], 1)
    pass_b(1, 2)
    pass_a(2, 2)
    send_z(2, 3)
    pass_c(2, 1)
    swap1.wait()

    def hidden_unit(n, u):
        us = tile(u, 512)
        column = jnp.concatenate([bias_column(u, 4 + s) for s in range(4)], axis=0)

        def hidden(t):
            rs = tile(t, 256)
            pre = contract(w_up[us, :], nm[rs, :], 1, 1) + column
            ga = contract(w_dn[us, :], gfin[rs, :], 1, 1)
            sq = pre * pre
            th = jnp.tanh(pre * (0.7978845608028654 + (0.7978845608028654 * 0.044715) * sq))
            hp = 0.5 + 0.5 * th
            act[us, rs] = (pre * hp).astype(bf16)
            slope = hp + pre * (hp * (1.0 - th)) * (
                0.7978845608028654 + (3 * 0.7978845608028654 * 0.044715) * sq
            )
            gp[us, rs] = (ga * slope).astype(bf16)

        loop(4, hidden)

    def weights_unit(n, u):
        us = tile(u, 512)
        bias_rows[u, :, 384:896] = contract(jnp.ones((8, BUCKET), bf16), gp[us, :], 1, 1)
        for i, left, right in ((0, gp, nm), (1, act, gfin)):
            if n > 0:
                pltpu.make_async_copy(stage.at[i], dwm_any.at[u, i], stage_sem.at[i]).wait()
            stage[i] = contract(left[us, :], right[...], 1, 0).astype(bf16)
            pltpu.make_async_copy(stage.at[i], dwm_any.at[u, i], stage_sem.at[i]).start()

    def partial_sums(n, u):
        us = tile(u, 512)
        for left, right, kept in ((act, w_dn, stream), (gp, w_up, acc)):
            for rows in (far, own):
                total = contract(left[us, rows], right[us, :], 0, 0)
                if n > 0:
                    total = total + kept[rows, :]
                kept[rows, :] = total

    bias_rows[...] = jnp.zeros_like(bias_rows)
    stream_saved.wait()
    hidden_unit(0, z)
    pass_a(1, 3)
    pass_b(2, 2)
    pass_c(1, 2)
    weights_unit(0, z)
    partial_sums(0, z)
    pass_b(1, 3)
    pass_c(2, 2)
    hidden_unit(1, peer(z, 1))
    pass_a(2, 3)
    weights_unit(1, peer(z, 1))
    partial_sums(1, peer(z, 1))
    pass_c(1, 3)
    hidden_unit(2, peer(z, 2))
    pass_b(2, 3)
    weights_unit(2, peer(z, 2))
    partial_sums(2, peer(z, 2))
    pass_c(2, 3)
    last_unit = peer(z, 3)
    hidden_unit(3, last_unit)
    us = tile(last_unit, 512)
    send[1] = (stream[far, :] + contract(act[us, far], w_dn[us, :], 0, 0)).astype(bf16)
    swap2 = swap(send.at[1], recv.at[1], 2)
    send[2] = (acc[far, :] + contract(gp[us, far], w_up[us, :], 0, 0)).astype(bf16)
    swap3 = swap(send.at[2], recv.at[2], 3)
    gmid[...] = stream[own, :] + contract(act[us, own], w_dn[us, :], 0, 0)
    swap2.wait()

    def finish(i):
        rs = tile(i, 128)
        ro = pl.ds(pl.multiple_of(core * half + i * 128, 128), 128)
        live = jnp.where(seg_col[ro, :][:, 0:1] < 1000.0, 1.0, 0.0)
        v = mid[rs, :] + (gmid[rs, :] + recv[1, rs, :].astype(f32)) + down_bias[...]
        lo[rs, :] = (live * v).astype(bf16)

    loop(4, finish)
    save(lo, out_any)
    gmid[...] = acc[own, :] + contract(gp[us, own], w_up[us, :], 0, 0)
    swap3.wait()
    small[...] = jnp.zeros_like(small)

    def back(i):
        rs = tile(i, 128)
        ro = pl.ds(pl.multiple_of(core * half + i * 128, 128), 128)
        err = gmid[rs, :] + recv[2, rs, :].astype(f32)
        grad, gain_grad = norm_back(mid[rs, :], mlp_gain[...], err)
        gf = gfin[ro, :].astype(f32)
        grad = grad + gf
        gmid[rs, :] = grad
        gm[ro, :] = grad.astype(bf16)
        small[0:1, :] += gain_grad
        small[1:2, :] += jnp.sum(grad, axis=0, keepdims=True)
        small[2:3, :] += jnp.sum(gf, axis=0, keepdims=True)

    loop(4, back)
    swap4 = swap(gm.at[own, :], gm.at[own, :], 4)
    save(gmid, gmid_any)
    weights_unit(3, last_unit)
    swap4.wait()
    save(gm, gm_any)
    for i in range(2):
        pltpu.make_async_copy(stage.at[i], dwm_any.at[0, i], stage_sem.at[i]).wait()
    for c in saves:
        if c is not stream_saved:
            c.wait()
    for k in range(3):
        for m in (1, 2, 3):
            for way in range(5):
                hop(k, m, way).wait_send()


def column_devices(me, z):
    both = (me, toggled(me, 1))
    return [(both[1], z)] + [(d, peer(z, m)) for m in (1, 2, 3) for d in both]


def backward_kernel(
    gather,
    meta, seg_col, trig, attn_gain, small_m, bias_rows, lse,
    wqo_any, gmid_any, gm_any, stream_any, normed_any, q_any, k_any, v_any, merged_any, lo_any, dwm_any,
    out_any, dwa_any, gin_any, gathered_any, parts, sums,
    wqo, gmid, gm, stream, normed, qt, kt, vt, merged,
    gmerged, gproj, acck, accv, send, recv, gin, stage, gin_low, small, mine,
    keep_m, got_m, last_m, keep_a, got_a, last_a, own_m, line_got_m, own_a, line_got_a, final,
    small_pair, small_line, small_x, small_y,
    load_sem, out_sem, stage_sem, send_sem, recv_sem, near_sem,
    lo_send, lo_recv, gin_send, gin_recv, pm_load, pm_send, pm_recv, pa_load, pa_send, pa_recv,
    lm_send, lm_recv, la_send, la_recv, gm_send, gm_recv, ga_send, ga_recv, small_send, small_recv,
):
    me, z = lax.axis_index("dp"), lax.axis_index("mp")
    core, other = lax.rem(me, 2), toggled(me, 1)
    half = BUCKET // 2
    units = wqo.shape[0] // 512
    n_qkv = units * 384
    w_qkv, w_out = pl.ds(0, n_qkv), pl.ds(n_qkv, units * 128)
    loads = {}
    for name, src, dst in (
        ("out", wqo_any.at[w_out, :], wqo.at[w_out, :]),
        ("gm", gm_any, gm),
        ("q", q_any, qt),
        ("k", k_any, kt),
        ("v", v_any, vt),
        ("merged", merged_any, merged),
        ("qkv", wqo_any.at[w_qkv, :], wqo.at[w_qkv, :]),
        ("stream", stream_any, stream),
        ("gmid", gmid_any, gmid),
        ("normed", normed_any, normed),
    ):
        loads[name] = pltpu.make_async_copy(src, dst, load_sem.at[len(loads)])
        loads[name].start()
    wqkv, wout = wqo.at[w_qkv, :], wqo.at[w_out, :]
    cosine, sine = trig.at[pl.ds(0, 32), :], trig.at[pl.ds(32, 32), :]
    greet([(toggled(me, 2), z), (toggled(me, 4), z)] + column_devices(me, z))
    plane_m = PlaneSum(dwm_any, keep_m, got_m, last_m, pm_load, pm_send, pm_recv)
    spread_lo = Spread(lo_any, out_any, near_sem.at[0], lo_send, lo_recv)
    plane_m.begin(0)
    spread_lo.begin()
    plane_m.begin(1)

    def put_m(u, order, total):
        for i in range(2):
            own_m[u, i * 128 + order * 64 : i * 128 + (order + 1) * 64, :] = total[i]

    def put_a(u, order, total):
        own_a[u, order * 64 : (order + 1) * 64, :] = total[0]

    own = tile(core, half)
    far = tile(1 - core, half)
    loads["out"].wait()
    loads["gm"].wait()
    for t in range(2):
        cs = pl.ds(t * 512, 512)
        gmerged[:, cs] = contract(wout[...], gm[cs, :], 1, 1).astype(bf16)
    for name in ("q", "k", "v", "merged"):
        loads[name].wait()

    def head(h):
        hs = tile(h, HEAD)
        u = h // 2
        j = lax.rem(h, 2)
        at = u * 384 + j * HEAD
        keys_t = (kt[hs, :].astype(f32) * 0.125).astype(bf16)
        keys = keys_t.astype(f32).T.astype(bf16)
        values = vt[hs, :].astype(f32).T.astype(bf16)
        for t in range(2):
            cs = pl.ds(t * 512, 512)
            q, go = qt[hs, cs], gmerged[hs, cs]
            dl = jnp.sum(go.astype(f32) * merged[hs, cs].astype(f32), axis=0, keepdims=True)
            s = jnp.dot(keys, q, preferred_element_type=f32)
            same = jnp.tile(seg_col[...], (1, 4)) == meta[8:9, cs]
            p = jnp.exp(jnp.where(same, s, -1e30) - lse[h, :, cs])
            dp = jnp.dot(values, go, preferred_element_type=f32)
            ds = (p * (dp - dl)).astype(bf16)
            dq = jnp.dot(keys_t, ds, preferred_element_type=f32)
            gproj[pl.ds(pl.multiple_of(at, HEAD), HEAD), cs] = rotate_rows(
                dq, cosine[:, cs], -sine[:, cs]
            ).astype(bf16)
            dv = contract(go, p.astype(bf16), 1, 1)
            dk = contract(q, ds, 1, 1)
            if t == 0:
                accv[...] = dv
                acck[...] = dk
            else:
                dk = (acck[...] + dk) * 0.125
                gproj[pl.ds(pl.multiple_of(at + 128, HEAD), HEAD), :] = rotate_rows(
                    dk, cosine[...], -sine[...]
                ).astype(bf16)
                gproj[pl.ds(pl.multiple_of(at + 256, HEAD), HEAD), :] = (accv[...] + dv).astype(bf16)

    def heads(i):
        head(2 * i)
        head(2 * i + 1)

        @pl.when(i == 1)
        def _():
            plane_m.middle(0)
            plane_m.begin(2)
            spread_lo.pass_first()

        @pl.when(i == 2)
        def _():
            plane_m.middle(1)
            plane_m.begin(3)

    loop(units, heads)
    plane_m.end(0, put_m)
    loads["qkv"].wait()
    send[...] = contract(gproj[:, far], wqkv[...], 0, 0).astype(bf16)
    swap = remote(send, recv, send_sem.at[0], recv_sem.at[0], other, z)
    swap.start()
    gin[...] = contract(gproj[:, own], wqkv[...], 0, 0)
    loads["stream"].wait()
    loads["gmid"].wait()
    swap.wait()
    small[...] = jnp.zeros_like(small)

    def back(i):
        rs = tile(i, 128)
        ro = pl.ds(pl.multiple_of(core * half + i * 128, 128), 128)
        err = gin[rs, :] + recv[rs, :].astype(f32)
        grad, gain_grad = norm_back(stream[rs, :], attn_gain[...], err)
        grad = grad + gmid[rs, :]
        high = grad.astype(bf16)
        gin_low[rs, :] = high
        small[0:1, :] += gain_grad
        member = one_hot(seg_col[ro, :], 1)
        low = (grad - high.astype(f32)).astype(bf16)
        small[8:16, :] += (contract(member, high, 0, 0) + contract(member, low, 0, 0))[0:8]

    loop(4, back)
    save = pltpu.make_async_copy(gin_low, gin_any, out_sem.at[0])
    save.start()
    save.wait()
    spread_gin = Spread(gin_any, gathered_any, near_sem.at[1], gin_send, gin_recv)
    spread_gin.begin()
    t_rows = small[8:16, :]
    mine[0:8, :] = jnp.concatenate(
        [
            small_m[0:3, :],
            small[0:1, :],
            jnp.sum(t_rows, axis=0, keepdims=True),
            jnp.zeros((3, t_rows.shape[1]), f32),
        ]
    )
    mine[8:16, :] = jnp.zeros((8, t_rows.shape[1]), f32)
    mine[16:24, :] = t_rows
    plane_m.middle(2)
    plane_m.end(1, put_m)
    loads["normed"].wait()
    plane_a = PlaneSum(dwa_any, keep_a, got_a, last_a, pa_load, pa_send, pa_recv)

    def stored(u):
        return pltpu.make_async_copy(stage.at[u % 2], dwa_any.at[u], stage_sem.at[u % 2])

    def weights(u):
        us = pl.ds(u * 384, 384)
        if u > 1:
            stored(u - 2).wait()
            plane_a.begin(u - 2)
        of_qkv = contract(gproj[us, :], normed[...], 1, 0).astype(bf16)
        of_out = contract(merged[pl.ds(u * 128, 128), :], gm[...], 1, 0).astype(bf16)
        for i in range(4):
            quarter = of_qkv[i * 128 : (i + 1) * 128] if i < 3 else of_out
            for j in range(2):
                stage[u % 2, 0, i // 2, i % 2, j] = quarter[j * 64 : (j + 1) * 64]
        stored(u).start()
        row = lax.broadcasted_iota(jnp.int32, (8, 1), 0) == core * units + u
        mine[8:16, 0:384] += jnp.where(
            row, contract(jnp.ones((8, BUCKET), bf16), gproj[us, :], 1, 1), 0.0
        )
        mine[8:16, 384:896] += jnp.where(row, bias_rows[u, :, 384:896], 0.0)

    for u in range(units):
        weights(u)
    sizes = small_pair, small_line, small_x, small_y
    little = SmallSum(mine, *sizes, sums, small_send, small_recv)
    little.begin()
    for u in range(units - 2, units):
        stored(u).wait()
        plane_a.begin(u)
    spread_lo.pass_second()
    plane_m.middle(3)
    little.step_line(meta[16:24, 0 : sums.shape[0] - 16])
    plane_m.end(2, put_m)
    plane_m.end(3, put_m)
    line_m = LineSum(own_m, line_got_m, lm_send, lm_recv)
    line_a = LineSum(own_a, line_got_a, la_send, la_recv)
    line_m.step(0)
    little.step_across()
    spread_gin.pass_first()
    for u in range(4):
        plane_a.middle(u)
    little.step_along()
    line_m.step(1)
    for u in range(4):
        plane_a.end(u, put_a)
    line_a.step(0)
    little.step_out()
    line_m.step(2)
    spread_gin.pass_second()

    def put_final_m(total):
        final[128:384, :] = total

    def put_final_a(total):
        final[0:128, :] = total

    if gather:
        gather_m = PlaneGather(final, parts, (128, 256), near_sem.at[2, 0], gm_send, gm_recv)
        gather_a = PlaneGather(final, parts, (0, 128), near_sem.at[3, 0], ga_send, ga_recv)
    line_m.finish(put_final_m)
    if gather:
        gather_m.begin()
    line_a.step(1)
    line_a.step(2)
    line_a.finish(put_final_a)
    if gather:
        gather_a.begin()
        gather_m.pass_on()
        gather_a.pass_on()
        gather_m.finish()
        gather_a.finish()
    else:
        out = pltpu.make_async_copy(final, parts, near_sem.at[2, 0])
        out.start()
        out.wait()
    little.finish()
    spread_lo.finish()
    spread_gin.finish()
    for u in range(4):
        plane_m.drain(u)
        plane_a.drain(u)


def deliver_kernel(parts, gin, lo, sums, grad_in, lo_out, time_out, qkv_out, out_out, up_out, down_out):
    s = lax.rem(pl.program_id(0), 4)
    grad_in[...] = gin[...].astype(f32)
    lo_out[...] = lo[...]
    time_out[...] = sums[...]
    down_out[...] = parts[0, 0, 256:384, :].astype(f32)
    up_out[...] = parts[0, 0, 128:256, :].T.astype(f32)

    @pl.when(s < 3)
    def _():
        qkv_out[0] = parts[0, 0, 0:128, :].T.astype(f32)

    @pl.when(s == 3)
    def _():
        out_out[...] = parts[0, 0, 0:128, :].astype(f32)


def shape(s, t):
    return jax.ShapeDtypeStruct(s, t)


def run_forward(args, here, units, width):
    rows = BUCKET
    half = rows // 2
    feat = units * 128
    hid = units * 512
    anyspec = pl.BlockSpec(memory_space=pl.ANY)
    vm = pl.BlockSpec(memory_space=VMEM)
    outs = (
        shape((half, width), bf16),
        shape((half, width), f32),
        shape((rows, width), bf16),
        shape((half, width), f32),
        shape((rows, width), bf16),
        shape((feat, rows), bf16),
        shape((feat, rows), bf16),
        shape((feat, rows), bf16),
        shape((feat, rows), bf16),
        shape((2 * units, 1, rows), f32),
        shape((units, 2, 512, width), bf16),
        shape((hid, width), bf16),
        shape((8, width), f32),
        shape((units, 8, width), f32),
        shape((rows, 128), f32),
        shape((64, rows), f32),
        shape((24, width), f32),
    )
    dma = pltpu.SemaphoreType.DMA
    return pl.pallas_call(
        forward_kernel,
        out_shape=outs,
        in_specs=[anyspec] * 2 + [pl.BlockSpec(memory_space=pltpu.SMEM)] + [vm] * 10 + [anyspec] * 4,
        out_specs=[anyspec] * 12 + [vm] * 5,
        scratch_shapes=[
            VMEM((3 * hid, width), bf16),
            VMEM((rows, width), bf16),
            VMEM((rows, width), bf16),
            VMEM((8, 128), f32),
            VMEM((units, 8, 128), f32),
            VMEM((rows, width), f32),
            VMEM((rows, width), bf16),
            VMEM((feat, rows), bf16),
            VMEM((feat, rows), bf16),
            VMEM((feat, rows), bf16),
            VMEM((feat, rows), bf16),
            VMEM((2 * units, 1, rows), f32),
            VMEM((3, half, width), bf16),
            VMEM((3, half, width), bf16),
            VMEM((half, width), f32),
            VMEM((rows, width), bf16),
            VMEM((hid, rows), bf16),
            VMEM((hid, rows), bf16),
            VMEM((rows, width), bf16),
            VMEM((2, 512, width), bf16),
            VMEM((half, width), bf16),
            VMEM((half, width), f32),
            VMEM((3, width, 128), bf16),
            VMEM((rows, width), f32),
            dma((7,)),
            dma((3,)),
            dma((3,)),
            dma((3,)),
            dma((3,)),
            dma((9, 5)),
            dma((9, 5)),
            dma((12,)),
            dma((2,)),
            dma((5,)),
            dma((5,)),
        ],
        compiler_params=pltpu.CompilerParams(
            collective_id=0, has_side_effects=True, vmem_limit_bytes=63 * MIB
        ),
        name="forward",
    )(*args)


def run_backward(args, gather, here, units, rows, width, n_time):
    half = rows // 2
    feat = units * 128
    anyspec = pl.BlockSpec(memory_space=pl.ANY)
    vm = pl.BlockSpec(memory_space=VMEM)
    dma = pltpu.SemaphoreType.DMA
    return pl.pallas_call(
        functools.partial(backward_kernel, gather),
        out_shape=(
            shape((here * rows, width), bf16),
            shape((units, 1, 2, 2, 2, 64, width), bf16),
            shape((half, width), bf16),
            shape((here * rows, width), bf16),
            shape((2, 4, 384, width) if gather else (384, width), bf16),
            shape((n_time + 16, width), f32),
        ),
        in_specs=[vm] * 7 + [anyspec] * (len(args) - 7),
        out_specs=[anyspec] * 5 + [vm],
        scratch_shapes=[
            VMEM((4 * feat, width), bf16),
            VMEM((half, width), f32),
            VMEM((rows, width), bf16),
            VMEM((half, width), f32),
            VMEM((rows, width), bf16),
            VMEM((feat, rows), bf16),
            VMEM((feat, rows), bf16),
            VMEM((feat, rows), bf16),
            VMEM((feat, rows), bf16),
            VMEM((feat, rows), bf16),
            VMEM((3 * feat, rows), bf16),
            VMEM((HEAD, rows), f32),
            VMEM((HEAD, rows), f32),
            VMEM((half, width), bf16),
            VMEM((half, width), bf16),
            VMEM((half, width), f32),
            VMEM((2, 1, 2, 2, 2, 64, width), bf16),
            VMEM((half, width), bf16),
            VMEM((16, width), f32),
            VMEM((24, width), f32),
            VMEM((2, units, 2, 2, 64, width), bf16),
            VMEM((2, units, 2, 2, 64, width), bf16),
            VMEM((2, units, 2, 64, width), bf16),
            VMEM((2, units, 1, 2, 64, width), bf16),
            VMEM((2, units, 1, 2, 64, width), bf16),
            VMEM((2, units, 1, 64, width), bf16),
            VMEM((units, 256, width), bf16),
            VMEM((2, 3, 256, width), bf16),
            VMEM((units, 128, width), bf16),
            VMEM((2, 3, 128, width), bf16),
            VMEM((384, width), bf16),
            VMEM((24, width // 2), f32),
            VMEM((4, 24, width // 2 + n_time), f32),
            VMEM((2, 48, width // 2 + n_time), f32),
            VMEM((2, 80, width // 2 + n_time), f32),
            dma((10,)),
            dma((1,)),
            dma((2,)),
            dma((1,)),
            dma((1,)),
            dma((4, 1)),
            dma((7,)),
            dma((4,)),
            dma((7,)),
            dma((4,)),
            dma((2, units)),
            dma((2, 2, units)),
            dma((2, 2, units)),
            dma((2, units)),
            dma((2, 2, units)),
            dma((2, 2, units)),
            dma((2, 3)),
            dma((2, 3)),
            dma((2, 3)),
            dma((2, 3)),
            dma((8,)),
            dma((8,)),
            dma((8,)),
            dma((8,)),
            dma((7,)),
            dma((7,)),
        ],
        compiler_params=pltpu.CompilerParams(
            collective_id=1, has_side_effects=True, vmem_limit_bytes=63 * MIB
        ),
        name="backward",
    )(*args)


def run_deliver(parts, gin, lo, sums, n_time):
    rows, width = gin.shape
    steps = 8
    part = parts.shape[2] // 3
    hid = steps * part
    at = lambda i: (i, 0)
    return pl.pallas_call(
        deliver_kernel,
        grid=(steps,),
        out_shape=(
            shape((rows, width), f32),
            shape((rows, width), bf16),
            shape((n_time, width), f32),
            shape((3, width, 2 * part), f32),
            shape((2 * part, width), f32),
            shape((width, hid), f32),
            shape((hid, width), f32),
        ),
        in_specs=[
            pl.BlockSpec((1, 1, 3 * part, width), lambda i: (i // 4, i % 4, 0, 0)),
            pl.BlockSpec((rows // steps, width), at),
            pl.BlockSpec((rows // steps, width), at),
            pl.BlockSpec((n_time // steps, width), at),
        ],
        out_specs=[
            pl.BlockSpec((rows // steps, width), at),
            pl.BlockSpec((rows // steps, width), at),
            pl.BlockSpec((n_time // steps, width), at),
            pl.BlockSpec((1, width, part), lambda i: (jnp.minimum(i % 4, 2), 0, i // 4)),
            pl.BlockSpec((part, width), lambda i: (i // 4, 0)),
            pl.BlockSpec((width, part), lambda i: (0, i)),
            pl.BlockSpec((part, width), at),
        ],
        compiler_params=pltpu.CompilerParams(vmem_limit_bytes=48 * MIB),
        name="deliver",
    )(parts, gin, lo, sums)


def local(
    ndp, nmp, activations, noise_embed, lengths, time_weight, time_bias, attn_gain, qkv_weight, qkv_bias,
    out_weight, out_bias, mlp_gain, up_weight, up_bias, down_weight, down_bias, cotangent,
):
    width = activations.shape[1]
    here = activations.shape[0] // BUCKET
    assert 2 * here == nmp and qkv_weight.shape[2] == 256 and up_weight.shape[1] == 1024
    assert ndp % 8 == 0 and noise_embed.shape[0] == here * SLOTS
    n_time = time_weight.shape[0]
    frequency = np.exp(np.arange(HEAD // 2, dtype=np.float32) * np.float32(-2.0 * math.log(10000.0) / HEAD))
    frequency = np.broadcast_to(frequency[:, None].astype(np.float32), (HEAD // 2, 128))

    def row(v):
        return v.reshape(1, width)

    (
        lo, gmid, gm, stream, normed, qt, kt, vt, merged, lse, dwm, wqo, small_m, bias_rows, seg_col, trig, meta,
    ) = run_forward(
        (
            activations, cotangent, lengths, noise_embed, time_weight, row(time_bias), row(attn_gain),
            row(out_bias), row(mlp_gain), row(down_bias), qkv_bias, up_bias.reshape(8, 128), jnp.asarray(frequency),
            qkv_weight.transpose(1, 0, 2), out_weight, up_weight, down_weight,
        ),
        here, nmp, width,
    )
    gather = ndp == 8
    lo_all, _, _, gathered, parts, sums = run_backward(
        (
            meta, seg_col, trig, row(attn_gain), small_m, bias_rows, lse, wqo, gmid, gm, stream, normed, qt, kt, vt,
            merged, lo, dwm.reshape(nmp, 2, 2, 2, 2, 64, width),
        ),
        gather, here, nmp, BUCKET, width, n_time,
    )
    if not gather:
        groups = [[i + 8 * k for k in range(ndp // 8)] for i in range(8)]
        parts = lax.psum(parts, "dp", axis_index_groups=groups)
        sums = lax.psum(sums, "dp", axis_index_groups=groups)
        groups = [[8 * k + i for i in range(8)] for k in range(ndp // 8)]
        parts = lax.all_gather(parts, "dp", axis_index_groups=groups)
        parts = parts.reshape(4, 2, 384, width).transpose(1, 0, 2, 3)
    grad_input, layer_output, grad_time_weight, grad_qkv, grad_out, grad_up, grad_down = run_deliver(
        parts, gathered, lo_all, sums, n_time
    )
    grad_qkv = grad_qkv.transpose(1, 0, 2)
    grad_mlp_gain, grad_out_bias, grad_down_bias, grad_attn_gain, grad_time_bias = (
        sums[n_time + i] for i in range(5)
    )
    bias_sums = sums[n_time + 8 :].reshape(2, nmp, width)
    bias_sums = lax.dynamic_index_in_dim(bias_sums, lax.axis_index("mp"), 1, keepdims=False)
    grad_qkv_bias = bias_sums[:, :384].reshape(2, 3, 128).transpose(1, 0, 2).reshape(3, 256)
    grad_up_bias = bias_sums[:, 384:896].reshape(-1)
    return (
        layer_output,
        grad_input,
        grad_time_weight,
        grad_time_bias,
        grad_attn_gain,
        grad_qkv,
        grad_qkv_bias,
        grad_out,
        grad_out_bias,
        grad_mlp_gain,
        grad_up,
        grad_up_bias,
        grad_down,
        grad_down_bias,
    )


def solution(mesh):
    in_specs = (
        P("dp", None),
        P("dp", None),
        P("dp"),
        P(),
        P(),
        P(),
        P(None, None, "mp"),
        P(None, "mp"),
        P("mp", None),
        P(),
        P(),
        P(None, "mp"),
        P("mp"),
        P("mp", None),
        P(),
        P("dp", None),
    )
    out_specs = (
        P("dp", None),
        P("dp", None),
        P(),
        P(),
        P(),
        P(None, None, "mp"),
        P(None, "mp"),
        P("mp", None),
        P(),
        P(),
        P(None, "mp"),
        P("mp"),
        P("mp", None),
        P(),
    )
    body = functools.partial(local, mesh.shape["dp"], mesh.shape["mp"])
    return jax.shard_map(body, mesh=mesh, in_specs=in_specs, out_specs=out_specs, check_vma=False)
```

```python
import functools
import math

import jax
import jax.numpy as jnp
from jax import lax
from jax.experimental import pallas as pl
from jax.experimental.pallas import tpu as pltpu
from jax.sharding import PartitionSpec as P

HEAD = 64
BUCKET = 1024
SLOTS = 8
MIB = 1 << 20
MESH = pl.DeviceIdType.MESH
VMEM = pltpu.VMEM
bf16 = jnp.bfloat16
f32 = jnp.float32


def contract(a, b, ca, cb):
    return lax.dot_general(a, b, (((ca,), (cb,)), ((), ())), preferred_element_type=f32)


def tile(i, n):
    return pl.ds(pl.multiple_of(i * n, n), n)


def loop(n, body):
    def step(i, carry):
        body(i)
        return carry

    lax.fori_loop(0, n, step, 0)


def row_stats(v):
    centered = v - jnp.mean(v, axis=-1, keepdims=True)
    return centered, lax.rsqrt(jnp.mean(centered * centered, axis=-1, keepdims=True) + 1e-05)


def norm_back(v, gain, err):
    centered, scale = row_stats(v)
    xhat = centered * scale
    u = err * gain
    grad = (
        u - jnp.mean(u, axis=-1, keepdims=True) - xhat * jnp.mean(u * xhat, axis=-1, keepdims=True)
    ) * scale
    return grad, jnp.sum(err * xhat, axis=0, keepdims=True)


def toggled(v, bit):
    return v + bit - 2 * bit * lax.rem(v // bit, 2)


def peer(z, m):
    low = lax.rem(lax.rem(z, 2) + m % 2, 2)
    return low + 2 * lax.rem(z // 2 + m // 2, 2)


def greet(targets):
    barrier = pltpu.get_barrier_semaphore()
    for d, z in targets:
        pl.semaphore_signal(barrier, inc=1, device_id={"dp": d, "mp": z}, device_id_type=MESH)
    pl.semaphore_wait(barrier, len(targets))


def remote(src, dst, ss, rs, d, z):
    return pltpu.make_async_remote_copy(
        src_ref=src,
        dst_ref=dst,
        send_sem=ss,
        recv_sem=rs,
        device_id={"dp": d, "mp": z},
        device_id_type=MESH,
    )


class Spread:
    def __init__(self, src, out, near_sem, send_sem, recv_sem):
        me, z = lax.axis_index("dp"), lax.axis_index("mp")
        self.core = core = lax.rem(me, 2)
        self.kind = kind = z // 2
        self.place = z + core * (3 - 2 * z)
        self.start_place = z + kind * (3 - 2 * z)
        self.out, self.send, self.recv = out, send_sem, recv_sem
        self.me, self.z, self.ahead = me, z, z + 1 - 2 * core
        keeper = me - core + kind
        dst = self.piece(self.start_place, core, kind)
        rs = recv_sem.at[2 * self.start_place + core]
        self.near = pltpu.make_async_copy(src, dst, near_sem.at[0])
        self.first = [
            remote(src, dst, send_sem.at[0], rs, keeper, z + 1 - 2 * kind),
            remote(src, dst, send_sem.at[1], rs, keeper, z - 1 + 2 * kind),
            remote(src, dst, send_sem.at[2], rs, toggled(me, 1), z),
        ]

    def piece(self, m, h, kind):
        rows = self.out.shape[0] // 4
        at = 2 * (m + kind * (1 - 2 * m)) + h
        return self.out.at[pl.ds(pl.multiple_of(at * rows, rows), rows), :]

    def hop(self, m, h, i):
        ref = self.piece(m, h, self.core)
        return remote(ref, ref, self.send.at[i], self.recv.at[2 * m + h], self.me, self.ahead)

    def begin(self):
        self.first[0].start()

        @pl.when(self.start_place == 1)
        def _():
            self.first[1].start()

        @pl.when(self.core == self.kind)
        def _():
            self.near.start()

        @pl.when(self.core != self.kind)
        def _():
            self.first[2].start()

    def forward(self, place, m, i):
        @pl.when(self.place == place)
        def _():
            for h in range(2):
                self.hop(m, h, i + h).wait_recv()
                self.hop(m, h, i + h).start()

    def pass_first(self):
        self.forward(1, 0, 3)
        self.forward(2, 1, 3)

    def pass_second(self):
        self.forward(2, 0, 5)

    def finish(self):
        @pl.when(self.core == self.kind)
        def _():
            self.near.wait()
            self.hop(self.place, 1 - self.core, 3).wait_recv()

        @pl.when(self.core != self.kind)
        def _():
            self.first[2].wait_send()

        @pl.when(self.place == 0)
        def _():
            for h in range(2):
                self.hop(1, h, 3).wait_recv()

        @pl.when(self.place == 3)
        def _():
            for m in range(2):
                for h in range(2):
                    self.hop(m, h, 3).wait_recv()

        self.first[0].wait_send()

        @pl.when(self.start_place == 1)
        def _():
            self.first[1].wait_send()

        for place, m, i in ((1, 0, 3), (2, 1, 3), (2, 0, 5)):

            @pl.when(self.place == place)
            def _(m=m, i=i):
                for h in range(2):
                    self.hop(m, h, i + h).wait_send()


class PlaneSum:
    def __init__(self, src, keep, got, last, load_sem, send_sem, recv_sem):
        me, z = lax.axis_index("dp"), lax.axis_index("mp")
        self.x, self.y = lax.rem(me // 2, 2), lax.rem(me // 4, 2)
        self.z, self.across, self.along = z, toggled(me, 2), toggled(me, 4)
        self.src, self.keep, self.got, self.last = src, keep, got, last
        self.load_sem, self.send_sem, self.recv_sem = load_sem, send_sem, recv_sem

    def part(self, u, order, mine):
        x = self.x if mine else 1 - self.x
        y = self.y if mine else 1 - self.y
        return self.src.at[u, :, :, x, 0] if order == 0 else self.src.at[u, :, y, :, 1]

    def load(self, u, order):
        return pltpu.make_async_copy(
            self.part(u, order, True), self.keep.at[order, u], self.load_sem.at[order, u]
        )

    def hop(self, u, order, stage):
        if stage == 0:
            src, dst = self.part(u, order, False), self.got.at[order, u]
        else:
            there = 1 - (self.y if order == 0 else self.x)
            src, dst = self.keep.at[order, u, :, there], self.last.at[order, u]
        to = self.across if order == stage else self.along
        return remote(
            src, dst, self.send_sem.at[order, stage, u], self.recv_sem.at[order, stage, u], to, self.z
        )

    def begin(self, u):
        for order in range(2):
            self.load(u, order).start()
            self.hop(u, order, 0).start()

    def middle(self, u):
        for order in range(2):
            self.load(u, order).wait()
            self.hop(u, order, 0).wait_recv()
            total = self.keep[order, u].astype(f32) + self.got[order, u].astype(f32)
            self.keep[order, u] = total.astype(bf16)
            self.hop(u, order, 1).start()

    def end(self, u, put):
        for order in range(2):
            self.hop(u, order, 1).wait_recv()
            here = self.y if order == 0 else self.x
            total = self.keep[order, u, :, here].astype(f32) + self.last[order, u].astype(f32)
            put(u, order, total.astype(bf16))

    def drain(self, u):
        for order in range(2):
            for stage in range(2):
                self.hop(u, order, stage).wait_send()


class LineSum:
    def __init__(self, own, got, send_sem, recv_sem):
        self.me, self.z = lax.axis_index("dp"), lax.axis_index("mp")
        self.own, self.got, self.send_sem, self.recv_sem = own, got, send_sem, recv_sem

    def hop(self, way, t):
        entry = t if way == 0 else 3 - t
        return remote(
            self.own.at[entry], self.got.at[way, t - 1], self.send_sem.at[way, t - 1],
            self.recv_sem.at[way, t - 1], self.me, self.z + 1 - 2 * way,
        )

    def step(self, s, entry):
        for way in range(2):
            t = entry if way == 0 else 3 - entry
            if s >= t:
                continue

            @pl.when(self.z == (s if way == 0 else 3 - s))
            def _(way=way, t=t):
                if s > 0:
                    self.hop(way, t).wait_recv()
                    total = self.own[entry].astype(f32) + self.got[way, t - 1].astype(f32)
                    self.own[entry] = total.astype(bf16)
                self.hop(way, t).start()

    def finish(self, put):
        for way in range(2):
            for t in range(1, 4):

                @pl.when(self.z == (t if way == 0 else 3 - t))
                def _(way=way, t=t):
                    self.hop(way, t).wait_recv()
                    entry = t if way == 0 else 3 - t
                    total = self.own[entry].astype(f32) + self.got[way, t - 1].astype(f32)
                    self.own[entry] = total.astype(bf16)

        put(self.own[self.z])
        for way in range(2):
            for s in range(3):

                @pl.when(self.z == (s if way == 0 else 3 - s))
                def _(way=way, s=s):
                    for t in range(3, s, -1):
                        self.hop(way, t).wait_send()


class PlaneGather:
    def __init__(self, final, parts, rows, own_sem, send_sem, recv_sem):
        me, self.z = lax.axis_index("dp"), lax.axis_index("mp")
        self.core, self.col = lax.rem(me, 2), lax.rem(me // 2, 4)
        self.other, self.across, self.along = toggled(me, 1), toggled(me, 2), toggled(me, 4)
        self.parts, self.rows = parts, rows
        self.send_sem, self.recv_sem = send_sem, recv_sem
        self.cols = (
            self.col, toggled(self.col, 1), toggled(self.col, 2), toggled(toggled(self.col, 1), 2),
        )
        src = final.at[pl.ds(rows[0], rows[1]), :]
        self.near = pltpu.make_async_copy(src, self.slot(self.core, self.col), own_sem)
        self.hops = [
            self.hop(self.slot(self.core, self.col), 4, self.across, src),
            self.hop(self.slot(self.core, self.col), 5, self.along, src),
            self.hop(self.slot(self.core, self.col), 0, self.other, src),
        ]

    def slot(self, c, s, h=None):
        at, n = self.rows
        if h is not None:
            at, n = at + h * (n // 2), n // 2
        return self.parts.at[c, s, pl.ds(at, n), :]

    def hop(self, dst, i, to, src=None):
        src = dst if src is None else src
        return remote(src, dst, self.send_sem.at[i], self.recv_sem.at[i], to, self.z)

    def begin(self):
        for c in self.hops:
            c.start()
        self.near.start()

    def pass_on(self):
        for j, (i, ahead, h, k) in enumerate(((4, self.along, 0, 6), (5, self.across, 1, 7))):
            s = self.cols[1 + j]
            self.hop(self.slot(self.core, s), i, self.other).wait_recv()
            more = [
                self.hop(self.slot(self.core, s, h), k, ahead),
                self.hop(self.slot(self.core, s), 1 + j, self.other),
            ]
            for c in more:
                c.start()
            self.hops += more

    def finish(self):
        s = self.cols[3]
        for h in range(2):
            self.hop(self.slot(self.core, s, h), 6 + h, self.other).wait_recv()
        last = self.hop(self.slot(self.core, s), 3, self.other)
        last.start()
        self.near.wait()
        for i in range(4):
            self.hop(self.slot(1 - self.core, self.cols[i]), i, self.other).wait_recv()
        for c in self.hops + [last]:
            c.wait_send()


class SmallSum:
    def __init__(self, mine, pair, line, across, along, out, send_sem, recv_sem):
        me, self.z = lax.axis_index("dp"), lax.axis_index("mp")
        self.me, self.core = me, lax.rem(me, 2)
        self.x, self.y = lax.rem(me // 2, 2), lax.rem(me // 4, 2)
        self.mine, self.pair, self.line, self.a, self.b, self.out = mine, pair, line, across, along, out
        self.send_sem, self.recv_sem = send_sem, recv_sem
        n = pair.shape[1]
        self.n = n
        self.lanes = pl.ds(pl.multiple_of(self.core * n, n), n)
        there = pl.ds(pl.multiple_of((1 - self.core) * n, n), n)

        def move(src, dst, i, d, z):
            return remote(src, dst, send_sem.at[i], recv_sem.at[i], d, z)

        other = toggled(me, 1)
        self.swap = move(mine.at[:, there], pair, 0, other, self.z)
        slot = line.at[self.z]
        self.hops = [move(slot, slot, m, me, peer(self.z, m)) for m in (1, 2, 3)]
        self.hop_x = move(across.at[self.x], across.at[self.x], 4, toggled(me, 2), self.z)
        self.hop_y = move(along.at[self.y], along.at[self.y], 5, toggled(me, 4), self.z)
        done = out.at[:, self.lanes]
        self.last = move(done, done, 6, other, self.z)

    def begin(self):
        self.swap.start()

    def step_line(self, noise):
        n, width = self.n, noise.shape[1]
        self.swap.wait()
        self.line[self.z, :, 0:n] = self.mine[:, self.lanes] + self.pair[...]
        self.line[self.z, 16:24, n : n + width] = noise
        self.line[self.z, 0:16, n : n + width] = jnp.zeros((16, width), f32)
        for c in self.hops:
            c.start()

    def step_across(self):
        for c in self.hops:
            c.wait()
        v = [self.line[i] for i in range(4)]
        self.a[self.x, 0:16, :] = ((v[0] + v[1]) + (v[2] + v[3]))[0:16]
        for i in range(4):
            self.a[self.x, 16 + 8 * i : 24 + 8 * i, :] = v[i][16:24]
        self.hop_x.start()

    def step_along(self):
        self.hop_x.wait()
        self.b[self.y, 0:16, :] = self.a[0, 0:16, :] + self.a[1, 0:16, :]
        for i in range(2):
            self.b[self.y, 16 + 32 * i : 48 + 32 * i, :] = self.a[i, 16:48, :]
        self.hop_y.start()

    def step_out(self):
        self.hop_y.wait()
        n, n_time = self.n, self.out.shape[0] - 16
        self.out[n_time : n_time + 16, self.lanes] = self.b[0, 0:16, 0:n] + self.b[1, 0:16, 0:n]
        rows = jnp.concatenate([self.b[0, 16:80, :], self.b[1, 16:80, :]])
        grads, noise = rows[:, 0:n], rows[:, n : n + n_time].astype(bf16)
        high = grads.astype(bf16)
        rest = grads - high.astype(f32)
        middle = rest.astype(bf16)
        low = (rest - middle.astype(f32)).astype(bf16)
        total = contract(noise, high, 0, 0) + contract(noise, middle, 0, 0)
        self.out[0:n_time, self.lanes] = total + contract(noise, low, 0, 0)
        self.last.start()

    def finish(self):
        self.last.wait()


def one_hot(seg, copies):
    lanes = lax.broadcasted_iota(jnp.int32, (1, 128), 1)
    lanes = jnp.where(lanes < 16 * copies, lax.rem(lanes, 16), -1).astype(f32)
    return jnp.where(seg == lanes, 1.0, 0.0).astype(bf16)


def rotate_rows(v, cosine, sine):
    a, b = v[: HEAD // 2], v[HEAD // 2 :]
    return jnp.concatenate([a * cosine - b * sine, b * cosine + a * sine], axis=0)


def forward_kernel(
    act_any, cot_any, lens, noise, time_weight, time_bias, attn_gain, out_bias, mlp_gain, down_bias,
    qkv_bias, up_bias, qkv_any, ow_any, uw_any, dn_any,
    out_any, gmid_any, gm_any, stream_any, normed_any, q_any, k_any, v_any, merged_any, lse_any,
    dwm_any, wqo_any, small, bias_rows, seg_col, trig, meta,
    w, x, gfin, bias, biases, stream, normed, qt, kt, vt, merged, lse, send, recv, mid, nm, act, gp, gm,
    stage, lo, gmid, raw_qkv, acc,
    load_sem, bring_send, bring_recv, bias_send, bias_recv, w_send, w_recv,
    out_sem, stage_sem, send_sem, recv_sem,
):
    me, z = lax.axis_index("dp"), lax.axis_index("mp")
    core, col = lax.rem(me, 2), lax.rem(me // 2, 4)
    other, across, along = toggled(me, 1), toggled(me, 2), toggled(me, 4)
    here = act_any.shape[0] // BUCKET
    units = biases.shape[0]
    half = BUCKET // 2
    own, far = tile(core, half), tile(1 - core, half)
    mine = core == z // here
    up_at, dn_at, out_at = units * 512, units * 1024, units * 384

    def block(start, n):
        return pl.ds(pl.multiple_of(start, n), n)

    loads = [
        pltpu.make_async_copy(s, d, load_sem.at[i])
        for i, (s, d) in enumerate(
            (
                (qkv_any.at[:, :, block(core * 128, 128)], raw_qkv),
                (ow_any.at[block(core * 128, 128), :], w.at[block(out_at + z * 128, 128), :]),
                (uw_any.at[:, block(core * 512, 512)], nm.at[:, pl.ds(0, 512)]),
                (dn_any.at[block(core * 512, 512), :], w.at[block(dn_at + z * 512, 512), :]),
            )
        )
    ]
    for c in loads:
        c.start()
    greet([(other, z), (across, z), (along, z)] + [(me, peer(z, m)) for m in (1, 2, 3)])

    bucket_at = lax.rem(z, here)
    bucket = pl.ds(pl.multiple_of(bucket_at * BUCKET, BUCKET), BUCKET)
    brought = (
        (meta, meta),
        (act_any.at[bucket, :], x),
        (cot_any.at[bucket, :], gfin),
    )

    def bring(i, begin):
        src, dst = brought[i]
        near = None if i == 0 else pltpu.make_async_copy(src, dst, load_sem.at[4 + i])
        sent = remote(src, dst, bring_send.at[i], bring_recv.at[i], other, z)

        @pl.when(mine)
        def _():
            if begin:
                sent.start()
                if near is not None:
                    near.start()
            else:
                if near is not None:
                    near.wait()
                sent.wait_send()

        if not begin:

            @pl.when(jnp.logical_not(mine))
            def _():
                sent.wait_recv()

    def row_of(k, u, s):
        if k == 0:
            return u * 384 + 128 * s + (s // 3) * (out_at - 384 + 128 * u - 384 * u)
        return (up_at if k == 1 else dn_at) + u * 512 + 128 * s

    def hop(k, m, way):
        i = 3 * k + m - 1
        u = peer(z, m)
        if way == 0 and m == 3:
            at, n, d, zz = row_of(k, peer(z, 2), col), 128, me, peer(z, 1)
        elif way == 0:
            at, n, d, zz = row_of(k, z, col), 128, me, u
        elif way == 1:
            at, n, d, zz = row_of(k, u, col), 128, across, z
        elif way == 2:
            at, n, d, zz = row_of(k, u, col), 128, along, z
        elif way == 3:
            at, n, d, zz = row_of(k, u, toggled(col, 1)), 64, along, z
        else:
            at, n, d, zz = row_of(k, u, toggled(col, 2)) + 64, 64, across, z
        rows = w.at[block(at, n), :]
        src = dn_any.at[block(core * 512 + col * 128, 128), :] if (k, way) == (2, 0) and m < 3 else rows
        return remote(src, rows, w_send.at[i, way], w_recv.at[i, way], d, zz)

    def arrived(k, m, way):
        i = 3 * k + m - 1
        u = peer(z, m)
        s = (col, toggled(col, 1), toggled(col, 2), toggled(toggled(col, 1), 2), toggled(toggled(col, 1), 2))[way]
        at = row_of(k, u, s) + (64 if way == 4 else 0)
        rows = w.at[block(at, 128 if way < 3 else 64), :]
        remote(rows, rows, w_send.at[i, way], w_recv.at[i, way], other, z).wait_recv()

    def send_z(k, *ms):
        for m in ms:
            hop(k, m, 0).start()

    def pass_a(k, m):
        arrived(k, m, 0)
        if m == 2:
            hop(k, 3, 0).start()
        hop(k, m, 1).start()
        hop(k, m, 2).start()

    def pass_b(k, m):
        arrived(k, m, 1)
        hop(k, m, 3).start()
        arrived(k, m, 2)
        hop(k, m, 4).start()

    def pass_c(k, m):
        arrived(k, m, 3)
        arrived(k, m, 4)

    bring(1, True)
    for c in range(2):

        @pl.when(core == c)
        def _(c=c):
            bias[0:3, :] = qkv_bias[:, c * 128 : (c + 1) * 128]
            bias[3:4, :] = jnp.zeros((1, 128), f32)
            bias[4:8, :] = up_bias[c * 4 : (c + 1) * 4, :]

    biases[z] = bias[...]
    bias_hops = [
        remote(bias, biases.at[z], bias_send.at[m - 1], bias_recv.at[m - 1], me, peer(z, m))
        for m in (1, 2, 3)
    ]

    loads[0].wait()
    for i in range(3):
        w[block(z * 384 + i * 128, 128), :] = raw_qkv[i].T
    loads[1].wait()
    send_z(0, 1)

    @pl.when(mine)
    def _():
        places = lax.broadcasted_iota(jnp.int32, (1, BUCKET), 1)
        past, start, end = jnp.zeros_like(places), jnp.zeros_like(places), 0
        for i in range(SLOTS):
            end = end + lens[bucket_at * SLOTS + i]
            beyond = places >= end
            past = past + beyond.astype(jnp.int32)
            start = jnp.where(beyond, end, start)
        live = places < end
        meta[8:9, :] = jnp.where(live, past, 2000 + places).astype(f32)
        meta[9:10, :] = (places - jnp.where(live, start, 0)).astype(f32)
        rows = jnp.dot(noise[...], time_weight[...], preferred_element_type=f32) + time_bias[...]
        first = bucket_at == 0
        meta[0:8, :] = jnp.where(first, rows[0:SLOTS], rows[SLOTS : 2 * SLOTS])
        loud = noise[...].astype(f32)
        meta[16:24, 0 : loud.shape[1]] = jnp.where(first, loud[0:SLOTS], loud[SLOTS : 2 * SLOTS])

    bring(0, True)
    bring(2, True)
    for c in bias_hops:
        c.start()
    loads[2].wait()
    for i in range(4):
        w[block(up_at + z * 512 + i * 128, 128), :] = nm[:, i * 128 : (i + 1) * 128].T
    loads[3].wait()
    send_z(0, 2)

    saves = []

    def save(src, dst):
        c = pltpu.make_async_copy(src, dst, out_sem.at[len(saves)])
        c.start()
        saves.append(c)

    def swap(src, dst, i):
        c = remote(src, dst, send_sem.at[i], recv_sem.at[i], other, z)
        c.start()
        return c

    bring(0, False)
    seg_col[...] = jnp.broadcast_to(meta[8:9, :], (128, BUCKET)).T
    step = lax.broadcasted_iota(jnp.int32, (HEAD // 2, 1), 0).astype(f32)
    angles = jnp.exp(step * (-2.0 * math.log(10000.0) / HEAD)) * meta[9:10, :]
    trig[0:32, :] = jnp.cos(angles)
    trig[32:64, :] = jnp.sin(angles)
    t_rows = meta[0:8, :]
    high = t_rows.astype(bf16).astype(f32)
    middle_part = (t_rows - high).astype(bf16).astype(f32)
    lowest = t_rows - high - middle_part
    gap = jnp.zeros((8, t_rows.shape[1]), f32)
    time_rows = jnp.concatenate(
        [high, gap, middle_part, gap, lowest, gap, jnp.zeros((80, t_rows.shape[1]), f32)]
    ).astype(bf16)
    pass_a(0, 1)
    send_z(1, 1)
    bring(1, False)

    def enter(i):
        rs = tile(i, 256)
        added = jnp.dot(one_hot(seg_col[rs, :], 3), time_rows, preferred_element_type=f32)
        stream[rs, :] = x[rs, :].astype(f32) + added

    loop(4, enter)

    def norm(i):
        rs = tile(i, 128)
        centered, scale = row_stats(stream[rs, :])
        normed[rs, :] = (centered * scale * attn_gain[...]).astype(bf16)

    loop(8, norm)
    save(normed, normed_any)
    save(stream.at[own, :], stream_any)
    stream_saved = saves[-1]

    def bias_column(u, s):
        return jnp.broadcast_to(biases[u, s : s + 1, :], (128, 128)).T[:, 0:1]

    def unit(u):
        column = jnp.concatenate([bias_column(u, s) for s in range(3)], axis=0)
        proj = contract(w[block(u * 384, 384), :], normed[...], 1, 1) + column
        cs, sn = trig[0:32, :], trig[32:64, :]
        us = tile(u, 128)
        qt[us, :] = jnp.concatenate(
            [rotate_rows(proj[h * HEAD : (h + 1) * HEAD], cs, sn) for h in range(2)], axis=0
        ).astype(bf16)
        kt[us, :] = jnp.concatenate(
            [rotate_rows(proj[128 + h * HEAD : 128 + (h + 1) * HEAD], cs, sn) for h in range(2)],
            axis=0,
        ).astype(bf16)
        vt[us, :] = proj[256:384].astype(bf16)

        def head(j):
            h = 2 * u + j
            hs = tile(h, HEAD)
            keys = (kt[hs, :].astype(f32) * 0.125).T.astype(bf16)
            values = vt[hs, :]
            for t in range(2):
                cs_t = pl.ds(t * 512, 512)
                s = jnp.dot(keys, qt[hs, cs_t], preferred_element_type=f32)
                same = jnp.tile(seg_col[...], (1, 4)) == meta[8:9, cs_t]
                s = jnp.where(same, s, -1e30)
                top = jnp.max(s, axis=0, keepdims=True)
                p = jnp.exp(s - top)
                total = jnp.sum(p, axis=0, keepdims=True)
                o = jnp.dot(values, p.astype(bf16), preferred_element_type=f32)
                merged[hs, cs_t] = (o / total).astype(bf16)
                lse[h, :, cs_t] = top + jnp.log(total)

        loop(2, head)

    pass_b(0, 1)
    pass_a(0, 2)
    send_z(2, 1)
    for c in bias_hops:
        c.wait()
    unit(z)
    pass_c(0, 1)
    pass_b(0, 2)
    pass_a(0, 3)
    send_z(1, 2)
    unit(peer(z, 1))
    pass_b(0, 3)
    pass_c(0, 2)
    pass_a(1, 1)
    send_z(2, 2)
    unit(peer(z, 2))
    pass_c(0, 3)
    pass_b(1, 1)
    pass_a(2, 1)
    unit(peer(z, 3))
    pass_c(1, 1)
    pass_b(2, 1)
    pass_a(1, 2)
    save(qt, q_any)
    save(kt, k_any)
    save(vt, v_any)
    save(merged, merged_any)
    save(lse, lse_any)
    save(w.at[pl.ds(0, up_at), :], wqo_any)

    w_out = w.at[pl.ds(out_at, units * 128), :]
    w_up = w.at[pl.ds(up_at, units * 512), :]
    w_dn = w.at[pl.ds(dn_at, units * 512), :]
    send[0] = contract(merged[:, far], w_out[...], 0, 0).astype(bf16)
    swap0 = swap(send.at[0], recv.at[0], 0)
    mid[...] = contract(merged[:, own], w_out[...], 0, 0)
    bring(2, False)

    def mask(i):
        rs = tile(i, 256)
        live = jnp.where(seg_col[rs, :][:, 0:1] < 1000.0, 1.0, 0.0)
        gfin[rs, :] = (gfin[rs, :].astype(f32) * live).astype(bf16)

    loop(4, mask)
    swap0.wait()

    def middle(i):
        rs = tile(i, 128)
        ro = pl.ds(pl.multiple_of(core * half + i * 128, 128), 128)
        v = stream[ro, :] + (mid[rs, :] + recv[0, rs, :].astype(f32)) + out_bias[...]
        mid[rs, :] = v
        centered, scale = row_stats(v)
        nm[ro, :] = (centered * scale * mlp_gain[...]).astype(bf16)

    loop(4, middle)
    swap1 = swap(nm.at[own, :], nm.at[own, :], 1)
    pass_c(2, 1)
    pass_b(1, 2)
    pass_a(2, 2)
    swap1.wait()

    def gelu_parts(u, rs):
        column = jnp.concatenate([bias_column(u, 4 + s) for s in range(4)], axis=0)
        pre = contract(w_up[tile(u, 512), :], nm[rs, :], 1, 1) + column
        sq = pre * pre
        th = jnp.tanh(pre * (0.7978845608028654 + (0.7978845608028654 * 0.044715) * sq))
        hp = 0.5 + 0.5 * th
        slope = hp + pre * (hp * (1.0 - th)) * (
            0.7978845608028654 + (3 * 0.7978845608028654 * 0.044715) * sq
        )
        return pre * hp, slope

    def hidden_unit(n, u):
        us = tile(u, 512)

        def hidden(t):
            rs = tile(t, 256)
            value, slope = gelu_parts(u, rs)
            act[us, rs] = value.astype(bf16)
            gp[us, rs] = (contract(w_dn[us, :], gfin[rs, :], 1, 1) * slope).astype(bf16)

        loop(4, hidden)

    def weights_unit(n, u):
        us = tile(u, 512)
        bias_rows[u, :, 384:896] = contract(jnp.ones((8, BUCKET), bf16), gp[us, :], 1, 1)
        for i, left, right in ((0, gp, nm), (1, act, gfin)):
            if n > 0:
                pltpu.make_async_copy(stage.at[i], dwm_any.at[u, i], stage_sem.at[i]).wait()
            stage[i] = contract(left[us, :], right[...], 1, 0).astype(bf16)
            pltpu.make_async_copy(stage.at[i], dwm_any.at[u, i], stage_sem.at[i]).start()

    def partial_sums(n, u):
        us = tile(u, 512)
        for left, right, kept in ((act, w_dn, stream), (gp, w_up, acc)):
            for rows in (far, own):
                total = contract(left[us, rows], right[us, :], 0, 0)
                if n > 0:
                    total = total + kept[rows, :]
                kept[rows, :] = total

    bias_rows[...] = jnp.zeros_like(bias_rows)
    stream_saved.wait()
    hidden_unit(0, z)
    pass_c(1, 2)
    pass_b(2, 2)
    pass_a(1, 3)
    weights_unit(0, z)
    partial_sums(0, z)
    pass_c(2, 2)
    pass_b(1, 3)
    pass_a(2, 3)
    hidden_unit(1, peer(z, 1))
    pass_c(1, 3)
    pass_b(2, 3)
    weights_unit(1, peer(z, 1))
    partial_sums(1, peer(z, 1))
    hidden_unit(2, peer(z, 2))
    weights_unit(2, peer(z, 2))
    partial_sums(2, peer(z, 2))
    last_unit = peer(z, 3)
    us = tile(last_unit, 512)

    def last_values(t):
        rs = tile(t, 256)
        value, slope = gelu_parts(last_unit, rs)
        act[us, rs] = value.astype(bf16)
        gmid[:, rs] = slope

    def last_slopes(t):
        rs = tile(t, 256)
        gp[us, rs] = (contract(w_dn[us, :], gfin[rs, :], 1, 1) * gmid[:, rs]).astype(bf16)

    loop(4, last_values)
    pass_c(2, 3)
    send[1] = (stream[far, :] + contract(act[us, far], w_dn[us, :], 0, 0)).astype(bf16)
    swap2 = swap(send.at[1], recv.at[1], 2)
    loop(4, last_slopes)
    gmid[...] = stream[own, :] + contract(act[us, own], w_dn[us, :], 0, 0)
    swap2.wait()

    def finish(i):
        rs = tile(i, 128)
        ro = pl.ds(pl.multiple_of(core * half + i * 128, 128), 128)
        live = jnp.where(seg_col[ro, :][:, 0:1] < 1000.0, 1.0, 0.0)
        v = mid[rs, :] + (gmid[rs, :] + recv[1, rs, :].astype(f32)) + down_bias[...]
        lo[rs, :] = (live * v).astype(bf16)

    loop(4, finish)
    save(lo, out_any)
    send[2] = (acc[far, :] + contract(gp[us, far], w_up[us, :], 0, 0)).astype(bf16)
    swap3 = swap(send.at[2], recv.at[2], 3)
    gmid[...] = acc[own, :] + contract(gp[us, own], w_up[us, :], 0, 0)
    swap3.wait()
    small[...] = jnp.zeros_like(small)

    def back(i):
        rs = tile(i, 128)
        ro = pl.ds(pl.multiple_of(core * half + i * 128, 128), 128)
        err = gmid[rs, :] + recv[2, rs, :].astype(f32)
        grad, gain_grad = norm_back(mid[rs, :], mlp_gain[...], err)
        gf = gfin[ro, :].astype(f32)
        grad = grad + gf
        gmid[rs, :] = grad
        gm[ro, :] = grad.astype(bf16)
        small[0:1, :] += gain_grad
        small[1:2, :] += jnp.sum(grad, axis=0, keepdims=True)
        small[2:3, :] += jnp.sum(gf, axis=0, keepdims=True)

    loop(4, back)
    swap4 = swap(gm.at[own, :], gm.at[own, :], 4)
    save(gmid, gmid_any)
    weights_unit(3, last_unit)
    swap4.wait()
    save(gm, gm_any)
    for i in range(2):
        pltpu.make_async_copy(stage.at[i], dwm_any.at[0, i], stage_sem.at[i]).wait()
    for c in saves:
        if c is not stream_saved:
            c.wait()
    for k in range(3):
        for m in (1, 2, 3):
            for way in range(5):
                hop(k, m, way).wait_send()


def column_devices(me, z):
    both = (me, toggled(me, 1))
    return [(both[1], z)] + [(d, peer(z, m)) for m in (1, 2, 3) for d in both]


def backward_kernel(
    gather,
    meta, seg_col, trig, attn_gain, small_m, bias_rows, lse,
    wqo_any, gmid_any, gm_any, stream_any, normed_any, q_any, k_any, v_any, merged_any, lo_any, dwm_any,
    out_any, dwa_any, gathered_any, parts, sums,
    wqo, gmid, gm, stream, normed, qt, kt, vt, merged,
    gmerged, gproj, acck, accv, send, recv, gin, stage, gin_low, small, mine,
    keep_m, got_m, last_m, keep_a, got_a, last_a, own_m, line_got_m, own_a, line_got_a, final,
    small_pair, small_line, small_x, small_y,
    load_sem, stage_sem, send_sem, recv_sem, near_sem,
    lo_send, lo_recv, gin_send, gin_recv, pm_load, pm_send, pm_recv, pa_load, pa_send, pa_recv,
    lm_send, lm_recv, la_send, la_recv, gm_send, gm_recv, ga_send, ga_recv, small_send, small_recv,
):
    me, z = lax.axis_index("dp"), lax.axis_index("mp")
    core, other = lax.rem(me, 2), toggled(me, 1)
    half = BUCKET // 2
    units = wqo.shape[0] // 512
    n_qkv = units * 384
    w_qkv, w_out = pl.ds(0, n_qkv), pl.ds(n_qkv, units * 128)
    loads = {}
    for name, src, dst in (
        ("out", wqo_any.at[w_out, :], wqo.at[w_out, :]),
        ("gm", gm_any, gm),
        ("q", q_any, qt),
        ("k", k_any, kt),
        ("v", v_any, vt),
        ("merged", merged_any, merged),
        ("qkv", wqo_any.at[w_qkv, :], wqo.at[w_qkv, :]),
        ("stream", stream_any, stream),
        ("gmid", gmid_any, gmid),
        ("normed", normed_any, normed),
    ):
        loads[name] = pltpu.make_async_copy(src, dst, load_sem.at[len(loads)])
        loads[name].start()
    wqkv, wout = wqo.at[w_qkv, :], wqo.at[w_out, :]
    cosine, sine = trig.at[pl.ds(0, 32), :], trig.at[pl.ds(32, 32), :]
    greet([(toggled(me, 2), z), (toggled(me, 4), z)] + column_devices(me, z))
    plane_m = PlaneSum(dwm_any, keep_m, got_m, last_m, pm_load, pm_send, pm_recv)
    spread_lo = Spread(lo_any, out_any, near_sem.at[0], lo_send, lo_recv)
    plane_m.begin(0)
    spread_lo.begin()
    plane_m.begin(3)

    def put_m(u, order, total):
        for i in range(2):
            own_m[u, i * 128 + order * 64 : i * 128 + (order + 1) * 64, :] = total[i]

    def put_a(u, order, total):
        own_a[u, order * 64 : (order + 1) * 64, :] = total[0]

    own = tile(core, half)
    far = tile(1 - core, half)
    loads["out"].wait()
    loads["gm"].wait()
    for t in range(2):
        cs = pl.ds(t * 512, 512)
        gmerged[:, cs] = contract(wout[...], gm[cs, :], 1, 1).astype(bf16)
    for name in ("q", "k", "v", "merged"):
        loads[name].wait()

    def head(h):
        hs = tile(h, HEAD)
        u = h // 2
        j = lax.rem(h, 2)
        at = u * 384 + j * HEAD
        keys_t = (kt[hs, :].astype(f32) * 0.125).astype(bf16)
        keys = keys_t.astype(f32).T.astype(bf16)
        values = vt[hs, :].astype(f32).T.astype(bf16)
        for t in range(2):
            cs = pl.ds(t * 512, 512)
            q, go = qt[hs, cs], gmerged[hs, cs]
            dl = jnp.sum(go.astype(f32) * merged[hs, cs].astype(f32), axis=0, keepdims=True)
            s = jnp.dot(keys, q, preferred_element_type=f32)
            same = jnp.tile(seg_col[...], (1, 4)) == meta[8:9, cs]
            p = jnp.exp(jnp.where(same, s, -1e30) - lse[h, :, cs])
            dp = jnp.dot(values, go, preferred_element_type=f32)
            ds = (p * (dp - dl)).astype(bf16)
            dq = jnp.dot(keys_t, ds, preferred_element_type=f32)
            gproj[pl.ds(pl.multiple_of(at, HEAD), HEAD), cs] = rotate_rows(
                dq, cosine[:, cs], -sine[:, cs]
            ).astype(bf16)
            dv = contract(go, p.astype(bf16), 1, 1)
            dk = contract(q, ds, 1, 1)
            if t == 0:
                accv[...] = dv
                acck[...] = dk
            else:
                dk = (acck[...] + dk) * 0.125
                gproj[pl.ds(pl.multiple_of(at + 128, HEAD), HEAD), :] = rotate_rows(
                    dk, cosine[...], -sine[...]
                ).astype(bf16)
                gproj[pl.ds(pl.multiple_of(at + 256, HEAD), HEAD), :] = (accv[...] + dv).astype(bf16)

    def heads(i):
        head(2 * i)
        head(2 * i + 1)

        @pl.when(i == 1)
        def _():
            plane_m.middle(0)
            plane_m.begin(1)
            spread_lo.pass_first()

        @pl.when(i == 2)
        def _():
            plane_m.middle(3)
            plane_m.begin(2)

    loop(units, heads)
    line_m = LineSum(own_m, line_got_m, lm_send, lm_recv)
    line_a = LineSum(own_a, line_got_a, la_send, la_recv)
    plane_m.end(0, put_m)
    line_m.step(0, 0)
    loads["qkv"].wait()
    send[...] = contract(gproj[:, far], wqkv[...], 0, 0).astype(bf16)
    swap = remote(send, recv, send_sem.at[0], recv_sem.at[0], other, z)
    swap.start()
    gin[...] = contract(gproj[:, own], wqkv[...], 0, 0)
    loads["stream"].wait()
    loads["gmid"].wait()
    swap.wait()
    small[...] = jnp.zeros_like(small)

    def back(i):
        rs = tile(i, 128)
        ro = pl.ds(pl.multiple_of(core * half + i * 128, 128), 128)
        err = gin[rs, :] + recv[rs, :].astype(f32)
        grad, gain_grad = norm_back(stream[rs, :], attn_gain[...], err)
        grad = grad + gmid[rs, :]
        high = grad.astype(bf16)
        gin_low[rs, :] = high
        small[0:1, :] += gain_grad
        member = one_hot(seg_col[ro, :], 1)
        low = (grad - high.astype(f32)).astype(bf16)
        small[8:16, :] += (contract(member, high, 0, 0) + contract(member, low, 0, 0))[0:8]

    loop(4, back)
    spread_gin = Spread(gin_low, gathered_any, near_sem.at[1], gin_send, gin_recv)
    spread_gin.begin()
    plane_m.end(3, put_m)
    line_m.step(0, 3)
    line_m.step(1, 0)
    t_rows = small[8:16, :]
    mine[0:8, :] = jnp.concatenate(
        [
            small_m[0:3, :],
            small[0:1, :],
            jnp.sum(t_rows, axis=0, keepdims=True),
            jnp.zeros((3, t_rows.shape[1]), f32),
        ]
    )
    mine[8:16, :] = jnp.zeros((8, t_rows.shape[1]), f32)
    mine[16:24, :] = t_rows
    loads["normed"].wait()
    plane_a = PlaneSum(dwa_any, keep_a, got_a, last_a, pa_load, pa_send, pa_recv)
    order = (0, 3, 1, 2)

    def stored(i):
        return pltpu.make_async_copy(stage.at[i % 2], dwa_any.at[order[i]], stage_sem.at[i % 2])

    def weights(i):
        u = order[i]
        us = pl.ds(u * 384, 384)
        if i > 1:
            stored(i - 2).wait()
            plane_a.begin(order[i - 2])
        of_qkv = contract(gproj[us, :], normed[...], 1, 0).astype(bf16)
        of_out = contract(merged[pl.ds(u * 128, 128), :], gm[...], 1, 0).astype(bf16)
        for k in range(4):
            quarter = of_qkv[k * 128 : (k + 1) * 128] if k < 3 else of_out
            for j in range(2):
                stage[i % 2, 0, k // 2, k % 2, j] = quarter[j * 64 : (j + 1) * 64]
        stored(i).start()
        row = lax.broadcasted_iota(jnp.int32, (8, 1), 0) == core * units + u
        mine[8:16, 0:384] += jnp.where(
            row, contract(jnp.ones((8, BUCKET), bf16), gproj[us, :], 1, 1), 0.0
        )
        mine[8:16, 384:896] += jnp.where(row, bias_rows[u, :, 384:896], 0.0)

    little = SmallSum(mine, small_pair, small_line, small_x, small_y, sums, small_send, small_recv)

    def put_final_m(total):
        final[128:384, :] = total

    def put_final_a(total):
        final[0:128, :] = total

    if gather:
        gather_m = PlaneGather(final, parts, (128, 256), near_sem.at[2, 0], gm_send, gm_recv)
        gather_a = PlaneGather(final, parts, (0, 128), near_sem.at[3, 0], ga_send, ga_recv)
    weights(0)
    weights(1)
    plane_m.middle(1)
    spread_lo.pass_second()
    weights(2)
    weights(3)
    little.begin()
    line_m.step(1, 3)
    line_m.step(2, 0)
    plane_m.middle(2)
    for i in (2, 3):
        stored(i).wait()
        plane_a.begin(order[i])
    plane_m.end(1, put_m)
    line_m.step(0, 1)
    line_m.step(2, 3)
    little.step_line(meta[16:24, 0 : sums.shape[0] - 16])
    plane_m.end(2, put_m)
    line_m.step(0, 2)
    line_m.step(1, 1)
    spread_gin.pass_first()
    line_m.step(1, 2)
    plane_a.middle(0)
    plane_a.middle(3)
    little.step_across()
    plane_a.middle(1)
    plane_a.middle(2)
    line_m.finish(put_final_m)
    little.step_along()
    if gather:
        gather_m.begin()
    plane_a.end(0, put_a)
    line_a.step(0, 0)
    plane_a.end(3, put_a)
    line_a.step(0, 3)
    line_a.step(1, 0)
    plane_a.end(1, put_a)
    line_a.step(0, 1)
    line_a.step(1, 3)
    plane_a.end(2, put_a)
    line_a.step(0, 2)
    line_a.step(1, 1)
    line_a.step(1, 2)
    line_a.step(2, 0)
    line_a.step(2, 3)
    spread_gin.pass_second()
    if gather:
        gather_m.pass_on()
    line_a.finish(put_final_a)
    if gather:
        gather_a.begin()
        little.step_out()
        gather_a.pass_on()
        gather_m.finish()
        gather_a.finish()
    else:
        little.step_out()
        out = pltpu.make_async_copy(final, parts, near_sem.at[2, 0])
        out.start()
        out.wait()
    little.finish()
    spread_lo.finish()
    spread_gin.finish()
    for u in range(4):
        plane_m.drain(u)
        plane_a.drain(u)


def deliver_kernel(parts, gin, lo, sums, grad_in, lo_out, time_out, qkv_out, out_out, up_out, down_out):
    s = lax.rem(pl.program_id(0), 4)
    grad_in[...] = gin[...].astype(f32)
    lo_out[...] = lo[...]
    time_out[...] = sums[...]
    down_out[...] = parts[0, 0, 256:384, :].astype(f32)
    up_out[...] = parts[0, 0, 128:256, :].T.astype(f32)

    @pl.when(s < 3)
    def _():
        qkv_out[0] = parts[0, 0, 0:128, :].T.astype(f32)

    @pl.when(s == 3)
    def _():
        out_out[...] = parts[0, 0, 0:128, :].astype(f32)


def shape(s, t):
    return jax.ShapeDtypeStruct(s, t)


def run_forward(args, here, units, width):
    rows = BUCKET
    half = rows // 2
    feat = units * 128
    hid = units * 512
    anyspec = pl.BlockSpec(memory_space=pl.ANY)
    vm = pl.BlockSpec(memory_space=VMEM)
    outs = (
        shape((half, width), bf16),
        shape((half, width), f32),
        shape((rows, width), bf16),
        shape((half, width), f32),
        shape((rows, width), bf16),
        shape((feat, rows), bf16),
        shape((feat, rows), bf16),
        shape((feat, rows), bf16),
        shape((feat, rows), bf16),
        shape((2 * units, 1, rows), f32),
        shape((units, 2, 512, width), bf16),
        shape((hid, width), bf16),
        shape((8, width), f32),
        shape((units, 8, width), f32),
        shape((rows, 128), f32),
        shape((64, rows), f32),
        shape((24, width), f32),
    )
    dma = pltpu.SemaphoreType.DMA
    return pl.pallas_call(
        forward_kernel,
        out_shape=outs,
        in_specs=[anyspec] * 2 + [pl.BlockSpec(memory_space=pltpu.SMEM)] + [vm] * 9 + [anyspec] * 4,
        out_specs=[anyspec] * 12 + [vm] * 5,
        scratch_shapes=[
            VMEM((3 * hid, width), bf16),
            VMEM((rows, width), bf16),
            VMEM((rows, width), bf16),
            VMEM((8, 128), f32),
            VMEM((units, 8, 128), f32),
            VMEM((rows, width), f32),
            VMEM((rows, width), bf16),
            VMEM((feat, rows), bf16),
            VMEM((feat, rows), bf16),
            VMEM((feat, rows), bf16),
            VMEM((feat, rows), bf16),
            VMEM((2 * units, 1, rows), f32),
            VMEM((3, half, width), bf16),
            VMEM((3, half, width), bf16),
            VMEM((half, width), f32),
            VMEM((rows, width), bf16),
            VMEM((hid, rows), bf16),
            VMEM((hid, rows), bf16),
            VMEM((rows, width), bf16),
            VMEM((2, 512, width), bf16),
            VMEM((half, width), bf16),
            VMEM((half, width), f32),
            VMEM((3, width, 128), bf16),
            VMEM((rows, width), f32),
            dma((7,)),
            dma((3,)),
            dma((3,)),
            dma((3,)),
            dma((3,)),
            dma((9, 5)),
            dma((9, 5)),
            dma((12,)),
            dma((2,)),
            dma((5,)),
            dma((5,)),
        ],
        compiler_params=pltpu.CompilerParams(
            collective_id=0, has_side_effects=True, vmem_limit_bytes=63 * MIB
        ),
        name="forward",
    )(*args)


def run_backward(args, gather, here, units, rows, width, n_time):
    half = rows // 2
    feat = units * 128
    anyspec = pl.BlockSpec(memory_space=pl.ANY)
    vm = pl.BlockSpec(memory_space=VMEM)
    dma = pltpu.SemaphoreType.DMA
    return pl.pallas_call(
        functools.partial(backward_kernel, gather),
        out_shape=(
            shape((here * rows, width), bf16),
            shape((units, 1, 2, 2, 2, 64, width), bf16),
            shape((here * rows, width), bf16),
            shape((2, 4, 384, width) if gather else (384, width), bf16),
            shape((n_time + 16, width), f32),
        ),
        in_specs=[vm] * 7 + [anyspec] * (len(args) - 7),
        out_specs=[anyspec] * 4 + [vm],
        scratch_shapes=[
            VMEM((4 * feat, width), bf16),
            VMEM((half, width), f32),
            VMEM((rows, width), bf16),
            VMEM((half, width), f32),
            VMEM((rows, width), bf16),
            VMEM((feat, rows), bf16),
            VMEM((feat, rows), bf16),
            VMEM((feat, rows), bf16),
            VMEM((feat, rows), bf16),
            VMEM((feat, rows), bf16),
            VMEM((3 * feat, rows), bf16),
            VMEM((HEAD, rows), f32),
            VMEM((HEAD, rows), f32),
            VMEM((half, width), bf16),
            VMEM((half, width), bf16),
            VMEM((half, width), f32),
            VMEM((2, 1, 2, 2, 2, 64, width), bf16),
            VMEM((half, width), bf16),
            VMEM((16, width), f32),
            VMEM((24, width), f32),
            VMEM((2, units, 2, 2, 64, width), bf16),
            VMEM((2, units, 2, 2, 64, width), bf16),
            VMEM((2, units, 2, 64, width), bf16),
            VMEM((2, units, 1, 2, 64, width), bf16),
            VMEM((2, units, 1, 2, 64, width), bf16),
            VMEM((2, units, 1, 64, width), bf16),
            VMEM((units, 256, width), bf16),
            VMEM((2, 3, 256, width), bf16),
            VMEM((units, 128, width), bf16),
            VMEM((2, 3, 128, width), bf16),
            VMEM((384, width), bf16),
            VMEM((24, width // 2), f32),
            VMEM((4, 24, width // 2 + n_time), f32),
            VMEM((2, 48, width // 2 + n_time), f32),
            VMEM((2, 80, width // 2 + n_time), f32),
            dma((10,)),
            dma((2,)),
            dma((1,)),
            dma((1,)),
            dma((4, 1)),
            dma((7,)),
            dma((4,)),
            dma((7,)),
            dma((4,)),
            dma((2, units)),
            dma((2, 2, units)),
            dma((2, 2, units)),
            dma((2, units)),
            dma((2, 2, units)),
            dma((2, 2, units)),
            dma((2, 3)),
            dma((2, 3)),
            dma((2, 3)),
            dma((2, 3)),
            dma((8,)),
            dma((8,)),
            dma((8,)),
            dma((8,)),
            dma((7,)),
            dma((7,)),
        ],
        compiler_params=pltpu.CompilerParams(
            collective_id=1, has_side_effects=True, vmem_limit_bytes=63 * MIB
        ),
        name="backward",
    )(*args)


def run_deliver(parts, gin, lo, sums, n_time):
    rows, width = gin.shape
    steps = 8
    part = parts.shape[2] // 3
    hid = steps * part
    at = lambda i: (i, 0)
    return pl.pallas_call(
        deliver_kernel,
        grid=(steps,),
        out_shape=(
            shape((rows, width), f32),
            shape((rows, width), bf16),
            shape((n_time, width), f32),
            shape((3, width, 2 * part), f32),
            shape((2 * part, width), f32),
            shape((width, hid), f32),
            shape((hid, width), f32),
        ),
        in_specs=[
            pl.BlockSpec((1, 1, 3 * part, width), lambda i: (i // 4, i % 4, 0, 0)),
            pl.BlockSpec((rows // steps, width), at),
            pl.BlockSpec((rows // steps, width), at),
            pl.BlockSpec((n_time // steps, width), at),
        ],
        out_specs=[
            pl.BlockSpec((rows // steps, width), at),
            pl.BlockSpec((rows // steps, width), at),
            pl.BlockSpec((n_time // steps, width), at),
            pl.BlockSpec((1, width, part), lambda i: (jnp.minimum(i % 4, 2), 0, i // 4)),
            pl.BlockSpec((part, width), lambda i: (i // 4, 0)),
            pl.BlockSpec((width, part), lambda i: (0, i)),
            pl.BlockSpec((part, width), at),
        ],
        compiler_params=pltpu.CompilerParams(vmem_limit_bytes=48 * MIB),
        name="deliver",
    )(parts, gin, lo, sums)


def local(
    ndp, nmp, activations, noise_embed, lengths, time_weight, time_bias, attn_gain, qkv_weight, qkv_bias,
    out_weight, out_bias, mlp_gain, up_weight, up_bias, down_weight, down_bias, cotangent,
):
    width = activations.shape[1]
    here = activations.shape[0] // BUCKET
    assert 2 * here == nmp and qkv_weight.shape[2] == 256 and up_weight.shape[1] == 1024
    assert ndp % 8 == 0 and noise_embed.shape[0] == here * SLOTS
    n_time = time_weight.shape[0]
    def row(v):
        return v.reshape(1, width)

    (
        lo, gmid, gm, stream, normed, qt, kt, vt, merged, lse, dwm, wqo, small_m, bias_rows, seg_col, trig, meta,
    ) = run_forward(
        (
            activations, cotangent, lengths, noise_embed, time_weight, row(time_bias), row(attn_gain),
            row(out_bias), row(mlp_gain), row(down_bias), qkv_bias, up_bias.reshape(8, 128),
            qkv_weight.transpose(1, 0, 2), out_weight, up_weight, down_weight,
        ),
        here, nmp, width,
    )
    gather = ndp == 8
    lo_all, _, gathered, parts, sums = run_backward(
        (
            meta, seg_col, trig, row(attn_gain), small_m, bias_rows, lse, wqo, gmid, gm, stream, normed, qt, kt, vt,
            merged, lo, dwm.reshape(nmp, 2, 2, 2, 2, 64, width),
        ),
        gather, here, nmp, BUCKET, width, n_time,
    )
    if not gather:
        groups = [[i + 8 * k for k in range(ndp // 8)] for i in range(8)]
        parts = lax.psum(parts, "dp", axis_index_groups=groups)
        sums = lax.psum(sums, "dp", axis_index_groups=groups)
        groups = [[8 * k + i for i in range(8)] for k in range(ndp // 8)]
        parts = lax.all_gather(parts, "dp", axis_index_groups=groups)
        parts = parts.reshape(4, 2, 384, width).transpose(1, 0, 2, 3)
    grad_input, layer_output, grad_time_weight, grad_qkv, grad_out, grad_up, grad_down = run_deliver(
        parts, gathered, lo_all, sums, n_time
    )
    grad_qkv = grad_qkv.transpose(1, 0, 2)
    grad_mlp_gain, grad_out_bias, grad_down_bias, grad_attn_gain, grad_time_bias = (
        sums[n_time + i] for i in range(5)
    )
    bias_sums = sums[n_time + 8 :].reshape(2, nmp, width)
    bias_sums = lax.dynamic_index_in_dim(bias_sums, lax.axis_index("mp"), 1, keepdims=False)
    grad_qkv_bias = bias_sums[:, :384].reshape(2, 3, 128).transpose(1, 0, 2).reshape(3, 256)
    grad_up_bias = bias_sums[:, 384:896].reshape(-1)
    return (
        layer_output,
        grad_input,
        grad_time_weight,
        grad_time_bias,
        grad_attn_gain,
        grad_qkv,
        grad_qkv_bias,
        grad_out,
        grad_out_bias,
        grad_mlp_gain,
        grad_up,
        grad_up_bias,
        grad_down,
        grad_down_bias,
    )


def solution(mesh):
    in_specs = (
        P("dp", None),
        P("dp", None),
        P("dp"),
        P(),
        P(),
        P(),
        P(None, None, "mp"),
        P(None, "mp"),
        P("mp", None),
        P(),
        P(),
        P(None, "mp"),
        P("mp"),
        P("mp", None),
        P(),
        P("dp", None),
    )
    out_specs = (
        P("dp", None),
        P("dp", None),
        P(),
        P(),
        P(),
        P(None, None, "mp"),
        P(None, "mp"),
        P("mp", None),
        P(),
        P(),
        P(None, "mp"),
        P("mp"),
        P("mp", None),
        P(),
    )
    body = functools.partial(local, mesh.shape["dp"], mesh.shape["mp"])
    return jax.shard_map(body, mesh=mesh, in_specs=in_specs, out_specs=out_specs, check_vma=False)
```

```python
import functools
import math

import jax
import jax.numpy as jnp
from jax import lax
from jax.experimental import pallas as pl
from jax.experimental.pallas import tpu as pltpu
from jax.sharding import PartitionSpec as P

HEAD = 64
BUCKET = 1024
SLOTS = 8
MIB = 1 << 20
MESH = pl.DeviceIdType.MESH
VMEM = pltpu.VMEM
bf16 = jnp.bfloat16
f32 = jnp.float32


def contract(a, b, ca, cb):
    return lax.dot_general(a, b, (((ca,), (cb,)), ((), ())), preferred_element_type=f32)


def tile(i, n):
    return pl.ds(pl.multiple_of(i * n, n), n)


def loop(n, body):
    def step(i, carry):
        body(i)
        return carry

    lax.fori_loop(0, n, step, 0)


def row_stats(v):
    centered = v - jnp.mean(v, axis=-1, keepdims=True)
    return centered, lax.rsqrt(jnp.mean(centered * centered, axis=-1, keepdims=True) + 1e-05)


def norm_back(v, gain, err):
    centered, scale = row_stats(v)
    xhat = centered * scale
    u = err * gain
    grad = (
        u - jnp.mean(u, axis=-1, keepdims=True) - xhat * jnp.mean(u * xhat, axis=-1, keepdims=True)
    ) * scale
    return grad, jnp.sum(err * xhat, axis=0, keepdims=True)


def toggled(v, bit):
    return v + bit - 2 * bit * lax.rem(v // bit, 2)


def peer(z, m):
    low = lax.rem(lax.rem(z, 2) + m % 2, 2)
    return low + 2 * lax.rem(z // 2 + m // 2, 2)


def greet(targets):
    barrier = pltpu.get_barrier_semaphore()
    for d, z in targets:
        pl.semaphore_signal(barrier, inc=1, device_id={"dp": d, "mp": z}, device_id_type=MESH)
    pl.semaphore_wait(barrier, len(targets))


def remote(src, dst, ss, rs, d, z):
    return pltpu.make_async_remote_copy(
        src_ref=src,
        dst_ref=dst,
        send_sem=ss,
        recv_sem=rs,
        device_id={"dp": d, "mp": z},
        device_id_type=MESH,
    )


class Spread:
    def __init__(self, src, out, near_sem, send_sem, recv_sem):
        me, z = lax.axis_index("dp"), lax.axis_index("mp")
        self.core = core = lax.rem(me, 2)
        self.kind = kind = z // 2
        self.place = z + core * (3 - 2 * z)
        self.start_place = z + kind * (3 - 2 * z)
        self.out, self.send, self.recv = out, send_sem, recv_sem
        self.me, self.z, self.ahead = me, z, z + 1 - 2 * core
        keeper = me - core + kind
        dst = self.piece(self.start_place, core, kind)
        rs = recv_sem.at[2 * self.start_place + core]
        self.near = pltpu.make_async_copy(src, dst, near_sem.at[0])
        self.first = [
            remote(src, dst, send_sem.at[0], rs, keeper, z + 1 - 2 * kind),
            remote(src, dst, send_sem.at[1], rs, keeper, z - 1 + 2 * kind),
            remote(src, dst, send_sem.at[2], rs, toggled(me, 1), z),
        ]

    def piece(self, m, h, kind):
        rows = self.out.shape[0] // 4
        at = 2 * (m + kind * (1 - 2 * m)) + h
        return self.out.at[pl.ds(pl.multiple_of(at * rows, rows), rows), :]

    def hop(self, m, h, i):
        ref = self.piece(m, h, self.core)
        return remote(ref, ref, self.send.at[i], self.recv.at[2 * m + h], self.me, self.ahead)

    def begin(self):
        self.first[0].start()

        @pl.when(self.start_place == 1)
        def _():
            self.first[1].start()

        @pl.when(self.core == self.kind)
        def _():
            self.near.start()

        @pl.when(self.core != self.kind)
        def _():
            self.first[2].start()

    def forward(self, place, m, i):
        @pl.when(self.place == place)
        def _():
            for h in range(2):
                self.hop(m, h, i + h).wait_recv()
                self.hop(m, h, i + h).start()

    def pass_first(self):
        self.forward(1, 0, 3)
        self.forward(2, 1, 3)

    def pass_second(self):
        self.forward(2, 0, 5)

    def finish(self):
        @pl.when(self.core == self.kind)
        def _():
            self.near.wait()
            self.hop(self.place, 1 - self.core, 3).wait_recv()

        @pl.when(self.core != self.kind)
        def _():
            self.first[2].wait_send()

        @pl.when(self.place == 0)
        def _():
            for h in range(2):
                self.hop(1, h, 3).wait_recv()

        @pl.when(self.place == 3)
        def _():
            for m in range(2):
                for h in range(2):
                    self.hop(m, h, 3).wait_recv()

        self.first[0].wait_send()

        @pl.when(self.start_place == 1)
        def _():
            self.first[1].wait_send()

        for place, m, i in ((1, 0, 3), (2, 1, 3), (2, 0, 5)):

            @pl.when(self.place == place)
            def _(m=m, i=i):
                for h in range(2):
                    self.hop(m, h, i + h).wait_send()


class PlaneSum:
    def __init__(self, src, keep, got, last, load_sem, send_sem, recv_sem):
        me, z = lax.axis_index("dp"), lax.axis_index("mp")
        self.x, self.y = lax.rem(me // 2, 2), lax.rem(me // 4, 2)
        self.z, self.across, self.along = z, toggled(me, 2), toggled(me, 4)
        self.src, self.keep, self.got, self.last = src, keep, got, last
        self.load_sem, self.send_sem, self.recv_sem = load_sem, send_sem, recv_sem

    def part(self, u, order, mine):
        x = self.x if mine else 1 - self.x
        y = self.y if mine else 1 - self.y
        return self.src.at[u, :, :, x, 0] if order == 0 else self.src.at[u, :, y, :, 1]

    def load(self, u, order):
        return pltpu.make_async_copy(
            self.part(u, order, True), self.keep.at[order, u], self.load_sem.at[order, u]
        )

    def hop(self, u, order, stage):
        if stage == 0:
            src, dst = self.part(u, order, False), self.got.at[order, u]
        else:
            there = 1 - (self.y if order == 0 else self.x)
            src, dst = self.keep.at[order, u, :, there], self.last.at[order, u]
        to = self.across if order == stage else self.along
        return remote(
            src, dst, self.send_sem.at[order, stage, u], self.recv_sem.at[order, stage, u], to, self.z
        )

    def begin(self, u):
        for order in range(2):
            self.load(u, order).start()
            self.hop(u, order, 0).start()

    def middle(self, u):
        for order in range(2):
            self.load(u, order).wait()
            self.hop(u, order, 0).wait_recv()
            total = self.keep[order, u].astype(f32) + self.got[order, u].astype(f32)
            self.keep[order, u] = total.astype(bf16)
            self.hop(u, order, 1).start()

    def end(self, u, put):
        for order in range(2):
            self.hop(u, order, 1).wait_recv()
            here = self.y if order == 0 else self.x
            total = self.keep[order, u, :, here].astype(f32) + self.last[order, u].astype(f32)
            put(u, order, total.astype(bf16))

    def drain(self, u):
        for order in range(2):
            for stage in range(2):
                self.hop(u, order, stage).wait_send()


class LineSum:
    def __init__(self, own, got, send_sem, recv_sem):
        self.me, self.z = lax.axis_index("dp"), lax.axis_index("mp")
        self.own, self.got, self.send_sem, self.recv_sem = own, got, send_sem, recv_sem

    def hop(self, way, t):
        entry = t if way == 0 else 3 - t
        return remote(
            self.own.at[entry], self.got.at[way, t - 1], self.send_sem.at[way, t - 1],
            self.recv_sem.at[way, t - 1], self.me, self.z + 1 - 2 * way,
        )

    def step(self, s, entry):
        for way in range(2):
            t = entry if way == 0 else 3 - entry
            if s >= t:
                continue

            @pl.when(self.z == (s if way == 0 else 3 - s))
            def _(way=way, t=t):
                if s > 0:
                    self.hop(way, t).wait_recv()
                    total = self.own[entry].astype(f32) + self.got[way, t - 1].astype(f32)
                    self.own[entry] = total.astype(bf16)
                self.hop(way, t).start()

    def finish(self, put):
        for way in range(2):
            for t in range(1, 4):

                @pl.when(self.z == (t if way == 0 else 3 - t))
                def _(way=way, t=t):
                    self.hop(way, t).wait_recv()
                    entry = t if way == 0 else 3 - t
                    total = self.own[entry].astype(f32) + self.got[way, t - 1].astype(f32)
                    self.own[entry] = total.astype(bf16)

        put(self.own[self.z])
        for way in range(2):
            for s in range(3):

                @pl.when(self.z == (s if way == 0 else 3 - s))
                def _(way=way, s=s):
                    for t in range(3, s, -1):
                        self.hop(way, t).wait_send()


class PlaneGather:
    def __init__(self, final, parts, rows, own_sem, send_sem, recv_sem):
        me, self.z = lax.axis_index("dp"), lax.axis_index("mp")
        self.core, self.col = lax.rem(me, 2), lax.rem(me // 2, 4)
        self.other, self.across, self.along = toggled(me, 1), toggled(me, 2), toggled(me, 4)
        self.parts, self.rows = parts, rows
        self.send_sem, self.recv_sem = send_sem, recv_sem
        self.cols = (
            self.col, toggled(self.col, 1), toggled(self.col, 2), toggled(toggled(self.col, 1), 2),
        )
        src = final.at[pl.ds(rows[0], rows[1]), :]
        self.near = pltpu.make_async_copy(src, self.slot(self.core, self.col), own_sem)
        self.hops = [
            self.hop(self.slot(self.core, self.col), 4, self.across, src),
            self.hop(self.slot(self.core, self.col), 5, self.along, src),
            self.hop(self.slot(self.core, self.col), 0, self.other, src),
        ]

    def slot(self, c, s, h=None):
        at, n = self.rows
        if h is not None:
            at, n = at + h * (n // 2), n // 2
        return self.parts.at[c, s, pl.ds(at, n), :]

    def hop(self, dst, i, to, src=None):
        src = dst if src is None else src
        return remote(src, dst, self.send_sem.at[i], self.recv_sem.at[i], to, self.z)

    def begin(self):
        for c in self.hops:
            c.start()
        self.near.start()

    def pass_on(self):
        for j, (i, ahead, h, k) in enumerate(((4, self.along, 0, 6), (5, self.across, 1, 7))):
            s = self.cols[1 + j]
            self.hop(self.slot(self.core, s), i, self.other).wait_recv()
            more = [
                self.hop(self.slot(self.core, s, h), k, ahead),
                self.hop(self.slot(self.core, s), 1 + j, self.other),
            ]
            for c in more:
                c.start()
            self.hops += more

    def finish(self):
        s = self.cols[3]
        for h in range(2):
            self.hop(self.slot(self.core, s, h), 6 + h, self.other).wait_recv()
        last = self.hop(self.slot(self.core, s), 3, self.other)
        last.start()
        self.near.wait()
        for i in range(4):
            self.hop(self.slot(1 - self.core, self.cols[i]), i, self.other).wait_recv()
        for c in self.hops + [last]:
            c.wait_send()


class SmallSum:
    def __init__(self, mine, pair, line, across, along, out, send_sem, recv_sem):
        me, self.z = lax.axis_index("dp"), lax.axis_index("mp")
        self.me, self.core = me, lax.rem(me, 2)
        self.x, self.y = lax.rem(me // 2, 2), lax.rem(me // 4, 2)
        self.mine, self.pair, self.line, self.a, self.b, self.out = mine, pair, line, across, along, out
        self.send_sem, self.recv_sem = send_sem, recv_sem
        n = pair.shape[1]
        self.n = n
        self.lanes = pl.ds(pl.multiple_of(self.core * n, n), n)
        there = pl.ds(pl.multiple_of((1 - self.core) * n, n), n)

        def move(src, dst, i, d, z):
            return remote(src, dst, send_sem.at[i], recv_sem.at[i], d, z)

        other = toggled(me, 1)
        self.swap = move(mine.at[:, there], pair, 0, other, self.z)
        slot = line.at[self.z]
        self.hops = [move(slot, slot, m, me, peer(self.z, m)) for m in (1, 2, 3)]
        self.hop_x = move(across.at[self.x], across.at[self.x], 4, toggled(me, 2), self.z)
        self.hop_y = move(along.at[self.y], along.at[self.y], 5, toggled(me, 4), self.z)
        done = out.at[:, self.lanes]
        self.last = move(done, done, 6, other, self.z)

    def begin(self):
        self.swap.start()

    def step_line(self, noise):
        n, width = self.n, noise.shape[1]
        self.swap.wait()
        self.line[self.z, :, 0:n] = self.mine[:, self.lanes] + self.pair[...]
        self.line[self.z, 16:24, n : n + width] = noise
        self.line[self.z, 0:16, n : n + width] = jnp.zeros((16, width), f32)
        for c in self.hops:
            c.start()

    def step_across(self):
        for c in self.hops:
            c.wait()
        v = [self.line[i] for i in range(4)]
        self.a[self.x, 0:16, :] = ((v[0] + v[1]) + (v[2] + v[3]))[0:16]
        for i in range(4):
            self.a[self.x, 16 + 8 * i : 24 + 8 * i, :] = v[i][16:24]
        self.hop_x.start()

    def step_along(self):
        self.hop_x.wait()
        self.b[self.y, 0:16, :] = self.a[0, 0:16, :] + self.a[1, 0:16, :]
        for i in range(2):
            self.b[self.y, 16 + 32 * i : 48 + 32 * i, :] = self.a[i, 16:48, :]
        self.hop_y.start()

    def step_out(self):
        self.hop_y.wait()
        n, n_time = self.n, self.out.shape[0] - 16
        self.out[n_time : n_time + 16, self.lanes] = self.b[0, 0:16, 0:n] + self.b[1, 0:16, 0:n]
        rows = jnp.concatenate([self.b[0, 16:80, :], self.b[1, 16:80, :]])
        grads, noise = rows[:, 0:n], rows[:, n : n + n_time].astype(bf16)
        high = grads.astype(bf16)
        rest = grads - high.astype(f32)
        middle = rest.astype(bf16)
        low = (rest - middle.astype(f32)).astype(bf16)
        total = contract(noise, high, 0, 0) + contract(noise, middle, 0, 0)
        self.out[0:n_time, self.lanes] = total + contract(noise, low, 0, 0)
        self.last.start()

    def finish(self):
        self.last.wait()


def one_hot(seg, copies):
    lanes = lax.broadcasted_iota(jnp.int32, (1, 128), 1)
    lanes = jnp.where(lanes < 16 * copies, lax.rem(lanes, 16), -1).astype(f32)
    return jnp.where(seg == lanes, 1.0, 0.0).astype(bf16)


def rotate_rows(v, cosine, sine):
    a, b = v[: HEAD // 2], v[HEAD // 2 :]
    return jnp.concatenate([a * cosine - b * sine, b * cosine + a * sine], axis=0)


def forward_kernel(
    act_any, cot_any, lens, noise, time_weight, time_bias, attn_gain, out_bias, mlp_gain, down_bias,
    qkv_bias, up_bias, qkv_any, ow_any, uw_any, dn_any,
    out_any, mid_any, gfin_any, acc_any, gp_any, wup_any, stream_any, normed_any, q_any, k_any, v_any, merged_any,
    lse_any, dwm_any, wqo_any, bias_rows, seg_col, trig, meta,
    w, x, gfin, bias, biases, stream, normed, qt, kt, vt, merged, lse, send, recv, mid, nm, act, gp,
    stage, lo, slopes, raw_qkv, acc,
    load_sem, bring_send, bring_recv, bias_send, bias_recv, w_send, w_recv,
    out_sem, stage_sem, send_sem, recv_sem,
):
    me, z = lax.axis_index("dp"), lax.axis_index("mp")
    core, col = lax.rem(me, 2), lax.rem(me // 2, 4)
    other, across, along = toggled(me, 1), toggled(me, 2), toggled(me, 4)
    here = act_any.shape[0] // BUCKET
    units = biases.shape[0]
    half = BUCKET // 2
    own, far = tile(core, half), tile(1 - core, half)
    mine = core == z // here
    up_at, dn_at, out_at = units * 512, units * 1024, units * 384

    def block(start, n):
        return pl.ds(pl.multiple_of(start, n), n)

    loads = [
        pltpu.make_async_copy(s, d, load_sem.at[i])
        for i, (s, d) in enumerate(
            (
                (qkv_any.at[:, :, block(core * 128, 128)], raw_qkv),
                (ow_any.at[block(core * 128, 128), :], w.at[block(out_at + z * 128, 128), :]),
                (uw_any.at[:, block(core * 512, 512)], nm.at[:, pl.ds(0, 512)]),
                (dn_any.at[block(core * 512, 512), :], w.at[block(dn_at + z * 512, 512), :]),
            )
        )
    ]
    for c in loads:
        c.start()
    greet([(other, z), (across, z), (along, z)] + [(me, peer(z, m)) for m in (1, 2, 3)])

    bucket_at = lax.rem(z, here)
    bucket = pl.ds(pl.multiple_of(bucket_at * BUCKET, BUCKET), BUCKET)
    brought = (
        (meta, meta),
        (act_any.at[bucket, :], x),
        (cot_any.at[bucket, :], gfin),
    )

    def bring(i, begin):
        src, dst = brought[i]
        near = None if i == 0 else pltpu.make_async_copy(src, dst, load_sem.at[4 + i])
        sent = remote(src, dst, bring_send.at[i], bring_recv.at[i], other, z)

        @pl.when(mine)
        def _():
            if begin:
                sent.start()
                if near is not None:
                    near.start()
            else:
                if near is not None:
                    near.wait()
                sent.wait_send()

        if not begin:

            @pl.when(jnp.logical_not(mine))
            def _():
                sent.wait_recv()

    def row_of(k, u, s):
        if k == 0:
            return u * 384 + 128 * s + (s // 3) * (out_at - 384 + 128 * u - 384 * u)
        return (up_at if k == 1 else dn_at) + u * 512 + 128 * s

    def diagonal(k, m):
        return k == 2 and m > 1

    far_col = toggled(toggled(col, 1), 2)

    def hop(k, m, way):
        i = 3 * k + m - 1
        u = peer(z, m)
        from_hbm = False
        if way == 0 or (way == 3 and diagonal(k, m)):
            s = col if way == 0 else far_col
            n, d = 128, me
            if m == 3:
                at, zz = row_of(k, peer(z, 2), s), peer(z, 1)
            else:
                at, zz, from_hbm = row_of(k, z, s), u, k == 2
        elif way == 1:
            at, n, d, zz = row_of(k, u, col), 128, across, z
        elif way == 2:
            at, n, d, zz = row_of(k, u, col), 128, along, z
        elif way == 3:
            at, n, d, zz = row_of(k, u, toggled(col, 1)), 64, along, z
        else:
            at, n, d, zz = row_of(k, u, toggled(col, 2)) + 64, 64, across, z
        rows = w.at[block(at, n), :]
        src = dn_any.at[block(core * 512 + s * 128, 128), :] if from_hbm else rows
        return remote(src, rows, w_send.at[i, way], w_recv.at[i, way], d, zz)

    def arrived(k, m, way):
        i = 3 * k + m - 1
        u = peer(z, m)
        s = (col, toggled(col, 1), toggled(col, 2), far_col, far_col)[way]
        at = row_of(k, u, s) + (64 if way == 4 else 0)
        rows = w.at[block(at, 128 if way < 3 or diagonal(k, m) else 64), :]
        remote(rows, rows, w_send.at[i, way], w_recv.at[i, way], other, z).wait_recv()

    def send_z(k, m):
        hop(k, m, 0).start()
        if diagonal(k, m):
            hop(k, m, 3).start()

    def pass_a(k, m):
        arrived(k, m, 0)
        if m == 2:
            hop(k, 3, 0).start()
        hop(k, m, 1).start()
        hop(k, m, 2).start()
        if m == 2 and diagonal(k, 3):
            arrived(k, m, 3)
            hop(k, 3, 3).start()

    def pass_b(k, m):
        arrived(k, m, 1)
        if not diagonal(k, m):
            hop(k, m, 3).start()
        arrived(k, m, 2)
        if not diagonal(k, m):
            hop(k, m, 4).start()

    def pass_c(k, m):
        if not (diagonal(k, m) and m == 2):
            arrived(k, m, 3)
        if not diagonal(k, m):
            arrived(k, m, 4)

    bring(1, True)
    for c in range(2):

        @pl.when(core == c)
        def _(c=c):
            bias[0:3, :] = qkv_bias[:, c * 128 : (c + 1) * 128]
            bias[3:4, :] = jnp.zeros((1, 128), f32)
            bias[4:8, :] = up_bias[c * 4 : (c + 1) * 4, :]

    biases[z] = bias[...]
    bias_hops = [
        remote(bias, biases.at[z], bias_send.at[m - 1], bias_recv.at[m - 1], me, peer(z, m))
        for m in (1, 2, 3)
    ]

    loads[0].wait()
    for i in range(3):
        w[block(z * 384 + i * 128, 128), :] = raw_qkv[i].T
    loads[1].wait()
    send_z(0, 1)

    @pl.when(mine)
    def _():
        places = lax.broadcasted_iota(jnp.int32, (1, BUCKET), 1)
        past, start, end = jnp.zeros_like(places), jnp.zeros_like(places), 0
        for i in range(SLOTS):
            end = end + lens[bucket_at * SLOTS + i]
            beyond = places >= end
            past = past + beyond.astype(jnp.int32)
            start = jnp.where(beyond, end, start)
        live = places < end
        meta[8:9, :] = jnp.where(live, past, 2000 + places).astype(f32)
        meta[9:10, :] = (places - jnp.where(live, start, 0)).astype(f32)
        rows = jnp.dot(noise[...], time_weight[...], preferred_element_type=f32) + time_bias[...]
        first = bucket_at == 0
        meta[0:8, :] = jnp.where(first, rows[0:SLOTS], rows[SLOTS : 2 * SLOTS])
        loud = noise[...].astype(f32)
        meta[16:24, 0 : loud.shape[1]] = jnp.where(first, loud[0:SLOTS], loud[SLOTS : 2 * SLOTS])

    bring(0, True)
    bring(2, True)
    for c in bias_hops:
        c.start()
    loads[2].wait()
    for i in range(4):
        w[block(up_at + z * 512 + i * 128, 128), :] = nm[:, i * 128 : (i + 1) * 128].T
    loads[3].wait()
    send_z(0, 2)

    saves = []

    def save(src, dst):
        c = pltpu.make_async_copy(src, dst, out_sem.at[len(saves)])
        c.start()
        saves.append(c)

    def swap(src, dst, i):
        c = remote(src, dst, send_sem.at[i], recv_sem.at[i], other, z)
        c.start()
        return c

    bring(0, False)
    seg_col[...] = jnp.broadcast_to(meta[8:9, :], (128, BUCKET)).T
    step = lax.broadcasted_iota(jnp.int32, (HEAD // 2, 1), 0).astype(f32)
    angles = jnp.exp(step * (-2.0 * math.log(10000.0) / HEAD)) * meta[9:10, :]
    trig[0:32, :] = jnp.cos(angles)
    trig[32:64, :] = jnp.sin(angles)
    pass_a(0, 1)
    send_z(1, 1)
    t_rows = meta[0:8, :]
    high = t_rows.astype(bf16).astype(f32)
    middle_part = (t_rows - high).astype(bf16).astype(f32)
    lowest = t_rows - high - middle_part
    gap = jnp.zeros((8, t_rows.shape[1]), f32)
    time_rows = jnp.concatenate(
        [high, gap, middle_part, gap, lowest, gap, jnp.zeros((80, t_rows.shape[1]), f32)]
    ).astype(bf16)
    bring(1, False)

    def enter(i):
        rs = tile(i, 256)
        added = jnp.dot(one_hot(seg_col[rs, :], 3), time_rows, preferred_element_type=f32)
        stream[rs, :] = x[rs, :].astype(f32) + added

    loop(4, enter)

    def norm(i):
        rs = tile(i, 128)
        centered, scale = row_stats(stream[rs, :])
        normed[rs, :] = (centered * scale * attn_gain[...]).astype(bf16)

    loop(8, norm)
    save(normed, normed_any)
    save(stream.at[own, :], stream_any)
    stream_saved = saves[-1]

    def bias_column(u, s):
        return jnp.broadcast_to(biases[u, s : s + 1, :], (128, 128)).T[:, 0:1]

    def unit(u, between):
        column = jnp.concatenate([bias_column(u, s) for s in range(3)], axis=0)
        proj = contract(w[block(u * 384, 384), :], normed[...], 1, 1) + column
        cs, sn = trig[0:32, :], trig[32:64, :]
        us = tile(u, 128)
        qt[us, :] = jnp.concatenate(
            [rotate_rows(proj[h * HEAD : (h + 1) * HEAD], cs, sn) for h in range(2)], axis=0
        ).astype(bf16)
        kt[us, :] = jnp.concatenate(
            [rotate_rows(proj[128 + h * HEAD : 128 + (h + 1) * HEAD], cs, sn) for h in range(2)],
            axis=0,
        ).astype(bf16)
        vt[us, :] = proj[256:384].astype(bf16)

        def head(j):
            h = 2 * u + j
            hs = tile(h, HEAD)
            keys = (kt[hs, :].astype(f32) * 0.125).T.astype(bf16)
            values = vt[hs, :]
            for t in range(2):
                cs_t = pl.ds(t * 512, 512)
                s = jnp.dot(keys, qt[hs, cs_t], preferred_element_type=f32)
                same = jnp.tile(seg_col[...], (1, 4)) == meta[8:9, cs_t]
                s = jnp.where(same, s, -1e30)
                top = jnp.max(s, axis=0, keepdims=True)
                p = jnp.exp(s - top)
                total = jnp.sum(p, axis=0, keepdims=True)
                o = jnp.dot(values, p.astype(bf16), preferred_element_type=f32)
                merged[hs, cs_t] = (o / total).astype(bf16)
                lse[h, :, cs_t] = top + jnp.log(total)

        for j in range(2):
            for step in between[j]:
                step[0](*step[1:])
            head(j)

    pass_a(0, 2)
    send_z(2, 1)
    for c in bias_hops:
        c.wait()
    unit(z, (((pass_b, 0, 1),), ((pass_a, 0, 3), (send_z, 1, 2))))
    pass_b(0, 2)
    pass_c(0, 1)
    unit(peer(z, 1), (((pass_a, 1, 1), (send_z, 2, 2)), ((pass_b, 0, 3), (pass_c, 0, 2))))
    unit(peer(z, 2), (((pass_a, 2, 1),), ((pass_b, 1, 1), (pass_c, 0, 3))))
    unit(peer(z, 3), (((pass_a, 1, 2), (pass_c, 1, 1)), ((pass_b, 2, 1),)))
    pass_a(2, 2)
    save(qt, q_any)
    save(kt, k_any)
    save(vt, v_any)
    save(merged, merged_any)
    save(lse, lse_any)
    save(w.at[pl.ds(0, up_at), :], wqo_any)

    w_out = w.at[pl.ds(out_at, units * 128), :]
    w_up = w.at[pl.ds(up_at, units * 512), :]
    w_dn = w.at[pl.ds(dn_at, units * 512), :]
    send[0] = contract(merged[:, far], w_out[...], 0, 0).astype(bf16)
    swap0 = swap(send.at[0], recv.at[0], 0)
    mid[...] = contract(merged[:, own], w_out[...], 0, 0)
    bring(2, False)

    def mask(i):
        rs = tile(i, 256)
        live = jnp.where(seg_col[rs, :][:, 0:1] < 1000.0, 1.0, 0.0)
        gfin[rs, :] = (gfin[rs, :].astype(f32) * live).astype(bf16)

    loop(4, mask)
    swap0.wait()

    def middle(i):
        rs = tile(i, 128)
        ro = pl.ds(pl.multiple_of(core * half + i * 128, 128), 128)
        v = stream[ro, :] + (mid[rs, :] + recv[0, rs, :].astype(f32)) + out_bias[...]
        mid[rs, :] = v
        centered, scale = row_stats(v)
        nm[ro, :] = (centered * scale * mlp_gain[...]).astype(bf16)

    loop(4, middle)
    save(mid, mid_any)
    save(gfin.at[own, :], gfin_any)
    swap1 = swap(nm.at[own, :], nm.at[own, :], 1)
    pass_c(2, 1)
    pass_b(1, 2)
    pass_a(1, 3)
    swap1.wait()

    def gelu_parts(u, rs):
        column = jnp.concatenate([bias_column(u, 4 + s) for s in range(4)], axis=0)
        pre = contract(w_up[tile(u, 512), :], nm[rs, :], 1, 1) + column
        sq = pre * pre
        th = jnp.tanh(pre * (0.7978845608028654 + (0.7978845608028654 * 0.044715) * sq))
        hp = 0.5 + 0.5 * th
        slope = hp + pre * (hp * (1.0 - th)) * (
            0.7978845608028654 + (3 * 0.7978845608028654 * 0.044715) * sq
        )
        return pre * hp, slope

    def hidden_unit(n, u):
        us = tile(u, 512)

        def hidden(t):
            rs = tile(t, 256)
            value, slope = gelu_parts(u, rs)
            act[us, rs] = value.astype(bf16)
            gp[us, rs] = (contract(w_dn[us, :], gfin[rs, :], 1, 1) * slope).astype(bf16)

        loop(4, hidden)

    def weight_part(n, u, i):
        us = tile(u, 512)
        if n > 0:
            pltpu.make_async_copy(stage.at[i], dwm_any.at[u, i], stage_sem.at[i]).wait()
        left, right = ((gp, nm), (act, gfin))[i]
        stage[i] = contract(left[us, :], right[...], 1, 0).astype(bf16)
        pltpu.make_async_copy(stage.at[i], dwm_any.at[u, i], stage_sem.at[i]).start()
        if i == 0:
            bias_rows[u, :, 384:896] = contract(jnp.ones((8, BUCKET), bf16), gp[us, :], 1, 1)

    def weights_unit(n, u):
        weight_part(n, u, 0)
        weight_part(n, u, 1)

    def partial_sums(n, u):
        us = tile(u, 512)
        for left, right, kept in ((act, w_dn, stream), (gp, w_up, acc)):
            for rows in (far, own):
                total = contract(left[us, rows], right[us, :], 0, 0)
                if n > 0:
                    total = total + kept[rows, :]
                kept[rows, :] = total

    bias_rows[...] = jnp.zeros_like(bias_rows)
    stream_saved.wait()
    hidden_unit(0, z)
    pass_c(1, 2)
    pass_b(2, 2)
    pass_a(2, 3)
    weights_unit(0, z)
    pass_c(2, 2)
    pass_b(1, 3)
    partial_sums(0, z)
    hidden_unit(1, peer(z, 1))
    pass_c(1, 3)
    pass_b(2, 3)
    weights_unit(1, peer(z, 1))
    partial_sums(1, peer(z, 1))
    hidden_unit(2, peer(z, 2))
    weights_unit(2, peer(z, 2))
    partial_sums(2, peer(z, 2))
    last_unit = peer(z, 3)
    us = tile(last_unit, 512)
    save(acc, acc_any)

    def last_values(t):
        rs = tile(t, 256)
        value, slope = gelu_parts(last_unit, rs)
        act[us, rs] = value.astype(bf16)
        slopes[:, rs] = slope

    def last_slopes(t):
        rs = tile(t, 256)
        gp[us, rs] = (contract(w_dn[us, :], gfin[rs, :], 1, 1) * slopes[:, rs]).astype(bf16)

    loop(4, last_values)
    save(w_up.at[us, :], wup_any)
    weight_part(3, last_unit, 1)
    pass_c(2, 3)
    send[1] = (stream[far, :] + contract(act[us, far], w_dn[us, :], 0, 0)).astype(bf16)
    swap2 = swap(send.at[1], recv.at[1], 2)
    loop(4, last_slopes)
    save(gp.at[us, :], gp_any)
    slopes[...] = stream[own, :] + contract(act[us, own], w_dn[us, :], 0, 0)
    swap2.wait()

    def finish(i):
        rs = tile(i, 128)
        ro = pl.ds(pl.multiple_of(core * half + i * 128, 128), 128)
        live = jnp.where(seg_col[ro, :][:, 0:1] < 1000.0, 1.0, 0.0)
        v = mid[rs, :] + (slopes[rs, :] + recv[1, rs, :].astype(f32)) + down_bias[...]
        lo[rs, :] = (live * v).astype(bf16)

    loop(4, finish)
    save(lo, out_any)
    weight_part(3, last_unit, 0)
    for i in range(2):
        pltpu.make_async_copy(stage.at[i], dwm_any.at[0, i], stage_sem.at[i]).wait()
    for c in saves:
        if c is not stream_saved:
            c.wait()
    for k in range(3):
        for m in (1, 2, 3):
            for way in range(4 if diagonal(k, m) else 5):
                hop(k, m, way).wait_send()


def column_devices(me, z):
    both = (me, toggled(me, 1))
    return [(both[1], z)] + [(d, peer(z, m)) for m in (1, 2, 3) for d in both]


def backward_kernel(
    gather,
    meta, seg_col, trig, attn_gain, mlp_gain, bias_rows, lse,
    wqo_any, mid_any, gfin_any, acc_any, gp_any, wup_any, stream_any, normed_any, q_any, k_any, v_any, merged_any, lo_any, dwm_any,
    out_any, dwa_any, gathered_any, parts, sums,
    wqo, mid, gfin, gmid, gm, stream, normed, qt, kt, vt, merged,
    gmerged, gproj, acck, accv, send, recv, gin, stage, gin_low, small, mine,
    keep_m, got_m, last_m, keep_a, got_a, last_a, own_m, line_got_m, own_a, line_got_a, final,
    small_pair, small_line, small_x, small_y,
    load_sem, stage_sem, send_sem, recv_sem, near_sem,
    lo_send, lo_recv, gin_send, gin_recv, pm_load, pm_send, pm_recv, pa_load, pa_send, pa_recv,
    lm_send, lm_recv, la_send, la_recv, gm_send, gm_recv, ga_send, ga_recv, small_send, small_recv,
):
    me, z = lax.axis_index("dp"), lax.axis_index("mp")
    core, other = lax.rem(me, 2), toggled(me, 1)
    half = BUCKET // 2
    units = wqo.shape[0] // 512
    n_qkv = units * 384
    w_qkv, w_out = pl.ds(0, n_qkv), pl.ds(n_qkv, units * 128)
    loads = {}
    for name, src, dst in (
        ("far", acc_any.at[tile(1 - core, half), :], gmid),
        ("gp", gp_any, gproj.at[pl.ds(0, 512), :]),
        ("up", wup_any, gproj.at[pl.ds(512, 512), :]),
        ("own", acc_any.at[tile(core, half), :], gin),
        ("mid", mid_any, mid),
        ("gfin", gfin_any, gfin),
        ("out", wqo_any.at[w_out, :], wqo.at[w_out, :]),
        ("q", q_any, qt),
        ("k", k_any, kt),
        ("v", v_any, vt),
        ("merged", merged_any, merged),
        ("qkv", wqo_any.at[w_qkv, :], wqo.at[w_qkv, :]),
        ("stream", stream_any, stream),
        ("normed", normed_any, normed),
    ):
        loads[name] = pltpu.make_async_copy(src, dst, load_sem.at[len(loads)])
        loads[name].start()
    wqkv, wout = wqo.at[w_qkv, :], wqo.at[w_out, :]
    cosine, sine = trig.at[pl.ds(0, 32), :], trig.at[pl.ds(32, 32), :]
    greet([(toggled(me, 2), z), (toggled(me, 4), z)] + column_devices(me, z))
    plane_m = PlaneSum(dwm_any, keep_m, got_m, last_m, pm_load, pm_send, pm_recv)
    spread_lo = Spread(lo_any, out_any, near_sem.at[0], lo_send, lo_recv)
    plane_m.begin(0)
    spread_lo.begin()
    plane_m.begin(3)

    def put_m(u, order, total):
        for i in range(2):
            own_m[u, i * 128 + order * 64 : i * 128 + (order + 1) * 64, :] = total[i]

    def put_a(u, order, total):
        own_a[u, order * 64 : (order + 1) * 64, :] = total[0]

    own = tile(core, half)
    far = tile(1 - core, half)
    gp_last, up_last = gproj.at[pl.ds(0, 512), :], gproj.at[pl.ds(512, 512), :]

    def swap(src, dst, i):
        c = remote(src, dst, send_sem.at[i], recv_sem.at[i], other, z)
        c.start()
        return c

    for name in ("far", "gp", "up"):
        loads[name].wait()
    send[...] = (gmid[...] + contract(gp_last[:, far], up_last[...], 0, 0)).astype(bf16)
    swap_in = swap(send, recv, 0)
    loads["own"].wait()
    gin[...] += contract(gp_last[:, own], up_last[...], 0, 0)
    loads["mid"].wait()
    loads["gfin"].wait()
    small[...] = jnp.zeros_like(small)
    swap_in.wait()

    def back_mlp(i):
        rs = tile(i, 128)
        ro = pl.ds(pl.multiple_of(core * half + i * 128, 128), 128)
        err = gin[rs, :] + recv[rs, :].astype(f32)
        grad, gain_grad = norm_back(mid[rs, :], mlp_gain[...], err)
        gf = gfin[rs, :].astype(f32)
        grad = grad + gf
        gmid[rs, :] = grad
        gm[ro, :] = grad.astype(bf16)
        small[0:1, :] += gain_grad
        small[1:2, :] += jnp.sum(grad, axis=0, keepdims=True)
        small[2:3, :] += jnp.sum(gf, axis=0, keepdims=True)

    loop(4, back_mlp)
    swap_gm = swap(gm.at[own, :], gm.at[own, :], 1)
    loads["out"].wait()
    swap_gm.wait()
    for t in range(2):
        cs = pl.ds(t * 512, 512)
        gmerged[:, cs] = contract(wout[...], gm[cs, :], 1, 1).astype(bf16)
    for name in ("q", "k", "v", "merged"):
        loads[name].wait()

    def head(h):
        hs = tile(h, HEAD)
        u = h // 2
        j = lax.rem(h, 2)
        at = u * 384 + j * HEAD
        keys_t = (kt[hs, :].astype(f32) * 0.125).astype(bf16)
        keys = keys_t.astype(f32).T.astype(bf16)
        values = vt[hs, :].astype(f32).T.astype(bf16)
        for t in range(2):
            cs = pl.ds(t * 512, 512)
            q, go = qt[hs, cs], gmerged[hs, cs]
            dl = jnp.sum(go.astype(f32) * merged[hs, cs].astype(f32), axis=0, keepdims=True)
            s = jnp.dot(keys, q, preferred_element_type=f32)
            same = jnp.tile(seg_col[...], (1, 4)) == meta[8:9, cs]
            p = jnp.exp(jnp.where(same, s, -1e30) - lse[h, :, cs])
            dp = jnp.dot(values, go, preferred_element_type=f32)
            ds = (p * (dp - dl)).astype(bf16)
            dq = jnp.dot(keys_t, ds, preferred_element_type=f32)
            gproj[pl.ds(pl.multiple_of(at, HEAD), HEAD), cs] = rotate_rows(
                dq, cosine[:, cs], -sine[:, cs]
            ).astype(bf16)
            dv = contract(go, p.astype(bf16), 1, 1)
            dk = contract(q, ds, 1, 1)
            if t == 0:
                accv[...] = dv
                acck[...] = dk
            else:
                dk = (acck[...] + dk) * 0.125
                gproj[pl.ds(pl.multiple_of(at + 128, HEAD), HEAD), :] = rotate_rows(
                    dk, cosine[...], -sine[...]
                ).astype(bf16)
                gproj[pl.ds(pl.multiple_of(at + 256, HEAD), HEAD), :] = (accv[...] + dv).astype(bf16)

    def heads(i):
        head(2 * i)
        head(2 * i + 1)

        @pl.when(i == 1)
        def _():
            plane_m.middle(0)
            plane_m.begin(1)
            spread_lo.pass_first()

        @pl.when(i == 2)
        def _():
            plane_m.middle(3)
            plane_m.begin(2)

    loop(units, heads)
    line_m = LineSum(own_m, line_got_m, lm_send, lm_recv)
    line_a = LineSum(own_a, line_got_a, la_send, la_recv)
    plane_m.end(0, put_m)
    line_m.step(0, 0)
    loads["qkv"].wait()
    send[...] = contract(gproj[:, far], wqkv[...], 0, 0).astype(bf16)
    swap_out = swap(send, recv, 2)
    gin[...] = contract(gproj[:, own], wqkv[...], 0, 0)
    loads["stream"].wait()
    swap_out.wait()

    def back(i):
        rs = tile(i, 128)
        ro = pl.ds(pl.multiple_of(core * half + i * 128, 128), 128)
        err = gin[rs, :] + recv[rs, :].astype(f32)
        grad, gain_grad = norm_back(stream[rs, :], attn_gain[...], err)
        grad = grad + gmid[rs, :]
        high = grad.astype(bf16)
        gin_low[rs, :] = high
        small[3:4, :] += gain_grad
        member = one_hot(seg_col[ro, :], 1)
        low = (grad - high.astype(f32)).astype(bf16)
        small[8:16, :] += (contract(member, high, 0, 0) + contract(member, low, 0, 0))[0:8]

    loop(4, back)
    spread_gin = Spread(gin_low, gathered_any, near_sem.at[1], gin_send, gin_recv)
    spread_gin.begin()
    plane_m.end(3, put_m)
    line_m.step(0, 3)
    line_m.step(1, 0)
    t_rows = small[8:16, :]
    mine[0:8, :] = jnp.concatenate(
        [
            small[0:4, :],
            jnp.sum(t_rows, axis=0, keepdims=True),
            jnp.zeros((3, t_rows.shape[1]), f32),
        ]
    )
    mine[8:16, :] = jnp.zeros((8, t_rows.shape[1]), f32)
    mine[16:24, :] = t_rows
    loads["normed"].wait()
    plane_a = PlaneSum(dwa_any, keep_a, got_a, last_a, pa_load, pa_send, pa_recv)
    order = (0, 3, 1, 2)

    def stored(i):
        return pltpu.make_async_copy(stage.at[i % 2], dwa_any.at[order[i]], stage_sem.at[i % 2])

    def weights(i):
        u = order[i]
        us = pl.ds(u * 384, 384)
        if i > 1:
            stored(i - 2).wait()
            plane_a.begin(order[i - 2])
        of_qkv = contract(gproj[us, :], normed[...], 1, 0).astype(bf16)
        of_out = contract(merged[pl.ds(u * 128, 128), :], gm[...], 1, 0).astype(bf16)
        for k in range(4):
            quarter = of_qkv[k * 128 : (k + 1) * 128] if k < 3 else of_out
            for j in range(2):
                stage[i % 2, 0, k // 2, k % 2, j] = quarter[j * 64 : (j + 1) * 64]
        stored(i).start()
        row = lax.broadcasted_iota(jnp.int32, (8, 1), 0) == core * units + u
        mine[8:16, 0:384] += jnp.where(
            row, contract(jnp.ones((8, BUCKET), bf16), gproj[us, :], 1, 1), 0.0
        )
        mine[8:16, 384:896] += jnp.where(row, bias_rows[u, :, 384:896], 0.0)

    little = SmallSum(mine, small_pair, small_line, small_x, small_y, sums, small_send, small_recv)

    def put_final_m(total):
        final[128:384, :] = total

    def put_final_a(total):
        final[0:128, :] = total

    if gather:
        gather_m = PlaneGather(final, parts, (128, 256), near_sem.at[2, 0], gm_send, gm_recv)
        gather_a = PlaneGather(final, parts, (0, 128), near_sem.at[3, 0], ga_send, ga_recv)
    weights(0)
    weights(1)
    plane_m.middle(1)
    spread_lo.pass_second()
    weights(2)
    weights(3)
    little.begin()
    line_m.step(1, 3)
    line_m.step(2, 0)
    plane_m.middle(2)
    for i in (2, 3):
        stored(i).wait()
        plane_a.begin(order[i])
    plane_m.end(1, put_m)
    line_m.step(0, 1)
    line_m.step(2, 3)
    little.step_line(meta[16:24, 0 : sums.shape[0] - 16])
    plane_m.end(2, put_m)
    line_m.step(0, 2)
    line_m.step(1, 1)
    spread_gin.pass_first()
    line_m.step(1, 2)
    plane_a.middle(0)
    plane_a.middle(3)
    little.step_across()
    plane_a.middle(1)
    plane_a.middle(2)
    line_m.finish(put_final_m)
    little.step_along()
    if gather:
        gather_m.begin()
    plane_a.end(0, put_a)
    line_a.step(0, 0)
    plane_a.end(3, put_a)
    line_a.step(0, 3)
    line_a.step(1, 0)
    plane_a.end(1, put_a)
    line_a.step(0, 1)
    line_a.step(1, 3)
    plane_a.end(2, put_a)
    line_a.step(0, 2)
    line_a.step(1, 1)
    line_a.step(1, 2)
    line_a.step(2, 0)
    line_a.step(2, 3)
    spread_gin.pass_second()
    if gather:
        gather_m.pass_on()
    line_a.finish(put_final_a)
    if gather:
        gather_a.begin()
        little.step_out()
        gather_a.pass_on()
        gather_m.finish()
        gather_a.finish()
    else:
        little.step_out()
        out = pltpu.make_async_copy(final, parts, near_sem.at[2, 0])
        out.start()
        out.wait()
    little.finish()
    spread_lo.finish()
    spread_gin.finish()
    for u in range(4):
        plane_m.drain(u)
        plane_a.drain(u)


def deliver_kernel(parts, gin, lo, sums, grad_in, lo_out, time_out, qkv_out, out_out, up_out, down_out):
    s = lax.rem(pl.program_id(0), 4)
    grad_in[...] = gin[...].astype(f32)
    lo_out[...] = lo[...]
    time_out[...] = sums[...]
    down_out[...] = parts[0, 0, 256:384, :].astype(f32)
    up_out[...] = parts[0, 0, 128:256, :].T.astype(f32)

    @pl.when(s < 3)
    def _():
        qkv_out[0] = parts[0, 0, 0:128, :].T.astype(f32)

    @pl.when(s == 3)
    def _():
        out_out[...] = parts[0, 0, 0:128, :].astype(f32)


def shape(s, t):
    return jax.ShapeDtypeStruct(s, t)


def run_forward(args, here, units, width):
    rows = BUCKET
    half = rows // 2
    feat = units * 128
    hid = units * 512
    anyspec = pl.BlockSpec(memory_space=pl.ANY)
    vm = pl.BlockSpec(memory_space=VMEM)
    outs = (
        shape((half, width), bf16),
        shape((half, width), f32),
        shape((half, width), bf16),
        shape((rows, width), f32),
        shape((512, width), bf16),
        shape((512, width), bf16),
        shape((half, width), f32),
        shape((rows, width), bf16),
        shape((feat, rows), bf16),
        shape((feat, rows), bf16),
        shape((feat, rows), bf16),
        shape((feat, rows), bf16),
        shape((2 * units, 1, rows), f32),
        shape((units, 2, 512, width), bf16),
        shape((hid, width), bf16),
        shape((units, 8, width), f32),
        shape((rows, 128), f32),
        shape((64, rows), f32),
        shape((24, width), f32),
    )
    dma = pltpu.SemaphoreType.DMA
    return pl.pallas_call(
        forward_kernel,
        out_shape=outs,
        in_specs=[anyspec] * 2 + [pl.BlockSpec(memory_space=pltpu.SMEM)] + [vm] * 9 + [anyspec] * 4,
        out_specs=[anyspec] * 15 + [vm] * 4,
        scratch_shapes=[
            VMEM((3 * hid, width), bf16),
            VMEM((rows, width), bf16),
            VMEM((rows, width), bf16),
            VMEM((8, 128), f32),
            VMEM((units, 8, 128), f32),
            VMEM((rows, width), f32),
            VMEM((rows, width), bf16),
            VMEM((feat, rows), bf16),
            VMEM((feat, rows), bf16),
            VMEM((feat, rows), bf16),
            VMEM((feat, rows), bf16),
            VMEM((2 * units, 1, rows), f32),
            VMEM((2, half, width), bf16),
            VMEM((2, half, width), bf16),
            VMEM((half, width), f32),
            VMEM((rows, width), bf16),
            VMEM((hid, rows), bf16),
            VMEM((hid, rows), bf16),
            VMEM((2, 512, width), bf16),
            VMEM((half, width), bf16),
            VMEM((half, width), f32),
            VMEM((3, width, 128), bf16),
            VMEM((rows, width), f32),
            dma((7,)),
            dma((3,)),
            dma((3,)),
            dma((3,)),
            dma((3,)),
            dma((9, 5)),
            dma((9, 5)),
            dma((16,)),
            dma((2,)),
            dma((3,)),
            dma((3,)),
        ],
        compiler_params=pltpu.CompilerParams(
            collective_id=0, has_side_effects=True, vmem_limit_bytes=63 * MIB
        ),
        name="forward",
    )(*args)


def run_backward(args, gather, here, units, rows, width, n_time):
    half = rows // 2
    feat = units * 128
    anyspec = pl.BlockSpec(memory_space=pl.ANY)
    vm = pl.BlockSpec(memory_space=VMEM)
    dma = pltpu.SemaphoreType.DMA
    return pl.pallas_call(
        functools.partial(backward_kernel, gather),
        out_shape=(
            shape((here * rows, width), bf16),
            shape((units, 1, 2, 2, 2, 64, width), bf16),
            shape((here * rows, width), bf16),
            shape((2, 4, 384, width) if gather else (384, width), bf16),
            shape((n_time + 16, width), f32),
        ),
        in_specs=[vm] * 7 + [anyspec] * (len(args) - 7),
        out_specs=[anyspec] * 4 + [vm],
        scratch_shapes=[
            VMEM((4 * feat, width), bf16),
            VMEM((half, width), f32),
            VMEM((half, width), bf16),
            VMEM((half, width), f32),
            VMEM((rows, width), bf16),
            VMEM((half, width), f32),
            VMEM((rows, width), bf16),
            VMEM((feat, rows), bf16),
            VMEM((feat, rows), bf16),
            VMEM((feat, rows), bf16),
            VMEM((feat, rows), bf16),
            VMEM((feat, rows), bf16),
            VMEM((3 * feat, rows), bf16),
            VMEM((HEAD, rows), f32),
            VMEM((HEAD, rows), f32),
            VMEM((half, width), bf16),
            VMEM((half, width), bf16),
            VMEM((half, width), f32),
            VMEM((2, 1, 2, 2, 2, 64, width), bf16),
            VMEM((half, width), bf16),
            VMEM((16, width), f32),
            VMEM((24, width), f32),
            VMEM((2, units, 2, 2, 64, width), bf16),
            VMEM((2, units, 2, 2, 64, width), bf16),
            VMEM((2, units, 2, 64, width), bf16),
            VMEM((2, units, 1, 2, 64, width), bf16),
            VMEM((2, units, 1, 2, 64, width), bf16),
            VMEM((2, units, 1, 64, width), bf16),
            VMEM((units, 256, width), bf16),
            VMEM((2, 3, 256, width), bf16),
            VMEM((units, 128, width), bf16),
            VMEM((2, 3, 128, width), bf16),
            VMEM((384, width), bf16),
            VMEM((24, width // 2), f32),
            VMEM((4, 24, width // 2 + n_time), f32),
            VMEM((2, 48, width // 2 + n_time), f32),
            VMEM((2, 80, width // 2 + n_time), f32),
            dma((14,)),
            dma((2,)),
            dma((3,)),
            dma((3,)),
            dma((4, 1)),
            dma((7,)),
            dma((4,)),
            dma((7,)),
            dma((4,)),
            dma((2, units)),
            dma((2, 2, units)),
            dma((2, 2, units)),
            dma((2, units)),
            dma((2, 2, units)),
            dma((2, 2, units)),
            dma((2, 3)),
            dma((2, 3)),
            dma((2, 3)),
            dma((2, 3)),
            dma((8,)),
            dma((8,)),
            dma((8,)),
            dma((8,)),
            dma((7,)),
            dma((7,)),
        ],
        compiler_params=pltpu.CompilerParams(
            collective_id=1, has_side_effects=True, vmem_limit_bytes=63 * MIB
        ),
        name="backward",
    )(*args)


def run_deliver(parts, gin, lo, sums, n_time):
    rows, width = gin.shape
    steps = 8
    part = parts.shape[2] // 3
    hid = steps * part
    at = lambda i: (i, 0)
    return pl.pallas_call(
        deliver_kernel,
        grid=(steps,),
        out_shape=(
            shape((rows, width), f32),
            shape((rows, width), bf16),
            shape((n_time, width), f32),
            shape((3, width, 2 * part), f32),
            shape((2 * part, width), f32),
            shape((width, hid), f32),
            shape((hid, width), f32),
        ),
        in_specs=[
            pl.BlockSpec((1, 1, 3 * part, width), lambda i: (i // 4, i % 4, 0, 0)),
            pl.BlockSpec((rows // steps, width), at),
            pl.BlockSpec((rows // steps, width), at),
            pl.BlockSpec((n_time // steps, width), at),
        ],
        out_specs=[
            pl.BlockSpec((rows // steps, width), at),
            pl.BlockSpec((rows // steps, width), at),
            pl.BlockSpec((n_time // steps, width), at),
            pl.BlockSpec((1, width, part), lambda i: (jnp.minimum(i % 4, 2), 0, i // 4)),
            pl.BlockSpec((part, width), lambda i: (i // 4, 0)),
            pl.BlockSpec((width, part), lambda i: (0, i)),
            pl.BlockSpec((part, width), at),
        ],
        compiler_params=pltpu.CompilerParams(vmem_limit_bytes=48 * MIB),
        name="deliver",
    )(parts, gin, lo, sums)


def local(
    ndp, nmp, activations, noise_embed, lengths, time_weight, time_bias, attn_gain, qkv_weight, qkv_bias,
    out_weight, out_bias, mlp_gain, up_weight, up_bias, down_weight, down_bias, cotangent,
):
    width = activations.shape[1]
    here = activations.shape[0] // BUCKET
    assert 2 * here == nmp and qkv_weight.shape[2] == 256 and up_weight.shape[1] == 1024
    assert ndp % 8 == 0 and noise_embed.shape[0] == here * SLOTS
    n_time = time_weight.shape[0]
    def row(v):
        return v.reshape(1, width)

    (
        lo, mid, gfin, acc, gp, wup, stream, normed, qt, kt, vt, merged, lse, dwm, wqo, bias_rows, seg_col, trig, meta,
    ) = run_forward(
        (
            activations, cotangent, lengths, noise_embed, time_weight, row(time_bias), row(attn_gain),
            row(out_bias), row(mlp_gain), row(down_bias), qkv_bias, up_bias.reshape(8, 128),
            qkv_weight.transpose(1, 0, 2), out_weight, up_weight, down_weight,
        ),
        here, nmp, width,
    )
    gather = ndp == 8
    lo_all, _, gathered, parts, sums = run_backward(
        (
            meta, seg_col, trig, row(attn_gain), row(mlp_gain), bias_rows, lse, wqo, mid, gfin, acc, gp, wup, stream,
            normed, qt, kt, vt,
            merged, lo, dwm.reshape(nmp, 2, 2, 2, 2, 64, width),
        ),
        gather, here, nmp, BUCKET, width, n_time,
    )
    if not gather:
        groups = [[i + 8 * k for k in range(ndp // 8)] for i in range(8)]
        parts = lax.psum(parts, "dp", axis_index_groups=groups)
        sums = lax.psum(sums, "dp", axis_index_groups=groups)
        groups = [[8 * k + i for i in range(8)] for k in range(ndp // 8)]
        parts = lax.all_gather(parts, "dp", axis_index_groups=groups)
        parts = parts.reshape(4, 2, 384, width).transpose(1, 0, 2, 3)
    grad_input, layer_output, grad_time_weight, grad_qkv, grad_out, grad_up, grad_down = run_deliver(
        parts, gathered, lo_all, sums, n_time
    )
    grad_qkv = grad_qkv.transpose(1, 0, 2)
    grad_mlp_gain, grad_out_bias, grad_down_bias, grad_attn_gain, grad_time_bias = (
        sums[n_time + i] for i in range(5)
    )
    bias_sums = sums[n_time + 8 :].reshape(2, nmp, width)
    bias_sums = lax.dynamic_index_in_dim(bias_sums, lax.axis_index("mp"), 1, keepdims=False)
    grad_qkv_bias = bias_sums[:, :384].reshape(2, 3, 128).transpose(1, 0, 2).reshape(3, 256)
    grad_up_bias = bias_sums[:, 384:896].reshape(-1)
    return (
        layer_output,
        grad_input,
        grad_time_weight,
        grad_time_bias,
        grad_attn_gain,
        grad_qkv,
        grad_qkv_bias,
        grad_out,
        grad_out_bias,
        grad_mlp_gain,
        grad_up,
        grad_up_bias,
        grad_down,
        grad_down_bias,
    )


def solution(mesh):
    in_specs = (
        P("dp", None),
        P("dp", None),
        P("dp"),
        P(),
        P(),
        P(),
        P(None, None, "mp"),
        P(None, "mp"),
        P("mp", None),
        P(),
        P(),
        P(None, "mp"),
        P("mp"),
        P("mp", None),
        P(),
        P("dp", None),
    )
    out_specs = (
        P("dp", None),
        P("dp", None),
        P(),
        P(),
        P(),
        P(None, None, "mp"),
        P(None, "mp"),
        P("mp", None),
        P(),
        P(),
        P(None, "mp"),
        P("mp"),
        P("mp", None),
        P(),
    )
    body = functools.partial(local, mesh.shape["dp"], mesh.shape["mp"])
    return jax.shard_map(body, mesh=mesh, in_specs=in_specs, out_specs=out_specs, check_vma=False)
```

```python
import functools
import math

import jax
import jax.numpy as jnp
from jax import lax
from jax.experimental import pallas as pl
from jax.experimental.pallas import tpu as pltpu
from jax.sharding import PartitionSpec as P

HEAD = 64
BUCKET = 1024
SLOTS = 8
MIB = 1 << 20
MESH = pl.DeviceIdType.MESH
VMEM = pltpu.VMEM
bf16 = jnp.bfloat16
f32 = jnp.float32


def contract(a, b, ca, cb):
    return lax.dot_general(a, b, (((ca,), (cb,)), ((), ())), preferred_element_type=f32)


def tile(i, n):
    return pl.ds(pl.multiple_of(i * n, n), n)


def loop(n, body):
    def step(i, carry):
        body(i)
        return carry

    lax.fori_loop(0, n, step, 0)


def row_stats(v):
    centered = v - jnp.mean(v, axis=-1, keepdims=True)
    return centered, lax.rsqrt(jnp.mean(centered * centered, axis=-1, keepdims=True) + 1e-05)


def norm_back(v, gain, err):
    centered, scale = row_stats(v)
    xhat = centered * scale
    u = err * gain
    grad = (
        u - jnp.mean(u, axis=-1, keepdims=True) - xhat * jnp.mean(u * xhat, axis=-1, keepdims=True)
    ) * scale
    return grad, jnp.sum(err * xhat, axis=0, keepdims=True)


def toggled(v, bit):
    return v + bit - 2 * bit * lax.rem(v // bit, 2)


def peer(z, m):
    low = lax.rem(lax.rem(z, 2) + m % 2, 2)
    return low + 2 * lax.rem(z // 2 + m // 2, 2)


def greet(targets):
    barrier = pltpu.get_barrier_semaphore()
    for d, z in targets:
        pl.semaphore_signal(barrier, inc=1, device_id={"dp": d, "mp": z}, device_id_type=MESH)
    pl.semaphore_wait(barrier, len(targets))


def remote(src, dst, ss, rs, d, z):
    return pltpu.make_async_remote_copy(
        src_ref=src,
        dst_ref=dst,
        send_sem=ss,
        recv_sem=rs,
        device_id={"dp": d, "mp": z},
        device_id_type=MESH,
    )


class Spread:
    def __init__(self, src, out, near_sem, send_sem, recv_sem):
        me, z = lax.axis_index("dp"), lax.axis_index("mp")
        self.core = core = lax.rem(me, 2)
        self.kind = kind = z // 2
        self.place = z + core * (3 - 2 * z)
        self.start_place = z + kind * (3 - 2 * z)
        self.out, self.send, self.recv = out, send_sem, recv_sem
        self.me, self.z, self.ahead = me, z, z + 1 - 2 * core
        keeper = me - core + kind
        dst = self.piece(self.start_place, core, kind)
        rs = recv_sem.at[2 * self.start_place + core]
        self.near = pltpu.make_async_copy(src, dst, near_sem.at[0])
        self.first = [
            remote(src, dst, send_sem.at[0], rs, keeper, z + 1 - 2 * kind),
            remote(src, dst, send_sem.at[1], rs, keeper, z - 1 + 2 * kind),
            remote(src, dst, send_sem.at[2], rs, toggled(me, 1), z),
        ]

    def piece(self, m, h, kind):
        rows = self.out.shape[0] // 4
        at = 2 * (m + kind * (1 - 2 * m)) + h
        return self.out.at[pl.ds(pl.multiple_of(at * rows, rows), rows), :]

    def hop(self, m, h, i):
        ref = self.piece(m, h, self.core)
        return remote(ref, ref, self.send.at[i], self.recv.at[2 * m + h], self.me, self.ahead)

    def begin(self):
        self.first[0].start()

        @pl.when(self.start_place == 1)
        def _():
            self.first[1].start()

        @pl.when(self.core == self.kind)
        def _():
            self.near.start()

        @pl.when(self.core != self.kind)
        def _():
            self.first[2].start()

    def forward(self, place, m, i):
        @pl.when(self.place == place)
        def _():
            for h in range(2):
                self.hop(m, h, i + h).wait_recv()
                self.hop(m, h, i + h).start()

    def pass_first(self):
        self.forward(1, 0, 3)
        self.forward(2, 1, 3)

    def pass_second(self):
        self.forward(2, 0, 5)

    def finish(self):
        @pl.when(self.core == self.kind)
        def _():
            self.near.wait()
            self.hop(self.place, 1 - self.core, 3).wait_recv()

        @pl.when(self.core != self.kind)
        def _():
            self.first[2].wait_send()

        @pl.when(self.place == 0)
        def _():
            for h in range(2):
                self.hop(1, h, 3).wait_recv()

        @pl.when(self.place == 3)
        def _():
            for m in range(2):
                for h in range(2):
                    self.hop(m, h, 3).wait_recv()

        self.first[0].wait_send()

        @pl.when(self.start_place == 1)
        def _():
            self.first[1].wait_send()

        for place, m, i in ((1, 0, 3), (2, 1, 3), (2, 0, 5)):

            @pl.when(self.place == place)
            def _(m=m, i=i):
                for h in range(2):
                    self.hop(m, h, i + h).wait_send()


class PlaneSum:
    def __init__(self, src, keep, got, last, load_sem, send_sem, recv_sem):
        me, z = lax.axis_index("dp"), lax.axis_index("mp")
        self.x, self.y = lax.rem(me // 2, 2), lax.rem(me // 4, 2)
        self.z, self.across, self.along = z, toggled(me, 2), toggled(me, 4)
        self.src, self.keep, self.got, self.last = src, keep, got, last
        self.load_sem, self.send_sem, self.recv_sem = load_sem, send_sem, recv_sem

    def part(self, u, order, mine):
        x = self.x if mine else 1 - self.x
        y = self.y if mine else 1 - self.y
        return self.src.at[u, :, :, x, 0] if order == 0 else self.src.at[u, :, y, :, 1]

    def load(self, u, order):
        return pltpu.make_async_copy(
            self.part(u, order, True), self.keep.at[order, u], self.load_sem.at[order, u]
        )

    def hop(self, u, order, stage):
        if stage == 0:
            src, dst = self.part(u, order, False), self.got.at[order, u]
        else:
            there = 1 - (self.y if order == 0 else self.x)
            src, dst = self.keep.at[order, u, :, there], self.last.at[order, u]
        to = self.across if order == stage else self.along
        return remote(
            src, dst, self.send_sem.at[order, stage, u], self.recv_sem.at[order, stage, u], to, self.z
        )

    def begin(self, u):
        for order in range(2):
            self.load(u, order).start()
            self.hop(u, order, 0).start()

    def middle(self, u):
        for order in range(2):
            self.load(u, order).wait()
            self.hop(u, order, 0).wait_recv()
            total = self.keep[order, u].astype(f32) + self.got[order, u].astype(f32)
            self.keep[order, u] = total.astype(bf16)
            self.hop(u, order, 1).start()

    def end(self, u, put):
        for order in range(2):
            self.hop(u, order, 1).wait_recv()
            here = self.y if order == 0 else self.x
            total = self.keep[order, u, :, here].astype(f32) + self.last[order, u].astype(f32)
            put(u, order, total.astype(bf16))

    def drain(self, u):
        for order in range(2):
            for stage in range(2):
                self.hop(u, order, stage).wait_send()


class LineSum:
    def __init__(self, own, got, send_sem, recv_sem):
        self.me, self.z = lax.axis_index("dp"), lax.axis_index("mp")
        self.own, self.got, self.send_sem, self.recv_sem = own, got, send_sem, recv_sem

    def hop(self, way, t):
        entry = t if way == 0 else 3 - t
        return remote(
            self.own.at[entry], self.got.at[way, t - 1], self.send_sem.at[way, t - 1],
            self.recv_sem.at[way, t - 1], self.me, self.z + 1 - 2 * way,
        )

    def step(self, s, entry):
        for way in range(2):
            t = entry if way == 0 else 3 - entry
            if s >= t:
                continue

            @pl.when(self.z == (s if way == 0 else 3 - s))
            def _(way=way, t=t):
                if s > 0:
                    self.hop(way, t).wait_recv()
                    total = self.own[entry].astype(f32) + self.got[way, t - 1].astype(f32)
                    self.own[entry] = total.astype(bf16)
                self.hop(way, t).start()

    def finish(self, put):
        for way in range(2):
            for t in range(1, 4):

                @pl.when(self.z == (t if way == 0 else 3 - t))
                def _(way=way, t=t):
                    self.hop(way, t).wait_recv()
                    entry = t if way == 0 else 3 - t
                    total = self.own[entry].astype(f32) + self.got[way, t - 1].astype(f32)
                    self.own[entry] = total.astype(bf16)

        put(self.own[self.z])
        for way in range(2):
            for s in range(3):

                @pl.when(self.z == (s if way == 0 else 3 - s))
                def _(way=way, s=s):
                    for t in range(3, s, -1):
                        self.hop(way, t).wait_send()


class PlaneGather:
    def __init__(self, final, parts, rows, own_sem, send_sem, recv_sem):
        me, self.z = lax.axis_index("dp"), lax.axis_index("mp")
        self.core, self.col = lax.rem(me, 2), lax.rem(me // 2, 4)
        self.other, self.across, self.along = toggled(me, 1), toggled(me, 2), toggled(me, 4)
        self.parts, self.rows = parts, rows
        self.send_sem, self.recv_sem = send_sem, recv_sem
        self.cols = (
            self.col, toggled(self.col, 1), toggled(self.col, 2), toggled(toggled(self.col, 1), 2),
        )
        src = final.at[pl.ds(rows[0], rows[1]), :]
        self.near = pltpu.make_async_copy(src, self.slot(self.core, self.col), own_sem)
        self.hops = [
            self.hop(self.slot(self.core, self.col), 4, self.across, src),
            self.hop(self.slot(self.core, self.col), 5, self.along, src),
            self.hop(self.slot(self.core, self.col), 0, self.other, src),
        ]

    def slot(self, c, s, h=None):
        at, n = self.rows
        if h is not None:
            at, n = at + h * (n // 2), n // 2
        return self.parts.at[c, s, pl.ds(at, n), :]

    def hop(self, dst, i, to, src=None):
        src = dst if src is None else src
        return remote(src, dst, self.send_sem.at[i], self.recv_sem.at[i], to, self.z)

    def begin(self):
        for c in self.hops:
            c.start()
        self.near.start()

    def pass_on(self):
        for j, (i, ahead, h, k) in enumerate(((4, self.along, 0, 6), (5, self.across, 1, 7))):
            s = self.cols[1 + j]
            self.hop(self.slot(self.core, s), i, self.other).wait_recv()
            more = [
                self.hop(self.slot(self.core, s, h), k, ahead),
                self.hop(self.slot(self.core, s), 1 + j, self.other),
            ]
            for c in more:
                c.start()
            self.hops += more

    def finish(self):
        s = self.cols[3]
        for h in range(2):
            self.hop(self.slot(self.core, s, h), 6 + h, self.other).wait_recv()
        last = self.hop(self.slot(self.core, s), 3, self.other)
        last.start()
        self.near.wait()
        for i in range(4):
            self.hop(self.slot(1 - self.core, self.cols[i]), i, self.other).wait_recv()
        for c in self.hops + [last]:
            c.wait_send()


class SmallSum:
    def __init__(self, mine, pair, line, across, along, out, send_sem, recv_sem):
        me, self.z = lax.axis_index("dp"), lax.axis_index("mp")
        self.me, self.core = me, lax.rem(me, 2)
        self.x, self.y = lax.rem(me // 2, 2), lax.rem(me // 4, 2)
        self.mine, self.pair, self.line, self.a, self.b, self.out = mine, pair, line, across, along, out
        self.send_sem, self.recv_sem = send_sem, recv_sem
        n = pair.shape[1]
        self.n = n
        self.lanes = pl.ds(pl.multiple_of(self.core * n, n), n)
        there = pl.ds(pl.multiple_of((1 - self.core) * n, n), n)

        def move(src, dst, i, d, z):
            return remote(src, dst, send_sem.at[i], recv_sem.at[i], d, z)

        other = toggled(me, 1)
        self.swap = move(mine.at[:, there], pair, 0, other, self.z)
        slot = line.at[self.z]
        self.hops = [move(slot, slot, m, me, peer(self.z, m)) for m in (1, 2, 3)]
        self.hop_x = move(across.at[self.x], across.at[self.x], 4, toggled(me, 2), self.z)
        self.hop_y = move(along.at[self.y], along.at[self.y], 5, toggled(me, 4), self.z)
        done = out.at[:, self.lanes]
        self.last = move(done, done, 6, other, self.z)

    def begin(self):
        self.swap.start()

    def step_line(self, noise):
        n, width = self.n, noise.shape[1]
        self.swap.wait()
        self.line[self.z, :, 0:n] = self.mine[:, self.lanes] + self.pair[...]
        self.line[self.z, 16:24, n : n + width] = noise
        self.line[self.z, 0:16, n : n + width] = jnp.zeros((16, width), f32)
        for c in self.hops:
            c.start()

    def step_across(self):
        for c in self.hops:
            c.wait()
        v = [self.line[i] for i in range(4)]
        self.a[self.x, 0:16, :] = ((v[0] + v[1]) + (v[2] + v[3]))[0:16]
        for i in range(4):
            self.a[self.x, 16 + 8 * i : 24 + 8 * i, :] = v[i][16:24]
        self.hop_x.start()

    def step_along(self):
        self.hop_x.wait()
        self.b[self.y, 0:16, :] = self.a[0, 0:16, :] + self.a[1, 0:16, :]
        for i in range(2):
            self.b[self.y, 16 + 32 * i : 48 + 32 * i, :] = self.a[i, 16:48, :]
        self.hop_y.start()

    def step_out(self):
        self.hop_y.wait()
        n, n_time = self.n, self.out.shape[0] - 16
        self.out[n_time : n_time + 16, self.lanes] = self.b[0, 0:16, 0:n] + self.b[1, 0:16, 0:n]
        rows = jnp.concatenate([self.b[0, 16:80, :], self.b[1, 16:80, :]])
        grads, noise = rows[:, 0:n], rows[:, n : n + n_time].astype(bf16)
        high = grads.astype(bf16)
        rest = grads - high.astype(f32)
        middle = rest.astype(bf16)
        low = (rest - middle.astype(f32)).astype(bf16)
        total = contract(noise, high, 0, 0) + contract(noise, middle, 0, 0)
        self.out[0:n_time, self.lanes] = total + contract(noise, low, 0, 0)
        self.last.start()

    def finish(self):
        self.last.wait()


def one_hot(seg, copies):
    lanes = lax.broadcasted_iota(jnp.int32, (1, 128), 1)
    lanes = jnp.where(lanes < 16 * copies, lax.rem(lanes, 16), -1).astype(f32)
    return jnp.where(seg == lanes, 1.0, 0.0).astype(bf16)


def rotate_rows(v, cosine, sine):
    a, b = v[: HEAD // 2], v[HEAD // 2 :]
    return jnp.concatenate([a * cosine - b * sine, b * cosine + a * sine], axis=0)


def forward_kernel(
    act_any, cot_any, lens, noise, time_weight, time_bias, attn_gain, out_bias, mlp_gain, down_bias,
    qkv_bias, up_bias, qkv_any, ow_any, uw_any, dn_any,
    out_any, mid_any, gfin_any, acc_any, gp_any, wup_any, stream_any, normed_any, q_any, k_any, v_any, merged_any,
    lse_any, dwm_any, wqo_any, bias_rows, seg_col, trig, meta,
    w, x, gfin, bias, biases, stream, normed, qt, kt, vt, merged, lse, send, recv, mid, nm, act, gp,
    stage, lo, slopes, raw_qkv, acc,
    load_sem, bring_send, bring_recv, bias_send, bias_recv, w_send, w_recv,
    out_sem, stage_sem, send_sem, recv_sem,
):
    me, z = lax.axis_index("dp"), lax.axis_index("mp")
    core, col = lax.rem(me, 2), lax.rem(me // 2, 4)
    other, across, along = toggled(me, 1), toggled(me, 2), toggled(me, 4)
    here = act_any.shape[0] // BUCKET
    units = biases.shape[0]
    half = BUCKET // 2
    own, far = tile(core, half), tile(1 - core, half)
    mine = core == z // here
    up_at, dn_at, out_at = units * 512, units * 1024, units * 384

    def block(start, n):
        return pl.ds(pl.multiple_of(start, n), n)

    loads = [
        pltpu.make_async_copy(s, d, load_sem.at[i])
        for i, (s, d) in enumerate(
            (
                (qkv_any.at[:, :, block(core * 128, 128)], raw_qkv),
                (ow_any.at[block(core * 128, 128), :], w.at[block(out_at + z * 128, 128), :]),
                (uw_any.at[:, block(core * 512, 512)], nm.at[:, pl.ds(0, 512)]),
                (dn_any.at[block(core * 512, 512), :], w.at[block(dn_at + z * 512, 512), :]),
            )
        )
    ]
    for c in loads:
        c.start()
    greet([(other, z), (across, z), (along, z)] + [(me, peer(z, m)) for m in (1, 2, 3)])

    bucket_at = lax.rem(z, here)
    bucket = pl.ds(pl.multiple_of(bucket_at * BUCKET, BUCKET), BUCKET)
    brought = (
        (meta, meta),
        (act_any.at[bucket, :], x),
        (cot_any.at[bucket, :], gfin),
    )

    def bring(i, begin):
        src, dst = brought[i]
        near = None if i == 0 else pltpu.make_async_copy(src, dst, load_sem.at[4 + i])
        sent = remote(src, dst, bring_send.at[i], bring_recv.at[i], other, z)

        @pl.when(mine)
        def _():
            if begin:
                sent.start()
                if near is not None:
                    near.start()
            else:
                if near is not None:
                    near.wait()
                sent.wait_send()

        if not begin:

            @pl.when(jnp.logical_not(mine))
            def _():
                sent.wait_recv()

    def row_of(k, u, s):
        if k == 0:
            return u * 384 + 128 * s + (s // 3) * (out_at - 384 + 128 * u - 384 * u)
        return (up_at if k == 1 else dn_at) + u * 512 + 128 * s

    def diagonal(k, m):
        return k == 2 and m > 1

    far_col = toggled(toggled(col, 1), 2)

    def hop(k, m, way):
        i = 3 * k + m - 1
        u = peer(z, m)
        from_hbm = False
        if way == 0 or (way == 3 and diagonal(k, m)):
            s = col if way == 0 else far_col
            n, d = 128, me
            if m == 3:
                at, zz = row_of(k, peer(z, 2), s), peer(z, 1)
            else:
                at, zz, from_hbm = row_of(k, z, s), u, k == 2
        elif way == 1:
            at, n, d, zz = row_of(k, u, col), 128, across, z
        elif way == 2:
            at, n, d, zz = row_of(k, u, col), 128, along, z
        elif way == 3:
            at, n, d, zz = row_of(k, u, toggled(col, 1)), 64, along, z
        else:
            at, n, d, zz = row_of(k, u, toggled(col, 2)) + 64, 64, across, z
        rows = w.at[block(at, n), :]
        src = dn_any.at[block(core * 512 + s * 128, 128), :] if from_hbm else rows
        return remote(src, rows, w_send.at[i, way], w_recv.at[i, way], d, zz)

    def arrived(k, m, way):
        i = 3 * k + m - 1
        u = peer(z, m)
        s = (col, toggled(col, 1), toggled(col, 2), far_col, far_col)[way]
        at = row_of(k, u, s) + (64 if way == 4 else 0)
        rows = w.at[block(at, 128 if way < 3 or diagonal(k, m) else 64), :]
        remote(rows, rows, w_send.at[i, way], w_recv.at[i, way], other, z).wait_recv()

    def send_z(k, m):
        hop(k, m, 0).start()
        if diagonal(k, m):
            hop(k, m, 3).start()

    def pass_a(k, m):
        arrived(k, m, 0)
        if m == 2:
            hop(k, 3, 0).start()
        hop(k, m, 1).start()
        hop(k, m, 2).start()
        if m == 2 and diagonal(k, 3):
            arrived(k, m, 3)
            hop(k, 3, 3).start()

    def pass_b(k, m):
        arrived(k, m, 1)
        if not diagonal(k, m):
            hop(k, m, 3).start()
        arrived(k, m, 2)
        if not diagonal(k, m):
            hop(k, m, 4).start()

    def pass_c(k, m):
        if not (diagonal(k, m) and m == 2):
            arrived(k, m, 3)
        if not diagonal(k, m):
            arrived(k, m, 4)

    bring(1, True)
    for c in range(2):

        @pl.when(core == c)
        def _(c=c):
            bias[0:3, :] = qkv_bias[:, c * 128 : (c + 1) * 128]
            bias[3:4, :] = jnp.zeros((1, 128), f32)
            bias[4:8, :] = up_bias[c * 4 : (c + 1) * 4, :]

    biases[z] = bias[...]
    bias_hops = [
        remote(bias, biases.at[z], bias_send.at[m - 1], bias_recv.at[m - 1], me, peer(z, m))
        for m in (1, 2, 3)
    ]

    loads[0].wait()
    for i in range(3):
        w[block(z * 384 + i * 128, 128), :] = raw_qkv[i].T
    loads[1].wait()
    send_z(0, 1)

    @pl.when(mine)
    def _():
        places = lax.broadcasted_iota(jnp.int32, (1, BUCKET), 1)
        past, start, end = jnp.zeros_like(places), jnp.zeros_like(places), 0
        for i in range(SLOTS):
            end = end + lens[bucket_at * SLOTS + i]
            beyond = places >= end
            past = past + beyond.astype(jnp.int32)
            start = jnp.where(beyond, end, start)
        live = places < end
        meta[8:9, :] = jnp.where(live, past, 2000 + places).astype(f32)
        meta[9:10, :] = (places - jnp.where(live, start, 0)).astype(f32)
        rows = jnp.dot(noise[...], time_weight[...], preferred_element_type=f32) + time_bias[...]
        first = bucket_at == 0
        meta[0:8, :] = jnp.where(first, rows[0:SLOTS], rows[SLOTS : 2 * SLOTS])
        loud = noise[...].astype(f32)
        meta[16:24, 0 : loud.shape[1]] = jnp.where(first, loud[0:SLOTS], loud[SLOTS : 2 * SLOTS])

    bring(0, True)
    bring(2, True)
    for c in bias_hops:
        c.start()
    loads[2].wait()
    for i in range(4):
        w[block(up_at + z * 512 + i * 128, 128), :] = nm[:, i * 128 : (i + 1) * 128].T
    loads[3].wait()
    send_z(0, 2)

    saves = []

    def save(src, dst):
        c = pltpu.make_async_copy(src, dst, out_sem.at[len(saves)])
        c.start()
        saves.append(c)

    def swap(src, dst, i):
        c = remote(src, dst, send_sem.at[i], recv_sem.at[i], other, z)
        c.start()
        return c

    bring(0, False)
    seg_col[...] = jnp.broadcast_to(meta[8:9, :], (128, BUCKET)).T
    step = lax.broadcasted_iota(jnp.int32, (HEAD // 2, 1), 0).astype(f32)
    angles = jnp.exp(step * (-2.0 * math.log(10000.0) / HEAD)) * meta[9:10, :]
    trig[0:32, :] = jnp.cos(angles)
    trig[32:64, :] = jnp.sin(angles)
    pass_a(0, 1)
    send_z(1, 1)
    t_rows = meta[0:8, :]
    high = t_rows.astype(bf16).astype(f32)
    middle_part = (t_rows - high).astype(bf16).astype(f32)
    lowest = t_rows - high - middle_part
    gap = jnp.zeros((8, t_rows.shape[1]), f32)
    time_rows = jnp.concatenate(
        [high, gap, middle_part, gap, lowest, gap, jnp.zeros((80, t_rows.shape[1]), f32)]
    ).astype(bf16)
    bring(1, False)

    def enter(i):
        rs = tile(i, 256)
        added = jnp.dot(one_hot(seg_col[rs, :], 3), time_rows, preferred_element_type=f32)
        stream[rs, :] = x[rs, :].astype(f32) + added

    loop(4, enter)

    def norm(i):
        rs = tile(i, 128)
        centered, scale = row_stats(stream[rs, :])
        normed[rs, :] = (centered * scale * attn_gain[...]).astype(bf16)

    loop(8, norm)
    save(normed, normed_any)
    save(stream.at[own, :], stream_any)
    stream_saved = saves[-1]

    def bias_column(u, s):
        return jnp.broadcast_to(biases[u, s : s + 1, :], (128, 128)).T[:, 0:1]

    def unit(u, between):
        column = jnp.concatenate([bias_column(u, s) for s in range(3)], axis=0)
        proj = contract(w[block(u * 384, 384), :], normed[...], 1, 1) + column
        cs, sn = trig[0:32, :], trig[32:64, :]
        us = tile(u, 128)
        qt[us, :] = jnp.concatenate(
            [rotate_rows(proj[h * HEAD : (h + 1) * HEAD], cs, sn) for h in range(2)], axis=0
        ).astype(bf16)
        kt[us, :] = jnp.concatenate(
            [rotate_rows(proj[128 + h * HEAD : 128 + (h + 1) * HEAD], cs, sn) for h in range(2)],
            axis=0,
        ).astype(bf16)
        vt[us, :] = proj[256:384].astype(bf16)

        def head(j):
            h = 2 * u + j
            hs = tile(h, HEAD)
            keys = (kt[hs, :].astype(f32) * 0.125).T.astype(bf16)
            values = vt[hs, :]
            for t in range(2):
                cs_t = pl.ds(t * 512, 512)
                s = jnp.dot(keys, qt[hs, cs_t], preferred_element_type=f32)
                same = jnp.tile(seg_col[...], (1, 4)) == meta[8:9, cs_t]
                s = jnp.where(same, s, -1e30)
                top = jnp.max(s, axis=0, keepdims=True)
                p = jnp.exp(s - top)
                total = jnp.sum(p, axis=0, keepdims=True)
                o = jnp.dot(values, p.astype(bf16), preferred_element_type=f32)
                merged[hs, cs_t] = (o / total).astype(bf16)
                lse[h, :, cs_t] = top + jnp.log(total)

        for j in range(2):
            for step in between[j]:
                step[0](*step[1:])
            head(j)

    pass_a(0, 2)
    send_z(2, 1)
    for c in bias_hops:
        c.wait()
    unit(z, (((pass_b, 0, 1),), ((pass_a, 0, 3), (send_z, 1, 2))))
    pass_b(0, 2)
    pass_c(0, 1)
    unit(peer(z, 1), (((pass_a, 1, 1), (send_z, 2, 2)), ((pass_b, 0, 3), (pass_c, 0, 2))))
    unit(peer(z, 2), (((pass_a, 2, 1),), ((pass_b, 1, 1), (pass_c, 0, 3))))
    unit(peer(z, 3), (((pass_a, 1, 2), (pass_c, 1, 1)), ((pass_b, 2, 1),)))
    pass_a(2, 2)
    save(qt, q_any)
    save(kt, k_any)
    save(vt, v_any)
    save(merged, merged_any)
    save(lse, lse_any)
    save(w.at[pl.ds(0, up_at), :], wqo_any)

    w_out = w.at[pl.ds(out_at, units * 128), :]
    w_up = w.at[pl.ds(up_at, units * 512), :]
    w_dn = w.at[pl.ds(dn_at, units * 512), :]
    send[0] = contract(merged[:, far], w_out[...], 0, 0).astype(bf16)
    swap0 = swap(send.at[0], recv.at[0], 0)
    mid[...] = contract(merged[:, own], w_out[...], 0, 0)
    bring(2, False)

    def mask(i):
        rs = tile(i, 256)
        live = jnp.where(seg_col[rs, :][:, 0:1] < 1000.0, 1.0, 0.0)
        gfin[rs, :] = (gfin[rs, :].astype(f32) * live).astype(bf16)

    loop(4, mask)
    swap0.wait()

    def middle(i):
        rs = tile(i, 128)
        ro = pl.ds(pl.multiple_of(core * half + i * 128, 128), 128)
        v = stream[ro, :] + (mid[rs, :] + recv[0, rs, :].astype(f32)) + out_bias[...]
        mid[rs, :] = v
        centered, scale = row_stats(v)
        nm[ro, :] = (centered * scale * mlp_gain[...]).astype(bf16)

    loop(4, middle)
    save(mid, mid_any)
    save(gfin.at[own, :], gfin_any)
    swap1 = swap(nm.at[own, :], nm.at[own, :], 1)
    pass_c(2, 1)
    pass_b(1, 2)
    pass_a(1, 3)
    swap1.wait()

    def gelu_parts(u, rs):
        column = jnp.concatenate([bias_column(u, 4 + s) for s in range(4)], axis=0)
        pre = contract(w_up[tile(u, 512), :], nm[rs, :], 1, 1) + column
        sq = pre * pre
        th = jnp.tanh(pre * (0.7978845608028654 + (0.7978845608028654 * 0.044715) * sq))
        hp = 0.5 + 0.5 * th
        slope = hp + pre * (hp * (1.0 - th)) * (
            0.7978845608028654 + (3 * 0.7978845608028654 * 0.044715) * sq
        )
        return pre * hp, slope

    def hidden_unit(n, u):
        us = tile(u, 512)

        def hidden(t):
            rs = tile(t, 256)
            value, slope = gelu_parts(u, rs)
            act[us, rs] = value.astype(bf16)
            gp[us, rs] = (contract(w_dn[us, :], gfin[rs, :], 1, 1) * slope).astype(bf16)

        loop(4, hidden)

    def weight_part(n, u, i):
        us = tile(u, 512)
        if n > 0:
            pltpu.make_async_copy(stage.at[i], dwm_any.at[u, i], stage_sem.at[i]).wait()
        left, right = ((gp, nm), (act, gfin))[i]
        stage[i] = contract(left[us, :], right[...], 1, 0).astype(bf16)
        pltpu.make_async_copy(stage.at[i], dwm_any.at[u, i], stage_sem.at[i]).start()
        if i == 0:
            bias_rows[u, :, 384:896] = contract(jnp.ones((8, BUCKET), bf16), gp[us, :], 1, 1)

    def weights_unit(n, u):
        weight_part(n, u, 0)
        weight_part(n, u, 1)

    def partial_sums(n, u):
        us = tile(u, 512)
        for left, right, kept in ((act, w_dn, stream), (gp, w_up, acc)):
            for rows in (far, own):
                total = contract(left[us, rows], right[us, :], 0, 0)
                if n > 0:
                    total = total + kept[rows, :]
                kept[rows, :] = total

    bias_rows[...] = jnp.zeros_like(bias_rows)
    stream_saved.wait()
    hidden_unit(0, z)
    pass_c(1, 2)
    pass_b(2, 2)
    pass_a(2, 3)
    weights_unit(0, z)
    pass_c(2, 2)
    pass_b(1, 3)
    partial_sums(0, z)
    hidden_unit(1, peer(z, 1))
    pass_c(1, 3)
    pass_b(2, 3)
    weights_unit(1, peer(z, 1))
    partial_sums(1, peer(z, 1))
    hidden_unit(2, peer(z, 2))
    weights_unit(2, peer(z, 2))
    partial_sums(2, peer(z, 2))
    last_unit = peer(z, 3)
    us = tile(last_unit, 512)
    save(acc, acc_any)

    def last_values(t):
        rs = tile(t, 256)
        value, slope = gelu_parts(last_unit, rs)
        act[us, rs] = value.astype(bf16)
        slopes[:, rs] = slope

    def last_slopes(t):
        rs = tile(t, 256)
        gp[us, rs] = (contract(w_dn[us, :], gfin[rs, :], 1, 1) * slopes[:, rs]).astype(bf16)

    loop(4, last_values)
    save(w_up.at[us, :], wup_any)
    weight_part(3, last_unit, 1)
    pass_c(2, 3)
    send[1] = (stream[far, :] + contract(act[us, far], w_dn[us, :], 0, 0)).astype(bf16)
    swap2 = swap(send.at[1], recv.at[1], 2)
    loop(4, last_slopes)
    save(gp.at[us, :], gp_any)
    slopes[...] = stream[own, :] + contract(act[us, own], w_dn[us, :], 0, 0)
    swap2.wait()

    def finish(i):
        rs = tile(i, 128)
        ro = pl.ds(pl.multiple_of(core * half + i * 128, 128), 128)
        live = jnp.where(seg_col[ro, :][:, 0:1] < 1000.0, 1.0, 0.0)
        v = mid[rs, :] + (slopes[rs, :] + recv[1, rs, :].astype(f32)) + down_bias[...]
        lo[rs, :] = (live * v).astype(bf16)

    loop(4, finish)
    save(lo, out_any)
    weight_part(3, last_unit, 0)
    for i in range(2):
        pltpu.make_async_copy(stage.at[i], dwm_any.at[0, i], stage_sem.at[i]).wait()
    for c in saves:
        if c is not stream_saved:
            c.wait()
    for k in range(3):
        for m in (1, 2, 3):
            for way in range(4 if diagonal(k, m) else 5):
                hop(k, m, way).wait_send()


def column_devices(me, z):
    both = (me, toggled(me, 1))
    return [(both[1], z)] + [(d, peer(z, m)) for m in (1, 2, 3) for d in both]


def backward_kernel(
    gather,
    meta, seg_col, trig, attn_gain, mlp_gain, bias_rows, lse,
    wqo_any, mid_any, gfin_any, acc_any, gp_any, wup_any, stream_any, normed_any, q_any, k_any, v_any, merged_any, lo_any, dwm_any,
    out_any, dwa_any, gathered_any, parts, sums,
    wqo, mid, gfin, gmid, gm, stream, normed, qt, kt, vt, merged,
    gmerged, gproj, acck, accv, send, recv, gin, stage, gin_low, small, mine,
    keep_m, got_m, last_m, keep_a, got_a, last_a, own_m, line_got_m, own_a, line_got_a, final,
    small_pair, small_line, small_x, small_y,
    load_sem, stage_sem, send_sem, recv_sem, near_sem,
    lo_send, lo_recv, gin_send, gin_recv, pm_load, pm_send, pm_recv, pa_load, pa_send, pa_recv,
    lm_send, lm_recv, la_send, la_recv, gm_send, gm_recv, ga_send, ga_recv, small_send, small_recv,
):
    me, z = lax.axis_index("dp"), lax.axis_index("mp")
    core, other = lax.rem(me, 2), toggled(me, 1)
    half = BUCKET // 2
    units = wqo.shape[0] // 512
    n_qkv = units * 384
    w_qkv, w_out = pl.ds(0, n_qkv), pl.ds(n_qkv, units * 128)
    loads = {}
    for name, src, dst in (
        ("far", acc_any.at[tile(1 - core, half), :], gmid),
        ("gp", gp_any, gproj.at[pl.ds(0, 512), :]),
        ("up", wup_any, gproj.at[pl.ds(512, 512), :]),
        ("own", acc_any.at[tile(core, half), :], gin),
        ("mid", mid_any, mid),
        ("gfin", gfin_any, gfin),
        ("out", wqo_any.at[w_out, :], wqo.at[w_out, :]),
        ("q", q_any, qt),
        ("k", k_any, kt),
        ("v", v_any, vt),
        ("merged", merged_any, merged),
        ("qkv", wqo_any.at[w_qkv, :], wqo.at[w_qkv, :]),
        ("stream", stream_any, stream),
        ("normed", normed_any, normed),
    ):
        loads[name] = pltpu.make_async_copy(src, dst, load_sem.at[len(loads)])
        loads[name].start()
    wqkv, wout = wqo.at[w_qkv, :], wqo.at[w_out, :]
    cosine, sine = trig.at[pl.ds(0, 32), :], trig.at[pl.ds(32, 32), :]
    greet([(toggled(me, 2), z), (toggled(me, 4), z)] + column_devices(me, z))
    plane_m = PlaneSum(dwm_any, keep_m, got_m, last_m, pm_load, pm_send, pm_recv)
    spread_lo = Spread(lo_any, out_any, near_sem.at[0], lo_send, lo_recv)
    plane_m.begin(0)
    spread_lo.begin()
    plane_m.begin(3)

    def put_m(u, order, total):
        for i in range(2):
            own_m[u, i * 128 + order * 64 : i * 128 + (order + 1) * 64, :] = total[i]

    def put_a(u, order, total):
        own_a[u, order * 64 : (order + 1) * 64, :] = total[0]

    own = tile(core, half)
    far = tile(1 - core, half)
    gp_last, up_last = gproj.at[pl.ds(0, 512), :], gproj.at[pl.ds(512, 512), :]

    def swap(src, dst, i):
        c = remote(src, dst, send_sem.at[i], recv_sem.at[i], other, z)
        c.start()
        return c

    for name in ("far", "gp", "up"):
        loads[name].wait()
    send[...] = (gmid[...] + contract(gp_last[:, far], up_last[...], 0, 0)).astype(bf16)
    swap_in = swap(send, recv, 0)
    loads["own"].wait()
    gin[...] += contract(gp_last[:, own], up_last[...], 0, 0)
    loads["mid"].wait()
    loads["gfin"].wait()
    small[...] = jnp.zeros_like(small)
    swap_in.wait()

    def back_mlp(i):
        rs = tile(i, 128)
        ro = pl.ds(pl.multiple_of(core * half + i * 128, 128), 128)
        err = gin[rs, :] + recv[rs, :].astype(f32)
        grad, gain_grad = norm_back(mid[rs, :], mlp_gain[...], err)
        gf = gfin[rs, :].astype(f32)
        grad = grad + gf
        gmid[rs, :] = grad
        gm[ro, :] = grad.astype(bf16)
        small[0:1, :] += gain_grad
        small[1:2, :] += jnp.sum(grad, axis=0, keepdims=True)
        small[2:3, :] += jnp.sum(gf, axis=0, keepdims=True)

    loop(4, back_mlp)
    swap_gm = swap(gm.at[own, :], gm.at[own, :], 1)
    loads["out"].wait()
    swap_gm.wait()
    for t in range(2):
        cs = pl.ds(t * 512, 512)
        gmerged[:, cs] = contract(wout[...], gm[cs, :], 1, 1).astype(bf16)
    for name in ("q", "k", "v", "merged"):
        loads[name].wait()

    def head(h):
        hs = tile(h, HEAD)
        u = h // 2
        j = lax.rem(h, 2)
        at = u * 384 + j * HEAD
        keys_t = (kt[hs, :].astype(f32) * 0.125).astype(bf16)
        keys = keys_t.astype(f32).T.astype(bf16)
        values = vt[hs, :].astype(f32).T.astype(bf16)
        for t in range(2):
            cs = pl.ds(t * 512, 512)
            q, go = qt[hs, cs], gmerged[hs, cs]
            dl = jnp.sum(go.astype(f32) * merged[hs, cs].astype(f32), axis=0, keepdims=True)
            s = jnp.dot(keys, q, preferred_element_type=f32)
            same = jnp.tile(seg_col[...], (1, 4)) == meta[8:9, cs]
            p = jnp.exp(jnp.where(same, s, -1e30) - lse[h, :, cs])
            dp = jnp.dot(values, go, preferred_element_type=f32)
            ds = (p * (dp - dl)).astype(bf16)
            dq = jnp.dot(keys_t, ds, preferred_element_type=f32)
            gproj[pl.ds(pl.multiple_of(at, HEAD), HEAD), cs] = rotate_rows(
                dq, cosine[:, cs], -sine[:, cs]
            ).astype(bf16)
            dv = contract(go, p.astype(bf16), 1, 1)
            dk = contract(q, ds, 1, 1)
            if t == 0:
                accv[...] = dv
                acck[...] = dk
            else:
                dk = (acck[...] + dk) * 0.125
                gproj[pl.ds(pl.multiple_of(at + 128, HEAD), HEAD), :] = rotate_rows(
                    dk, cosine[...], -sine[...]
                ).astype(bf16)
                gproj[pl.ds(pl.multiple_of(at + 256, HEAD), HEAD), :] = (accv[...] + dv).astype(bf16)

    def heads(i):
        head(2 * i)
        head(2 * i + 1)

        @pl.when(i == 1)
        def _():
            plane_m.middle(0)
            plane_m.begin(1)
            spread_lo.pass_first()

        @pl.when(i == 2)
        def _():
            plane_m.middle(3)
            plane_m.begin(2)

    loop(units, heads)
    line_m = LineSum(own_m, line_got_m, lm_send, lm_recv)
    line_a = LineSum(own_a, line_got_a, la_send, la_recv)
    plane_m.end(0, put_m)
    line_m.step(0, 0)
    loads["qkv"].wait()
    send[...] = contract(gproj[:, far], wqkv[...], 0, 0).astype(bf16)
    swap_out = swap(send, recv, 2)
    gin[...] = contract(gproj[:, own], wqkv[...], 0, 0)
    loads["stream"].wait()
    swap_out.wait()

    def back(i):
        rs = tile(i, 128)
        ro = pl.ds(pl.multiple_of(core * half + i * 128, 128), 128)
        err = gin[rs, :] + recv[rs, :].astype(f32)
        grad, gain_grad = norm_back(stream[rs, :], attn_gain[...], err)
        grad = grad + gmid[rs, :]
        high = grad.astype(bf16)
        gin_low[rs, :] = high
        small[3:4, :] += gain_grad
        member = one_hot(seg_col[ro, :], 1)
        low = (grad - high.astype(f32)).astype(bf16)
        small[8:16, :] += (contract(member, high, 0, 0) + contract(member, low, 0, 0))[0:8]

    loop(4, back)
    spread_gin = Spread(gin_low, gathered_any, near_sem.at[1], gin_send, gin_recv)
    spread_gin.begin()
    plane_m.end(3, put_m)
    line_m.step(0, 3)
    line_m.step(1, 0)
    t_rows = small[8:16, :]
    mine[0:8, :] = jnp.concatenate(
        [
            small[0:4, :],
            jnp.sum(t_rows, axis=0, keepdims=True),
            jnp.zeros((3, t_rows.shape[1]), f32),
        ]
    )
    mine[8:16, :] = jnp.zeros((8, t_rows.shape[1]), f32)
    mine[16:24, :] = t_rows
    loads["normed"].wait()
    plane_a = PlaneSum(dwa_any, keep_a, got_a, last_a, pa_load, pa_send, pa_recv)
    order = (0, 3, 1, 2)

    def stored(i):
        return pltpu.make_async_copy(stage.at[i % 2], dwa_any.at[order[i]], stage_sem.at[i % 2])

    def weights(i):
        u = order[i]
        us = pl.ds(u * 384, 384)
        if i > 1:
            stored(i - 2).wait()
            plane_a.begin(order[i - 2])
        of_qkv = contract(gproj[us, :], normed[...], 1, 0).astype(bf16)
        of_out = contract(merged[pl.ds(u * 128, 128), :], gm[...], 1, 0).astype(bf16)
        for k in range(4):
            quarter = of_qkv[k * 128 : (k + 1) * 128] if k < 3 else of_out
            for j in range(2):
                stage[i % 2, 0, k // 2, k % 2, j] = quarter[j * 64 : (j + 1) * 64]
        stored(i).start()
        row = lax.broadcasted_iota(jnp.int32, (8, 1), 0) == core * units + u
        mine[8:16, 0:384] += jnp.where(
            row, contract(jnp.ones((8, BUCKET), bf16), gproj[us, :], 1, 1), 0.0
        )
        mine[8:16, 384:896] += jnp.where(row, bias_rows[u, :, 384:896], 0.0)

    little = SmallSum(mine, small_pair, small_line, small_x, small_y, sums, small_send, small_recv)

    def put_final_m(total):
        final[128:384, :] = total

    def put_final_a(total):
        final[0:128, :] = total

    if gather:
        gather_m = PlaneGather(final, parts, (128, 256), near_sem.at[2, 0], gm_send, gm_recv)
        gather_a = PlaneGather(final, parts, (0, 128), near_sem.at[3, 0], ga_send, ga_recv)
    weights(0)
    weights(1)
    plane_m.middle(1)
    spread_lo.pass_second()
    weights(2)
    weights(3)
    little.begin()
    line_m.step(1, 3)
    line_m.step(2, 0)
    plane_m.middle(2)
    for i in (2, 3):
        stored(i).wait()
        plane_a.begin(order[i])
    plane_m.end(1, put_m)
    line_m.step(0, 1)
    line_m.step(2, 3)
    little.step_line(meta[16:24, 0 : sums.shape[0] - 16])
    plane_m.end(2, put_m)
    line_m.step(0, 2)
    line_m.step(1, 1)
    spread_gin.pass_first()
    line_m.step(1, 2)
    plane_a.middle(0)
    plane_a.middle(3)
    little.step_across()
    plane_a.middle(1)
    plane_a.middle(2)
    line_m.finish(put_final_m)
    little.step_along()
    if gather:
        gather_m.begin()
    plane_a.end(0, put_a)
    line_a.step(0, 0)
    plane_a.end(3, put_a)
    line_a.step(0, 3)
    line_a.step(1, 0)
    plane_a.end(1, put_a)
    line_a.step(0, 1)
    line_a.step(1, 3)
    plane_a.end(2, put_a)
    line_a.step(0, 2)
    line_a.step(1, 1)
    line_a.step(1, 2)
    line_a.step(2, 0)
    line_a.step(2, 3)
    spread_gin.pass_second()
    if gather:
        gather_m.pass_on()
    line_a.finish(put_final_a)
    if gather:
        gather_a.begin()
        little.step_out()
        gather_a.pass_on()
        gather_m.finish()
        gather_a.finish()
    else:
        little.step_out()
        out = pltpu.make_async_copy(final, parts, near_sem.at[2, 0])
        out.start()
        out.wait()
    little.finish()
    spread_lo.finish()
    spread_gin.finish()
    for u in range(4):
        plane_m.drain(u)
        plane_a.drain(u)


def deliver_kernel(
    parts, gin, lo, sums, little, grad_in, lo_out, time_out, qkv_out, out_out, up_out, down_out,
    gain_m, out_bias, down_bias, gain_a, time_bias, qkv_bias, up_bias,
):
    s = lax.rem(pl.program_id(0), 4)

    @pl.when(pl.program_id(0) == 0)
    def _():
        for i, ref in enumerate((gain_m, out_bias, down_bias, gain_a, time_bias)):
            ref[...] = little[i : i + 1, :]
        units = 4
        rows = lax.broadcasted_iota(jnp.int32, (8, 1), 0)
        for c in range(2):
            here = rows == c * units + lax.axis_index("mp")
            mine = jnp.sum(jnp.where(here, little[8:16, :], 0.0), axis=0, keepdims=True)
            for i in range(3):
                qkv_bias[i : i + 1, c * 128 : (c + 1) * 128] = mine[:, i * 128 : (i + 1) * 128]
            up_bias[:, c * 512 : (c + 1) * 512] = mine[:, 384:896]

    grad_in[...] = gin[...].astype(f32)
    lo_out[...] = lo[...]
    time_out[...] = sums[...]
    down_out[...] = parts[0, 0, 256:384, :].astype(f32)
    up_out[...] = parts[0, 0, 128:256, :].T.astype(f32)

    @pl.when(s < 3)
    def _():
        qkv_out[0] = parts[0, 0, 0:128, :].T.astype(f32)

    @pl.when(s == 3)
    def _():
        out_out[...] = parts[0, 0, 0:128, :].astype(f32)


def shape(s, t):
    return jax.ShapeDtypeStruct(s, t)


def run_forward(args, here, units, width):
    rows = BUCKET
    half = rows // 2
    feat = units * 128
    hid = units * 512
    anyspec = pl.BlockSpec(memory_space=pl.ANY)
    vm = pl.BlockSpec(memory_space=VMEM)
    outs = (
        shape((half, width), bf16),
        shape((half, width), f32),
        shape((half, width), bf16),
        shape((rows, width), f32),
        shape((512, width), bf16),
        shape((512, width), bf16),
        shape((half, width), f32),
        shape((rows, width), bf16),
        shape((feat, rows), bf16),
        shape((feat, rows), bf16),
        shape((feat, rows), bf16),
        shape((feat, rows), bf16),
        shape((2 * units, 1, rows), f32),
        shape((units, 2, 512, width), bf16),
        shape((hid, width), bf16),
        shape((units, 8, width), f32),
        shape((rows, 128), f32),
        shape((64, rows), f32),
        shape((24, width), f32),
    )
    dma = pltpu.SemaphoreType.DMA
    return pl.pallas_call(
        forward_kernel,
        out_shape=outs,
        in_specs=[anyspec] * 2 + [pl.BlockSpec(memory_space=pltpu.SMEM)] + [vm] * 9 + [anyspec] * 4,
        out_specs=[anyspec] * 15 + [vm] * 4,
        scratch_shapes=[
            VMEM((3 * hid, width), bf16),
            VMEM((rows, width), bf16),
            VMEM((rows, width), bf16),
            VMEM((8, 128), f32),
            VMEM((units, 8, 128), f32),
            VMEM((rows, width), f32),
            VMEM((rows, width), bf16),
            VMEM((feat, rows), bf16),
            VMEM((feat, rows), bf16),
            VMEM((feat, rows), bf16),
            VMEM((feat, rows), bf16),
            VMEM((2 * units, 1, rows), f32),
            VMEM((2, half, width), bf16),
            VMEM((2, half, width), bf16),
            VMEM((half, width), f32),
            VMEM((rows, width), bf16),
            VMEM((hid, rows), bf16),
            VMEM((hid, rows), bf16),
            VMEM((2, 512, width), bf16),
            VMEM((half, width), bf16),
            VMEM((half, width), f32),
            VMEM((3, width, 128), bf16),
            VMEM((rows, width), f32),
            dma((7,)),
            dma((3,)),
            dma((3,)),
            dma((3,)),
            dma((3,)),
            dma((9, 5)),
            dma((9, 5)),
            dma((16,)),
            dma((2,)),
            dma((3,)),
            dma((3,)),
        ],
        compiler_params=pltpu.CompilerParams(
            collective_id=0, has_side_effects=True, vmem_limit_bytes=63 * MIB
        ),
        name="forward",
    )(*args)


def run_backward(args, gather, here, units, rows, width, n_time):
    half = rows // 2
    feat = units * 128
    anyspec = pl.BlockSpec(memory_space=pl.ANY)
    vm = pl.BlockSpec(memory_space=VMEM)
    dma = pltpu.SemaphoreType.DMA
    return pl.pallas_call(
        functools.partial(backward_kernel, gather),
        out_shape=(
            shape((here * rows, width), bf16),
            shape((units, 1, 2, 2, 2, 64, width), bf16),
            shape((here * rows, width), bf16),
            shape((2, 4, 384, width) if gather else (384, width), bf16),
            shape((n_time + 16, width), f32),
        ),
        in_specs=[vm] * 7 + [anyspec] * (len(args) - 7),
        out_specs=[anyspec] * 4 + [vm],
        scratch_shapes=[
            VMEM((4 * feat, width), bf16),
            VMEM((half, width), f32),
            VMEM((half, width), bf16),
            VMEM((half, width), f32),
            VMEM((rows, width), bf16),
            VMEM((half, width), f32),
            VMEM((rows, width), bf16),
            VMEM((feat, rows), bf16),
            VMEM((feat, rows), bf16),
            VMEM((feat, rows), bf16),
            VMEM((feat, rows), bf16),
            VMEM((feat, rows), bf16),
            VMEM((3 * feat, rows), bf16),
            VMEM((HEAD, rows), f32),
            VMEM((HEAD, rows), f32),
            VMEM((half, width), bf16),
            VMEM((half, width), bf16),
            VMEM((half, width), f32),
            VMEM((2, 1, 2, 2, 2, 64, width), bf16),
            VMEM((half, width), bf16),
            VMEM((16, width), f32),
            VMEM((24, width), f32),
            VMEM((2, units, 2, 2, 64, width), bf16),
            VMEM((2, units, 2, 2, 64, width), bf16),
            VMEM((2, units, 2, 64, width), bf16),
            VMEM((2, units, 1, 2, 64, width), bf16),
            VMEM((2, units, 1, 2, 64, width), bf16),
            VMEM((2, units, 1, 64, width), bf16),
            VMEM((units, 256, width), bf16),
            VMEM((2, 3, 256, width), bf16),
            VMEM((units, 128, width), bf16),
            VMEM((2, 3, 128, width), bf16),
            VMEM((384, width), bf16),
            VMEM((24, width // 2), f32),
            VMEM((4, 24, width // 2 + n_time), f32),
            VMEM((2, 48, width // 2 + n_time), f32),
            VMEM((2, 80, width // 2 + n_time), f32),
            dma((14,)),
            dma((2,)),
            dma((3,)),
            dma((3,)),
            dma((4, 1)),
            dma((7,)),
            dma((4,)),
            dma((7,)),
            dma((4,)),
            dma((2, units)),
            dma((2, 2, units)),
            dma((2, 2, units)),
            dma((2, units)),
            dma((2, 2, units)),
            dma((2, 2, units)),
            dma((2, 3)),
            dma((2, 3)),
            dma((2, 3)),
            dma((2, 3)),
            dma((8,)),
            dma((8,)),
            dma((8,)),
            dma((8,)),
            dma((7,)),
            dma((7,)),
        ],
        compiler_params=pltpu.CompilerParams(
            collective_id=1, has_side_effects=True, vmem_limit_bytes=63 * MIB
        ),
        name="backward",
    )(*args)


def run_deliver(parts, gin, lo, sums, n_time):
    rows, width = gin.shape
    steps = 8
    part = parts.shape[2] // 3
    hid = steps * part
    at = lambda i: (i, 0)
    return pl.pallas_call(
        deliver_kernel,
        grid=(steps,),
        out_shape=(
            shape((rows, width), f32),
            shape((rows, width), bf16),
            shape((n_time, width), f32),
            shape((3, width, 2 * part), f32),
            shape((2 * part, width), f32),
            shape((width, hid), f32),
            shape((hid, width), f32),
            *(shape((1, width), f32) for _ in range(5)),
            shape((3, 2 * part), f32),
            shape((1, hid), f32),
        ),
        in_specs=[
            pl.BlockSpec((1, 1, 3 * part, width), lambda i: (i // 4, i % 4, 0, 0)),
            pl.BlockSpec((rows // steps, width), at),
            pl.BlockSpec((rows // steps, width), at),
            pl.BlockSpec((n_time // steps, width), at),
            pl.BlockSpec((16, width), lambda i: (n_time // 16, 0)),
        ],
        out_specs=[
            pl.BlockSpec((rows // steps, width), at),
            pl.BlockSpec((rows // steps, width), at),
            pl.BlockSpec((n_time // steps, width), at),
            pl.BlockSpec((1, width, part), lambda i: (jnp.minimum(i % 4, 2), 0, i // 4)),
            pl.BlockSpec((part, width), lambda i: (i // 4, 0)),
            pl.BlockSpec((width, part), lambda i: (0, i)),
            pl.BlockSpec((part, width), at),
            *(pl.BlockSpec((1, width), lambda i: (0, 0)) for _ in range(5)),
            pl.BlockSpec((3, 2 * part), lambda i: (0, 0)),
            pl.BlockSpec((1, hid), lambda i: (0, 0)),
        ],
        compiler_params=pltpu.CompilerParams(vmem_limit_bytes=63 * MIB),
        name="deliver",
    )(parts, gin, lo, sums, sums)


def local(
    ndp, nmp, activations, noise_embed, lengths, time_weight, time_bias, attn_gain, qkv_weight, qkv_bias,
    out_weight, out_bias, mlp_gain, up_weight, up_bias, down_weight, down_bias, cotangent,
):
    width = activations.shape[1]
    here = activations.shape[0] // BUCKET
    assert 2 * here == nmp and qkv_weight.shape[2] == 256 and up_weight.shape[1] == 1024
    assert ndp % 8 == 0 and noise_embed.shape[0] == here * SLOTS
    n_time = time_weight.shape[0]
    def row(v):
        return v.reshape(1, width)

    (
        lo, mid, gfin, acc, gp, wup, stream, normed, qt, kt, vt, merged, lse, dwm, wqo, bias_rows, seg_col, trig, meta,
    ) = run_forward(
        (
            activations, cotangent, lengths, noise_embed, time_weight, row(time_bias), row(attn_gain),
            row(out_bias), row(mlp_gain), row(down_bias), qkv_bias, up_bias.reshape(8, 128),
            qkv_weight.transpose(1, 0, 2), out_weight, up_weight, down_weight,
        ),
        here, nmp, width,
    )
    gather = ndp == 8
    lo_all, _, gathered, parts, sums = run_backward(
        (
            meta, seg_col, trig, row(attn_gain), row(mlp_gain), bias_rows, lse, wqo, mid, gfin, acc, gp, wup, stream,
            normed, qt, kt, vt,
            merged, lo, dwm.reshape(nmp, 2, 2, 2, 2, 64, width),
        ),
        gather, here, nmp, BUCKET, width, n_time,
    )
    if not gather:
        groups = [[i + 8 * k for k in range(ndp // 8)] for i in range(8)]
        parts = lax.psum(parts, "dp", axis_index_groups=groups)
        sums = lax.psum(sums, "dp", axis_index_groups=groups)
        groups = [[8 * k + i for i in range(8)] for k in range(ndp // 8)]
        parts = lax.all_gather(parts, "dp", axis_index_groups=groups)
        parts = parts.reshape(4, 2, 384, width).transpose(1, 0, 2, 3)
    (
        grad_input, layer_output, grad_time_weight, grad_qkv, grad_out, grad_up, grad_down,
        grad_mlp_gain, grad_out_bias, grad_down_bias, grad_attn_gain, grad_time_bias, grad_qkv_bias, grad_up_bias,
    ) = run_deliver(parts, gathered, lo_all, sums, n_time)
    grad_qkv = grad_qkv.transpose(1, 0, 2)
    return (
        layer_output,
        grad_input,
        grad_time_weight,
        grad_time_bias.reshape(-1),
        grad_attn_gain.reshape(-1),
        grad_qkv,
        grad_qkv_bias,
        grad_out,
        grad_out_bias.reshape(-1),
        grad_mlp_gain.reshape(-1),
        grad_up,
        grad_up_bias.reshape(-1),
        grad_down,
        grad_down_bias.reshape(-1),
    )


def solution(mesh):
    in_specs = (
        P("dp", None),
        P("dp", None),
        P("dp"),
        P(),
        P(),
        P(),
        P(None, None, "mp"),
        P(None, "mp"),
        P("mp", None),
        P(),
        P(),
        P(None, "mp"),
        P("mp"),
        P("mp", None),
        P(),
        P("dp", None),
    )
    out_specs = (
        P("dp", None),
        P("dp", None),
        P(),
        P(),
        P(),
        P(None, None, "mp"),
        P(None, "mp"),
        P("mp", None),
        P(),
        P(),
        P(None, "mp"),
        P("mp"),
        P("mp", None),
        P(),
    )
    body = functools.partial(local, mesh.shape["dp"], mesh.shape["mp"])
    return jax.shard_map(body, mesh=mesh, in_specs=in_specs, out_specs=out_specs, check_vma=False)
```

```python
import functools
import math

import jax
import jax.numpy as jnp
from jax import lax
from jax.experimental import pallas as pl
from jax.experimental.pallas import tpu as pltpu
from jax.sharding import PartitionSpec as P

HEAD = 64
BUCKET = 1024
SLOTS = 8
MIB = 1 << 20
MESH = pl.DeviceIdType.MESH
VMEM = pltpu.VMEM
bf16 = jnp.bfloat16
f32 = jnp.float32


def contract(a, b, ca, cb):
    return lax.dot_general(a, b, (((ca,), (cb,)), ((), ())), preferred_element_type=f32)


def tile(i, n):
    return pl.ds(pl.multiple_of(i * n, n), n)


def loop(n, body):
    def step(i, carry):
        body(i)
        return carry

    lax.fori_loop(0, n, step, 0)


def row_stats(v):
    centered = v - jnp.mean(v, axis=-1, keepdims=True)
    return centered, lax.rsqrt(jnp.mean(centered * centered, axis=-1, keepdims=True) + 1e-05)


def norm_back(v, gain, err):
    centered, scale = row_stats(v)
    xhat = centered * scale
    u = err * gain
    grad = (
        u - jnp.mean(u, axis=-1, keepdims=True) - xhat * jnp.mean(u * xhat, axis=-1, keepdims=True)
    ) * scale
    return grad, jnp.sum(err * xhat, axis=0, keepdims=True)


def toggled(v, bit):
    return v + bit - 2 * bit * lax.rem(v // bit, 2)


def peer(z, m):
    low = lax.rem(lax.rem(z, 2) + m % 2, 2)
    return low + 2 * lax.rem(z // 2 + m // 2, 2)


def greet(targets):
    barrier = pltpu.get_barrier_semaphore()
    for d, z in targets:
        pl.semaphore_signal(barrier, inc=1, device_id={"dp": d, "mp": z}, device_id_type=MESH)
    pl.semaphore_wait(barrier, len(targets))


def remote(src, dst, ss, rs, d, z):
    return pltpu.make_async_remote_copy(
        src_ref=src,
        dst_ref=dst,
        send_sem=ss,
        recv_sem=rs,
        device_id={"dp": d, "mp": z},
        device_id_type=MESH,
    )


class Spread:
    def __init__(self, src, out, near_sem, send_sem, recv_sem):
        me, z = lax.axis_index("dp"), lax.axis_index("mp")
        self.core = core = lax.rem(me, 2)
        self.kind = kind = z // 2
        self.place = z + core * (3 - 2 * z)
        self.start_place = z + kind * (3 - 2 * z)
        self.out, self.send, self.recv = out, send_sem, recv_sem
        self.me, self.z, self.ahead = me, z, z + 1 - 2 * core
        keeper = me - core + kind
        dst = self.piece(self.start_place, core, kind)
        rs = recv_sem.at[2 * self.start_place + core]
        self.near = pltpu.make_async_copy(src, dst, near_sem.at[0])
        self.first = [
            remote(src, dst, send_sem.at[0], rs, keeper, z + 1 - 2 * kind),
            remote(src, dst, send_sem.at[1], rs, keeper, z - 1 + 2 * kind),
            remote(src, dst, send_sem.at[2], rs, toggled(me, 1), z),
        ]

    def piece(self, m, h, kind):
        rows = self.out.shape[0] // 4
        at = 2 * (m + kind * (1 - 2 * m)) + h
        return self.out.at[pl.ds(pl.multiple_of(at * rows, rows), rows), :]

    def hop(self, m, h, i):
        ref = self.piece(m, h, self.core)
        return remote(ref, ref, self.send.at[i], self.recv.at[2 * m + h], self.me, self.ahead)

    def begin(self):
        self.first[0].start()

        @pl.when(self.start_place == 1)
        def _():
            self.first[1].start()

        @pl.when(self.core == self.kind)
        def _():
            self.near.start()

        @pl.when(self.core != self.kind)
        def _():
            self.first[2].start()

    def forward(self, place, m, i):
        @pl.when(self.place == place)
        def _():
            for h in range(2):
                self.hop(m, h, i + h).wait_recv()
                self.hop(m, h, i + h).start()

    def pass_first(self):
        self.forward(1, 0, 3)
        self.forward(2, 1, 3)

    def pass_second(self):
        self.forward(2, 0, 5)

    def finish(self):
        @pl.when(self.core == self.kind)
        def _():
            self.near.wait()
            self.hop(self.place, 1 - self.core, 3).wait_recv()

        @pl.when(self.core != self.kind)
        def _():
            self.first[2].wait_send()

        @pl.when(self.place == 0)
        def _():
            for h in range(2):
                self.hop(1, h, 3).wait_recv()

        @pl.when(self.place == 3)
        def _():
            for m in range(2):
                for h in range(2):
                    self.hop(m, h, 3).wait_recv()

        self.first[0].wait_send()

        @pl.when(self.start_place == 1)
        def _():
            self.first[1].wait_send()

        for place, m, i in ((1, 0, 3), (2, 1, 3), (2, 0, 5)):

            @pl.when(self.place == place)
            def _(m=m, i=i):
                for h in range(2):
                    self.hop(m, h, i + h).wait_send()


class PlaneSum:
    def __init__(self, src, keep, got, last, load_sem, send_sem, recv_sem):
        me, z = lax.axis_index("dp"), lax.axis_index("mp")
        self.x, self.y = lax.rem(me // 2, 2), lax.rem(me // 4, 2)
        self.z, self.across, self.along = z, toggled(me, 2), toggled(me, 4)
        self.src, self.keep, self.got, self.last = src, keep, got, last
        self.load_sem, self.send_sem, self.recv_sem = load_sem, send_sem, recv_sem

    def part(self, u, order, mine):
        x = self.x if mine else 1 - self.x
        y = self.y if mine else 1 - self.y
        return self.src.at[u, :, :, x, 0] if order == 0 else self.src.at[u, :, y, :, 1]

    def load(self, u, order):
        return pltpu.make_async_copy(
            self.part(u, order, True), self.keep.at[order, u], self.load_sem.at[order, u]
        )

    def hop(self, u, order, stage):
        if stage == 0:
            src, dst = self.part(u, order, False), self.got.at[order, u]
        else:
            there = 1 - (self.y if order == 0 else self.x)
            src, dst = self.keep.at[order, u, :, there], self.last.at[order, u]
        to = self.across if order == stage else self.along
        return remote(
            src, dst, self.send_sem.at[order, stage, u], self.recv_sem.at[order, stage, u], to, self.z
        )

    def begin(self, u):
        for order in range(2):
            self.load(u, order).start()
            self.hop(u, order, 0).start()

    def middle(self, u):
        for order in range(2):
            self.load(u, order).wait()
            self.hop(u, order, 0).wait_recv()
            total = self.keep[order, u].astype(f32) + self.got[order, u].astype(f32)
            self.keep[order, u] = total.astype(bf16)
            self.hop(u, order, 1).start()

    def end(self, u, put):
        for order in range(2):
            self.hop(u, order, 1).wait_recv()
            here = self.y if order == 0 else self.x
            total = self.keep[order, u, :, here].astype(f32) + self.last[order, u].astype(f32)
            put(u, order, total.astype(bf16))

    def drain(self, u):
        for order in range(2):
            for stage in range(2):
                self.hop(u, order, stage).wait_send()


class LineSum:
    def __init__(self, own, got, send_sem, recv_sem):
        self.me, self.z = lax.axis_index("dp"), lax.axis_index("mp")
        self.own, self.got, self.send_sem, self.recv_sem = own, got, send_sem, recv_sem

    def hop(self, way, t):
        entry = t if way == 0 else 3 - t
        return remote(
            self.own.at[entry], self.got.at[way, t - 1], self.send_sem.at[way, t - 1],
            self.recv_sem.at[way, t - 1], self.me, self.z + 1 - 2 * way,
        )

    def step(self, s, entry):
        for way in range(2):
            t = entry if way == 0 else 3 - entry
            if s >= t:
                continue

            @pl.when(self.z == (s if way == 0 else 3 - s))
            def _(way=way, t=t):
                if s > 0:
                    self.hop(way, t).wait_recv()
                    total = self.own[entry].astype(f32) + self.got[way, t - 1].astype(f32)
                    self.own[entry] = total.astype(bf16)
                self.hop(way, t).start()

    def finish(self, put):
        for way in range(2):
            for t in range(1, 4):

                @pl.when(self.z == (t if way == 0 else 3 - t))
                def _(way=way, t=t):
                    self.hop(way, t).wait_recv()
                    entry = t if way == 0 else 3 - t
                    total = self.own[entry].astype(f32) + self.got[way, t - 1].astype(f32)
                    self.own[entry] = total.astype(bf16)

        put(self.own[self.z])
        for way in range(2):
            for s in range(3):

                @pl.when(self.z == (s if way == 0 else 3 - s))
                def _(way=way, s=s):
                    for t in range(3, s, -1):
                        self.hop(way, t).wait_send()


class PlaneGather:
    def __init__(self, final, parts, rows, own_sem, send_sem, recv_sem):
        me, self.z = lax.axis_index("dp"), lax.axis_index("mp")
        self.core, self.col = lax.rem(me, 2), lax.rem(me // 2, 4)
        self.other, self.across, self.along = toggled(me, 1), toggled(me, 2), toggled(me, 4)
        self.parts, self.rows = parts, rows
        self.send_sem, self.recv_sem = send_sem, recv_sem
        self.cols = (
            self.col, toggled(self.col, 1), toggled(self.col, 2), toggled(toggled(self.col, 1), 2),
        )
        src = final.at[pl.ds(rows[0], rows[1]), :]
        self.near = pltpu.make_async_copy(src, self.slot(self.core, self.col), own_sem)
        self.hops = [
            self.hop(self.slot(self.core, self.col), 4, self.across, src),
            self.hop(self.slot(self.core, self.col), 5, self.along, src),
            self.hop(self.slot(self.core, self.col), 0, self.other, src),
        ]

    def slot(self, c, s, h=None):
        at, n = self.rows
        if h is not None:
            at, n = at + h * (n // 2), n // 2
        return self.parts.at[c, s, pl.ds(at, n), :]

    def hop(self, dst, i, to, src=None):
        src = dst if src is None else src
        return remote(src, dst, self.send_sem.at[i], self.recv_sem.at[i], to, self.z)

    def begin(self):
        for c in self.hops:
            c.start()
        self.near.start()

    def pass_on(self):
        for j, (i, ahead, h, k) in enumerate(((4, self.along, 0, 6), (5, self.across, 1, 7))):
            s = self.cols[1 + j]
            self.hop(self.slot(self.core, s), i, self.other).wait_recv()
            more = [
                self.hop(self.slot(self.core, s, h), k, ahead),
                self.hop(self.slot(self.core, s), 1 + j, self.other),
            ]
            for c in more:
                c.start()
            self.hops += more

    def finish(self):
        s = self.cols[3]
        for h in range(2):
            self.hop(self.slot(self.core, s, h), 6 + h, self.other).wait_recv()
        last = self.hop(self.slot(self.core, s), 3, self.other)
        last.start()
        self.near.wait()
        for i in range(4):
            self.hop(self.slot(1 - self.core, self.cols[i]), i, self.other).wait_recv()
        for c in self.hops + [last]:
            c.wait_send()


class SmallSum:
    def __init__(self, mine, pair, line, across, along, out, send_sem, recv_sem):
        me, self.z = lax.axis_index("dp"), lax.axis_index("mp")
        self.me, self.core = me, lax.rem(me, 2)
        self.x, self.y = lax.rem(me // 2, 2), lax.rem(me // 4, 2)
        self.mine, self.pair, self.line, self.a, self.b, self.out = mine, pair, line, across, along, out
        self.send_sem, self.recv_sem = send_sem, recv_sem
        n = pair.shape[1]
        self.n = n
        self.lanes = pl.ds(pl.multiple_of(self.core * n, n), n)
        there = pl.ds(pl.multiple_of((1 - self.core) * n, n), n)

        def move(src, dst, i, d, z):
            return remote(src, dst, send_sem.at[i], recv_sem.at[i], d, z)

        other = toggled(me, 1)
        self.swap = move(mine.at[:, there], pair, 0, other, self.z)
        slot = line.at[self.z]
        self.hops = [move(slot, slot, m, me, peer(self.z, m)) for m in (1, 2, 3)]
        self.hop_x = move(across.at[self.x], across.at[self.x], 4, toggled(me, 2), self.z)
        self.hop_y = move(along.at[self.y], along.at[self.y], 5, toggled(me, 4), self.z)
        done = out.at[:, self.lanes]
        self.last = move(done, done, 6, other, self.z)

    def begin(self):
        self.swap.start()

    def step_line(self, noise):
        n, width = self.n, noise.shape[1]
        self.swap.wait()
        self.line[self.z, :, 0:n] = self.mine[:, self.lanes] + self.pair[...]
        self.line[self.z, 16:24, n : n + width] = noise
        self.line[self.z, 0:16, n : n + width] = jnp.zeros((16, width), f32)
        for c in self.hops:
            c.start()

    def step_across(self):
        for c in self.hops:
            c.wait()
        v = [self.line[i] for i in range(4)]
        self.a[self.x, 0:16, :] = ((v[0] + v[1]) + (v[2] + v[3]))[0:16]
        for i in range(4):
            self.a[self.x, 16 + 8 * i : 24 + 8 * i, :] = v[i][16:24]
        self.hop_x.start()

    def step_along(self):
        self.hop_x.wait()
        self.b[self.y, 0:16, :] = self.a[0, 0:16, :] + self.a[1, 0:16, :]
        for i in range(2):
            self.b[self.y, 16 + 32 * i : 48 + 32 * i, :] = self.a[i, 16:48, :]
        self.hop_y.start()

    def step_out(self):
        self.hop_y.wait()
        n, n_time = self.n, self.out.shape[0] - 16
        self.out[n_time : n_time + 16, self.lanes] = self.b[0, 0:16, 0:n] + self.b[1, 0:16, 0:n]
        rows = jnp.concatenate([self.b[0, 16:80, :], self.b[1, 16:80, :]])
        grads, noise = rows[:, 0:n], rows[:, n : n + n_time].astype(bf16)
        high = grads.astype(bf16)
        rest = grads - high.astype(f32)
        middle = rest.astype(bf16)
        low = (rest - middle.astype(f32)).astype(bf16)
        total = contract(noise, high, 0, 0) + contract(noise, middle, 0, 0)
        self.out[0:n_time, self.lanes] = total + contract(noise, low, 0, 0)
        self.last.start()

    def finish(self):
        self.last.wait()


def one_hot(seg, copies):
    lanes = lax.broadcasted_iota(jnp.int32, (1, 128), 1)
    lanes = jnp.where(lanes < 16 * copies, lax.rem(lanes, 16), -1).astype(f32)
    return jnp.where(seg == lanes, 1.0, 0.0).astype(bf16)


def rotate_rows(v, cosine, sine):
    a, b = v[: HEAD // 2], v[HEAD // 2 :]
    return jnp.concatenate([a * cosine - b * sine, b * cosine + a * sine], axis=0)


def forward_kernel(
    act_any, cot_any, lens, noise, time_weight, time_bias, attn_gain, out_bias, mlp_gain, down_bias,
    qkv_bias, up_bias, qkv_any, ow_any, uw_any, dn_any,
    out_any, mid_any, gfin_any, acc_any, gp_any, wup_any, stream_any, normed_any, q_any, k_any, v_any, merged_any,
    lse_any, dwm_any, wqo_any, bias_rows, seg_col, trig, meta,
    w, x, gfin, bias, biases, stream, normed, qt, kt, vt, merged, lse, send, recv, mid, nm, act, gp,
    stage, lo, slopes, raw_qkv, acc,
    load_sem, bring_send, bring_recv, bias_send, bias_recv, w_send, w_recv,
    out_sem, stage_sem, send_sem, recv_sem,
):
    me, z = lax.axis_index("dp"), lax.axis_index("mp")
    core, col = lax.rem(me, 2), lax.rem(me // 2, 4)
    other, across, along = toggled(me, 1), toggled(me, 2), toggled(me, 4)
    here = act_any.shape[0] // BUCKET
    units = biases.shape[0]
    half = BUCKET // 2
    own, far = tile(core, half), tile(1 - core, half)
    mine = core == z // here
    up_at, dn_at, out_at = units * 512, units * 1024, units * 384

    def block(start, n):
        return pl.ds(pl.multiple_of(start, n), n)

    loads = [
        pltpu.make_async_copy(s, d, load_sem.at[i])
        for i, (s, d) in enumerate(
            (
                (qkv_any.at[:, :, block(core * 128, 128)], raw_qkv),
                (ow_any.at[block(core * 128, 128), :], w.at[block(out_at + z * 128, 128), :]),
                (uw_any.at[:, block(core * 512, 512)], nm.at[:, pl.ds(0, 512)]),
                (dn_any.at[block(core * 512, 512), :], w.at[block(dn_at + z * 512, 512), :]),
            )
        )
    ]
    for c in loads:
        c.start()
    greet([(other, z), (across, z), (along, z)] + [(me, peer(z, m)) for m in (1, 2, 3)])

    bucket_at = lax.rem(z, here)
    bucket = pl.ds(pl.multiple_of(bucket_at * BUCKET, BUCKET), BUCKET)
    brought = (
        (meta, meta),
        (act_any.at[bucket, :], x),
        (cot_any.at[bucket, :], gfin),
    )

    def bring(i, begin):
        src, dst = brought[i]
        near = None if i == 0 else pltpu.make_async_copy(src, dst, load_sem.at[4 + i])
        sent = remote(src, dst, bring_send.at[i], bring_recv.at[i], other, z)

        @pl.when(mine)
        def _():
            if begin:
                sent.start()
                if near is not None:
                    near.start()
            else:
                if near is not None:
                    near.wait()
                sent.wait_send()

        if not begin:

            @pl.when(jnp.logical_not(mine))
            def _():
                sent.wait_recv()

    def row_of(k, u, s):
        if k == 0:
            return u * 384 + 128 * s + (s // 3) * (out_at - 384 + 128 * u - 384 * u)
        return (up_at if k == 1 else dn_at) + u * 512 + 128 * s

    def diagonal(k, m):
        return k == 2 and m > 1

    far_col = toggled(toggled(col, 1), 2)

    def hop(k, m, way):
        i = 3 * k + m - 1
        u = peer(z, m)
        from_hbm = False
        if way == 0 or (way == 3 and diagonal(k, m)):
            s = col if way == 0 else far_col
            n, d = 128, me
            if m == 3:
                at, zz = row_of(k, peer(z, 2), s), peer(z, 1)
            else:
                at, zz, from_hbm = row_of(k, z, s), u, k == 2
        elif way == 1:
            at, n, d, zz = row_of(k, u, col), 128, across, z
        elif way == 2:
            at, n, d, zz = row_of(k, u, col), 128, along, z
        elif way == 3:
            at, n, d, zz = row_of(k, u, toggled(col, 1)), 64, along, z
        else:
            at, n, d, zz = row_of(k, u, toggled(col, 2)) + 64, 64, across, z
        rows = w.at[block(at, n), :]
        src = dn_any.at[block(core * 512 + s * 128, 128), :] if from_hbm else rows
        return remote(src, rows, w_send.at[i, way], w_recv.at[i, way], d, zz)

    def arrived(k, m, way):
        i = 3 * k + m - 1
        u = peer(z, m)
        s = (col, toggled(col, 1), toggled(col, 2), far_col, far_col)[way]
        at = row_of(k, u, s) + (64 if way == 4 else 0)
        rows = w.at[block(at, 128 if way < 3 or diagonal(k, m) else 64), :]
        remote(rows, rows, w_send.at[i, way], w_recv.at[i, way], other, z).wait_recv()

    def send_z(k, m):
        hop(k, m, 0).start()
        if diagonal(k, m):
            hop(k, m, 3).start()

    def pass_a(k, m):
        arrived(k, m, 0)
        if m == 2:
            hop(k, 3, 0).start()
        hop(k, m, 1).start()
        hop(k, m, 2).start()
        if m == 2 and diagonal(k, 3):
            arrived(k, m, 3)
            hop(k, 3, 3).start()

    def pass_b(k, m):
        arrived(k, m, 1)
        if not diagonal(k, m):
            hop(k, m, 3).start()
        arrived(k, m, 2)
        if not diagonal(k, m):
            hop(k, m, 4).start()

    def pass_c(k, m):
        if not (diagonal(k, m) and m == 2):
            arrived(k, m, 3)
        if not diagonal(k, m):
            arrived(k, m, 4)

    bring(1, True)
    for c in range(2):

        @pl.when(core == c)
        def _(c=c):
            bias[0:3, :] = qkv_bias[:, c * 128 : (c + 1) * 128]
            bias[3:4, :] = jnp.zeros((1, 128), f32)
            bias[4:8, :] = up_bias[c * 4 : (c + 1) * 4, :]

    biases[z] = bias[...]
    bias_hops = [
        remote(bias, biases.at[z], bias_send.at[m - 1], bias_recv.at[m - 1], me, peer(z, m))
        for m in (1, 2, 3)
    ]

    loads[0].wait()
    for i in range(3):
        w[block(z * 384 + i * 128, 128), :] = raw_qkv[i].T
    loads[1].wait()
    send_z(0, 1)

    @pl.when(mine)
    def _():
        places = lax.broadcasted_iota(jnp.int32, (1, BUCKET), 1)
        past, start, end = jnp.zeros_like(places), jnp.zeros_like(places), 0
        for i in range(SLOTS):
            end = end + lens[bucket_at * SLOTS + i]
            beyond = places >= end
            past = past + beyond.astype(jnp.int32)
            start = jnp.where(beyond, end, start)
        live = places < end
        meta[8:9, :] = jnp.where(live, past, 2000 + places).astype(f32)
        meta[9:10, :] = (places - jnp.where(live, start, 0)).astype(f32)
        rows = jnp.dot(noise[...], time_weight[...], preferred_element_type=f32) + time_bias[...]
        first = bucket_at == 0
        meta[0:8, :] = jnp.where(first, rows[0:SLOTS], rows[SLOTS : 2 * SLOTS])
        loud = noise[...].astype(f32)
        meta[16:24, 0 : loud.shape[1]] = jnp.where(first, loud[0:SLOTS], loud[SLOTS : 2 * SLOTS])

    bring(0, True)
    bring(2, True)
    for c in bias_hops:
        c.start()
    loads[2].wait()
    for i in range(4):
        w[block(up_at + z * 512 + i * 128, 128), :] = nm[:, i * 128 : (i + 1) * 128].T
    loads[3].wait()
    send_z(0, 2)

    saves = []

    def save(src, dst):
        c = pltpu.make_async_copy(src, dst, out_sem.at[len(saves)])
        c.start()
        saves.append(c)

    def swap(src, dst, i):
        c = remote(src, dst, send_sem.at[i], recv_sem.at[i], other, z)
        c.start()
        return c

    bring(0, False)
    seg_col[...] = jnp.broadcast_to(meta[8:9, :], (128, BUCKET)).T
    step = lax.broadcasted_iota(jnp.int32, (HEAD // 2, 1), 0).astype(f32)
    angles = jnp.exp(step * (-2.0 * math.log(10000.0) / HEAD)) * meta[9:10, :]
    trig[0:32, :] = jnp.cos(angles)
    trig[32:64, :] = jnp.sin(angles)
    pass_a(0, 1)
    send_z(1, 1)
    t_rows = meta[0:8, :]
    high = t_rows.astype(bf16).astype(f32)
    middle_part = (t_rows - high).astype(bf16).astype(f32)
    lowest = t_rows - high - middle_part
    gap = jnp.zeros((8, t_rows.shape[1]), f32)
    time_rows = jnp.concatenate(
        [high, gap, middle_part, gap, lowest, gap, jnp.zeros((80, t_rows.shape[1]), f32)]
    ).astype(bf16)
    bring(1, False)

    def enter(i):
        rs = tile(i, 256)
        added = jnp.dot(one_hot(seg_col[rs, :], 3), time_rows, preferred_element_type=f32)
        stream[rs, :] = x[rs, :].astype(f32) + added

    loop(4, enter)

    def norm(i):
        rs = tile(i, 128)
        centered, scale = row_stats(stream[rs, :])
        normed[rs, :] = (centered * scale * attn_gain[...]).astype(bf16)

    loop(8, norm)
    save(normed, normed_any)
    save(stream.at[own, :], stream_any)
    stream_saved = saves[-1]

    def bias_column(u, s):
        return jnp.broadcast_to(biases[u, s : s + 1, :], (128, 128)).T[:, 0:1]

    def unit(u, between):
        column = jnp.concatenate([bias_column(u, s) for s in range(3)], axis=0)
        proj = contract(w[block(u * 384, 384), :], normed[...], 1, 1) + column
        cs, sn = trig[0:32, :], trig[32:64, :]
        us = tile(u, 128)
        qt[us, :] = jnp.concatenate(
            [rotate_rows(proj[h * HEAD : (h + 1) * HEAD], cs, sn) for h in range(2)], axis=0
        ).astype(bf16)
        kt[us, :] = jnp.concatenate(
            [rotate_rows(proj[128 + h * HEAD : 128 + (h + 1) * HEAD], cs, sn) for h in range(2)],
            axis=0,
        ).astype(bf16)
        vt[us, :] = proj[256:384].astype(bf16)

        def head(j):
            h = 2 * u + j
            hs = tile(h, HEAD)
            keys = (kt[hs, :].astype(f32) * 0.125).T.astype(bf16)
            values = vt[hs, :]
            for t in range(2):
                cs_t = pl.ds(t * 512, 512)
                s = jnp.dot(keys, qt[hs, cs_t], preferred_element_type=f32)
                same = jnp.tile(seg_col[...], (1, 4)) == meta[8:9, cs_t]
                s = jnp.where(same, s, -1e30)
                top = jnp.max(s, axis=0, keepdims=True)
                p = jnp.exp(s - top)
                total = jnp.sum(p, axis=0, keepdims=True)
                o = jnp.dot(values, p.astype(bf16), preferred_element_type=f32)
                merged[hs, cs_t] = (o / total).astype(bf16)
                lse[h, :, cs_t] = top + jnp.log(total)

        for j in range(2):
            for step in between[j]:
                step[0](*step[1:])
            head(j)

    pass_a(0, 2)
    send_z(2, 1)
    for c in bias_hops:
        c.wait()
    unit(z, (((pass_b, 0, 1),), ((pass_a, 0, 3), (send_z, 1, 2))))
    pass_b(0, 2)
    pass_c(0, 1)
    unit(peer(z, 1), (((pass_a, 1, 1), (send_z, 2, 2)), ((pass_b, 0, 3), (pass_c, 0, 2))))
    unit(peer(z, 2), (((pass_a, 2, 1),), ((pass_b, 1, 1), (pass_c, 0, 3))))
    unit(peer(z, 3), (((pass_a, 1, 2), (pass_c, 1, 1)), ((pass_b, 2, 1),)))
    pass_a(2, 2)
    save(qt, q_any)
    save(kt, k_any)
    save(vt, v_any)
    save(merged, merged_any)
    save(lse, lse_any)
    save(w.at[pl.ds(0, up_at), :], wqo_any)

    w_out = w.at[pl.ds(out_at, units * 128), :]
    w_up = w.at[pl.ds(up_at, units * 512), :]
    w_dn = w.at[pl.ds(dn_at, units * 512), :]
    send[0] = contract(merged[:, far], w_out[...], 0, 0).astype(bf16)
    swap0 = swap(send.at[0], recv.at[0], 0)
    mid[...] = contract(merged[:, own], w_out[...], 0, 0)
    bring(2, False)

    def mask(i):
        rs = tile(i, 256)
        live = jnp.where(seg_col[rs, :][:, 0:1] < 1000.0, 1.0, 0.0)
        gfin[rs, :] = (gfin[rs, :].astype(f32) * live).astype(bf16)

    loop(4, mask)
    swap0.wait()

    def middle(i):
        rs = tile(i, 128)
        ro = pl.ds(pl.multiple_of(core * half + i * 128, 128), 128)
        v = stream[ro, :] + (mid[rs, :] + recv[0, rs, :].astype(f32)) + out_bias[...]
        mid[rs, :] = v
        centered, scale = row_stats(v)
        nm[ro, :] = (centered * scale * mlp_gain[...]).astype(bf16)

    loop(4, middle)
    save(mid, mid_any)
    save(gfin.at[own, :], gfin_any)
    swap1 = swap(nm.at[own, :], nm.at[own, :], 1)
    pass_c(2, 1)
    pass_b(1, 2)
    pass_a(1, 3)
    swap1.wait()

    def gelu_parts(u, rs):
        column = jnp.concatenate([bias_column(u, 4 + s) for s in range(4)], axis=0)
        pre = contract(w_up[tile(u, 512), :], nm[rs, :], 1, 1) + column
        sq = pre * pre
        th = jnp.tanh(pre * (0.7978845608028654 + (0.7978845608028654 * 0.044715) * sq))
        hp = 0.5 + 0.5 * th
        slope = hp + pre * (hp * (1.0 - th)) * (
            0.7978845608028654 + (3 * 0.7978845608028654 * 0.044715) * sq
        )
        return pre * hp, slope

    def hidden_unit(n, u):
        us = tile(u, 512)

        def hidden(t):
            rs = tile(t, 256)
            value, slope = gelu_parts(u, rs)
            act[us, rs] = value.astype(bf16)
            gp[us, rs] = (contract(w_dn[us, :], gfin[rs, :], 1, 1) * slope).astype(bf16)

        loop(4, hidden)

    def weight_part(n, u, i):
        us = tile(u, 512)
        if n > 0:
            pltpu.make_async_copy(stage.at[i], dwm_any.at[u, i], stage_sem.at[i]).wait()
        left, right = ((gp, nm), (act, gfin))[i]
        stage[i] = contract(left[us, :], right[...], 1, 0).astype(bf16)
        pltpu.make_async_copy(stage.at[i], dwm_any.at[u, i], stage_sem.at[i]).start()
        if i == 0:
            bias_rows[u, :, 384:896] = contract(jnp.ones((8, BUCKET), bf16), gp[us, :], 1, 1)

    def weights_unit(n, u):
        weight_part(n, u, 0)
        weight_part(n, u, 1)

    def partial_sums(n, u):
        us = tile(u, 512)
        for left, right, kept in ((act, w_dn, stream), (gp, w_up, acc)):
            for rows in (far, own):
                total = contract(left[us, rows], right[us, :], 0, 0)
                if n > 0:
                    total = total + kept[rows, :]
                kept[rows, :] = total

    bias_rows[...] = jnp.zeros_like(bias_rows)
    stream_saved.wait()
    hidden_unit(0, z)
    pass_c(1, 2)
    pass_b(2, 2)
    pass_a(2, 3)
    weights_unit(0, z)
    pass_c(2, 2)
    pass_b(1, 3)
    partial_sums(0, z)
    hidden_unit(1, peer(z, 1))
    pass_c(1, 3)
    pass_b(2, 3)
    weights_unit(1, peer(z, 1))
    partial_sums(1, peer(z, 1))
    hidden_unit(2, peer(z, 2))
    weights_unit(2, peer(z, 2))
    partial_sums(2, peer(z, 2))
    last_unit = peer(z, 3)
    us = tile(last_unit, 512)
    save(acc, acc_any)

    def last_values(t):
        rs = tile(t, 256)
        value, slope = gelu_parts(last_unit, rs)
        act[us, rs] = value.astype(bf16)
        slopes[:, rs] = slope

    def last_slopes(t):
        rs = tile(t, 256)
        gp[us, rs] = (contract(w_dn[us, :], gfin[rs, :], 1, 1) * slopes[:, rs]).astype(bf16)

    loop(4, last_values)
    save(w_up.at[us, :], wup_any)
    weight_part(3, last_unit, 1)
    pass_c(2, 3)
    send[1] = (stream[far, :] + contract(act[us, far], w_dn[us, :], 0, 0)).astype(bf16)
    swap2 = swap(send.at[1], recv.at[1], 2)
    loop(4, last_slopes)
    save(gp.at[us, :], gp_any)
    slopes[...] = stream[own, :] + contract(act[us, own], w_dn[us, :], 0, 0)
    swap2.wait()

    def finish(i):
        rs = tile(i, 128)
        ro = pl.ds(pl.multiple_of(core * half + i * 128, 128), 128)
        live = jnp.where(seg_col[ro, :][:, 0:1] < 1000.0, 1.0, 0.0)
        v = mid[rs, :] + (slopes[rs, :] + recv[1, rs, :].astype(f32)) + down_bias[...]
        lo[rs, :] = (live * v).astype(bf16)

    loop(4, finish)
    save(lo, out_any)
    weight_part(3, last_unit, 0)
    for i in range(2):
        pltpu.make_async_copy(stage.at[i], dwm_any.at[0, i], stage_sem.at[i]).wait()
    for c in saves:
        if c is not stream_saved:
            c.wait()
    for k in range(3):
        for m in (1, 2, 3):
            for way in range(4 if diagonal(k, m) else 5):
                hop(k, m, way).wait_send()


def column_devices(me, z):
    both = (me, toggled(me, 1))
    return [(both[1], z)] + [(d, peer(z, m)) for m in (1, 2, 3) for d in both]


def backward_kernel(
    gather,
    meta, seg_col, trig, attn_gain, mlp_gain, bias_rows, lse,
    wqo_any, mid_any, gfin_any, acc_any, gp_any, wup_any, stream_any, normed_any, q_any, k_any, v_any, merged_any, lo_any, dwm_any,
    out_any, dwa_any, gathered_any, parts, sums,
    wqo, mid, gfin, gmid, gm, stream, normed, qt, kt, vt, merged,
    gmerged, gproj, acck, accv, send, recv, gin, stage, gin_low, small, mine,
    keep_m, got_m, last_m, keep_a, got_a, last_a, own_m, line_got_m, own_a, line_got_a, final,
    small_pair, small_line, small_x, small_y,
    load_sem, stage_sem, send_sem, recv_sem, near_sem,
    lo_send, lo_recv, gin_send, gin_recv, pm_load, pm_send, pm_recv, pa_load, pa_send, pa_recv,
    lm_send, lm_recv, la_send, la_recv, gm_send, gm_recv, ga_send, ga_recv, small_send, small_recv,
):
    me, z = lax.axis_index("dp"), lax.axis_index("mp")
    core, other = lax.rem(me, 2), toggled(me, 1)
    half = BUCKET // 2
    units = wqo.shape[0] // 512
    n_qkv = units * 384
    w_qkv, w_out = pl.ds(0, n_qkv), pl.ds(n_qkv, units * 128)
    loads = {}
    for name, src, dst in (
        ("far", acc_any.at[tile(1 - core, half), :], gmid),
        ("gp", gp_any, gproj.at[pl.ds(0, 512), :]),
        ("up", wup_any, gproj.at[pl.ds(512, 512), :]),
        ("own", acc_any.at[tile(core, half), :], gin),
        ("mid", mid_any, mid),
        ("gfin", gfin_any, gfin),
        ("out", wqo_any.at[w_out, :], wqo.at[w_out, :]),
        ("q", q_any, qt),
        ("k", k_any, kt),
        ("v", v_any, vt),
        ("merged", merged_any, merged),
        ("qkv", wqo_any.at[w_qkv, :], wqo.at[w_qkv, :]),
        ("stream", stream_any, stream),
        ("normed", normed_any, normed),
    ):
        loads[name] = pltpu.make_async_copy(src, dst, load_sem.at[len(loads)])
        loads[name].start()
    wqkv, wout = wqo.at[w_qkv, :], wqo.at[w_out, :]
    cosine, sine = trig.at[pl.ds(0, 32), :], trig.at[pl.ds(32, 32), :]
    greet([(toggled(me, 2), z), (toggled(me, 4), z)] + column_devices(me, z))
    plane_m = PlaneSum(dwm_any, keep_m, got_m, last_m, pm_load, pm_send, pm_recv)
    spread_lo = Spread(lo_any, out_any, near_sem.at[0], lo_send, lo_recv)
    plane_m.begin(0)
    spread_lo.begin()
    plane_m.begin(3)

    def put_m(u, order, total):
        for i in range(2):
            own_m[u, i * 128 + order * 64 : i * 128 + (order + 1) * 64, :] = total[i]

    def put_a(u, order, total):
        own_a[u, order * 64 : (order + 1) * 64, :] = total[0]

    own = tile(core, half)
    far = tile(1 - core, half)
    gp_last, up_last = gproj.at[pl.ds(0, 512), :], gproj.at[pl.ds(512, 512), :]

    def swap(src, dst, i):
        c = remote(src, dst, send_sem.at[i], recv_sem.at[i], other, z)
        c.start()
        return c

    for name in ("far", "gp", "up"):
        loads[name].wait()
    send[...] = (gmid[...] + contract(gp_last[:, far], up_last[...], 0, 0)).astype(bf16)
    swap_in = swap(send, recv, 0)
    loads["own"].wait()
    gin[...] += contract(gp_last[:, own], up_last[...], 0, 0)
    loads["mid"].wait()
    loads["gfin"].wait()
    small[...] = jnp.zeros_like(small)
    swap_in.wait()

    def back_mlp(i):
        rs = tile(i, 128)
        ro = pl.ds(pl.multiple_of(core * half + i * 128, 128), 128)
        err = gin[rs, :] + recv[rs, :].astype(f32)
        grad, gain_grad = norm_back(mid[rs, :], mlp_gain[...], err)
        gf = gfin[rs, :].astype(f32)
        grad = grad + gf
        gmid[rs, :] = grad
        gm[ro, :] = grad.astype(bf16)
        small[0:1, :] += gain_grad
        small[1:2, :] += jnp.sum(grad, axis=0, keepdims=True)
        small[2:3, :] += jnp.sum(gf, axis=0, keepdims=True)

    loop(4, back_mlp)
    swap_gm = swap(gm.at[own, :], gm.at[own, :], 1)
    loads["out"].wait()
    swap_gm.wait()
    for t in range(2):
        cs = pl.ds(t * 512, 512)
        gmerged[:, cs] = contract(wout[...], gm[cs, :], 1, 1).astype(bf16)
    for name in ("q", "k", "v", "merged"):
        loads[name].wait()

    def head(h):
        hs = tile(h, HEAD)
        u = h // 2
        j = lax.rem(h, 2)
        at = u * 384 + j * HEAD
        keys_t = (kt[hs, :].astype(f32) * 0.125).astype(bf16)
        keys = keys_t.astype(f32).T.astype(bf16)
        values = vt[hs, :].astype(f32).T.astype(bf16)
        for t in range(4):
            cs = pl.ds(t * 256, 256)
            q, go = qt[hs, cs], gmerged[hs, cs]
            s = jnp.dot(keys, q, preferred_element_type=f32)
            same = jnp.tile(seg_col[...], (1, 2)) == meta[8:9, cs]
            p = jnp.exp(jnp.where(same, s, -1e30) - lse[h, :, cs])
            dp = jnp.dot(values, go, preferred_element_type=f32)
            ds = (p * (dp - jnp.sum(p * dp, axis=0, keepdims=True))).astype(bf16)
            dq = jnp.dot(keys_t, ds, preferred_element_type=f32)
            gproj[pl.ds(pl.multiple_of(at, HEAD), HEAD), cs] = rotate_rows(
                dq, cosine[:, cs], -sine[:, cs]
            ).astype(bf16)
            dv = contract(go, p.astype(bf16), 1, 1)
            dk = contract(q, ds, 1, 1)
            if t == 0:
                accv[...] = dv
                acck[...] = dk
            elif t < 3:
                accv[...] += dv
                acck[...] += dk
            else:
                dk = (acck[...] + dk) * 0.125
                gproj[pl.ds(pl.multiple_of(at + 128, HEAD), HEAD), :] = rotate_rows(
                    dk, cosine[...], -sine[...]
                ).astype(bf16)
                gproj[pl.ds(pl.multiple_of(at + 256, HEAD), HEAD), :] = (accv[...] + dv).astype(bf16)

    def heads(i):
        head(2 * i)
        head(2 * i + 1)

        @pl.when(i == 1)
        def _():
            plane_m.middle(0)
            plane_m.begin(1)
            spread_lo.pass_first()

        @pl.when(i == 2)
        def _():
            plane_m.middle(3)
            plane_m.begin(2)

    loop(units, heads)
    line_m = LineSum(own_m, line_got_m, lm_send, lm_recv)
    line_a = LineSum(own_a, line_got_a, la_send, la_recv)
    plane_m.end(0, put_m)
    line_m.step(0, 0)
    loads["qkv"].wait()
    send[...] = contract(gproj[:, far], wqkv[...], 0, 0).astype(bf16)
    swap_out = swap(send, recv, 2)
    gin[...] = contract(gproj[:, own], wqkv[...], 0, 0)
    loads["stream"].wait()
    swap_out.wait()

    def back(i):
        rs = tile(i, 128)
        ro = pl.ds(pl.multiple_of(core * half + i * 128, 128), 128)
        err = gin[rs, :] + recv[rs, :].astype(f32)
        grad, gain_grad = norm_back(stream[rs, :], attn_gain[...], err)
        grad = grad + gmid[rs, :]
        high = grad.astype(bf16)
        gin_low[rs, :] = high
        small[3:4, :] += gain_grad
        member = one_hot(seg_col[ro, :], 1)
        low = (grad - high.astype(f32)).astype(bf16)
        small[8:16, :] += (contract(member, high, 0, 0) + contract(member, low, 0, 0))[0:8]

    loop(4, back)
    spread_gin = Spread(gin_low, gathered_any, near_sem.at[1], gin_send, gin_recv)
    spread_gin.begin()
    plane_m.end(3, put_m)
    line_m.step(0, 3)
    line_m.step(1, 0)
    t_rows = small[8:16, :]
    mine[0:8, :] = jnp.concatenate(
        [
            small[0:4, :],
            jnp.sum(t_rows, axis=0, keepdims=True),
            jnp.zeros((3, t_rows.shape[1]), f32),
        ]
    )
    mine[8:16, :] = jnp.zeros((8, t_rows.shape[1]), f32)
    mine[16:24, :] = t_rows
    loads["normed"].wait()
    plane_a = PlaneSum(dwa_any, keep_a, got_a, last_a, pa_load, pa_send, pa_recv)
    order = (0, 3, 1, 2)

    def stored(i):
        return pltpu.make_async_copy(stage.at[i % 2], dwa_any.at[order[i]], stage_sem.at[i % 2])

    def weights(i):
        u = order[i]
        us = pl.ds(u * 384, 384)
        if i > 1:
            stored(i - 2).wait()
            plane_a.begin(order[i - 2])
        of_qkv = contract(gproj[us, :], normed[...], 1, 0).astype(bf16)
        of_out = contract(merged[pl.ds(u * 128, 128), :], gm[...], 1, 0).astype(bf16)
        for k in range(4):
            quarter = of_qkv[k * 128 : (k + 1) * 128] if k < 3 else of_out
            for j in range(2):
                stage[i % 2, 0, k // 2, k % 2, j] = quarter[j * 64 : (j + 1) * 64]
        stored(i).start()
        row = lax.broadcasted_iota(jnp.int32, (8, 1), 0) == core * units + u
        mine[8:16, 0:384] += jnp.where(
            row, contract(jnp.ones((8, BUCKET), bf16), gproj[us, :], 1, 1), 0.0
        )
        mine[8:16, 384:896] += jnp.where(row, bias_rows[u, :, 384:896], 0.0)

    little = SmallSum(mine, small_pair, small_line, small_x, small_y, sums, small_send, small_recv)

    def put_final_m(total):
        final[128:384, :] = total

    def put_final_a(total):
        final[0:128, :] = total

    if gather:
        gather_m = PlaneGather(final, parts, (128, 256), near_sem.at[2, 0], gm_send, gm_recv)
        gather_a = PlaneGather(final, parts, (0, 128), near_sem.at[3, 0], ga_send, ga_recv)
    weights(0)
    weights(1)
    plane_m.middle(1)
    spread_lo.pass_second()
    weights(2)
    weights(3)
    little.begin()
    line_m.step(1, 3)
    line_m.step(2, 0)
    plane_m.middle(2)
    for i in (2, 3):
        stored(i).wait()
        plane_a.begin(order[i])
    plane_m.end(1, put_m)
    line_m.step(0, 1)
    line_m.step(2, 3)
    little.step_line(meta[16:24, 0 : sums.shape[0] - 16])
    plane_m.end(2, put_m)
    line_m.step(0, 2)
    line_m.step(1, 1)
    spread_gin.pass_first()
    line_m.step(1, 2)
    plane_a.middle(0)
    plane_a.middle(3)
    little.step_across()
    plane_a.middle(1)
    plane_a.middle(2)
    line_m.finish(put_final_m)
    little.step_along()
    if gather:
        gather_m.begin()
    plane_a.end(0, put_a)
    line_a.step(0, 0)
    plane_a.end(3, put_a)
    line_a.step(0, 3)
    line_a.step(1, 0)
    plane_a.end(1, put_a)
    line_a.step(0, 1)
    line_a.step(1, 3)
    plane_a.end(2, put_a)
    line_a.step(0, 2)
    line_a.step(1, 1)
    line_a.step(1, 2)
    line_a.step(2, 0)
    line_a.step(2, 3)
    spread_gin.pass_second()
    if gather:
        gather_m.pass_on()
    line_a.finish(put_final_a)
    if gather:
        gather_a.begin()
        little.step_out()
        gather_a.pass_on()
        gather_m.finish()
        gather_a.finish()
    else:
        little.step_out()
        out = pltpu.make_async_copy(final, parts, near_sem.at[2, 0])
        out.start()
        out.wait()
    little.finish()
    spread_lo.finish()
    spread_gin.finish()
    for u in range(4):
        plane_m.drain(u)
        plane_a.drain(u)


def deliver_kernel(
    parts, gin, lo, sums, little, grad_in, lo_out, time_out, qkv_out, out_out, up_out, down_out,
    gain_m, out_bias, down_bias, gain_a, time_bias, qkv_bias, up_bias,
):
    s = lax.rem(pl.program_id(0), 4)

    @pl.when(pl.program_id(0) == 0)
    def _():
        for i, ref in enumerate((gain_m, out_bias, down_bias, gain_a, time_bias)):
            ref[...] = little[i : i + 1, :]
        units = 4
        rows = lax.broadcasted_iota(jnp.int32, (8, 1), 0)
        for c in range(2):
            here = rows == c * units + lax.axis_index("mp")
            mine = jnp.sum(jnp.where(here, little[8:16, :], 0.0), axis=0, keepdims=True)
            for i in range(3):
                qkv_bias[i : i + 1, c * 128 : (c + 1) * 128] = mine[:, i * 128 : (i + 1) * 128]
            up_bias[:, c * 512 : (c + 1) * 512] = mine[:, 384:896]

    grad_in[...] = gin[...].astype(f32)
    lo_out[...] = lo[...]
    time_out[...] = sums[...]
    down_out[...] = parts[0, 0, 256:384, :].astype(f32)
    up_out[...] = parts[0, 0, 128:256, :].T.astype(f32)

    @pl.when(s < 3)
    def _():
        qkv_out[0] = parts[0, 0, 0:128, :].T.astype(f32)

    @pl.when(s == 3)
    def _():
        out_out[...] = parts[0, 0, 0:128, :].astype(f32)


def shape(s, t):
    return jax.ShapeDtypeStruct(s, t)


def run_forward(args, here, units, width):
    rows = BUCKET
    half = rows // 2
    feat = units * 128
    hid = units * 512
    anyspec = pl.BlockSpec(memory_space=pl.ANY)
    vm = pl.BlockSpec(memory_space=VMEM)
    outs = (
        shape((half, width), bf16),
        shape((half, width), f32),
        shape((half, width), bf16),
        shape((rows, width), f32),
        shape((512, width), bf16),
        shape((512, width), bf16),
        shape((half, width), f32),
        shape((rows, width), bf16),
        shape((feat, rows), bf16),
        shape((feat, rows), bf16),
        shape((feat, rows), bf16),
        shape((feat, rows), bf16),
        shape((2 * units, 1, rows), f32),
        shape((units, 2, 512, width), bf16),
        shape((hid, width), bf16),
        shape((units, 8, width), f32),
        shape((rows, 128), f32),
        shape((64, rows), f32),
        shape((24, width), f32),
    )
    dma = pltpu.SemaphoreType.DMA
    return pl.pallas_call(
        forward_kernel,
        out_shape=outs,
        in_specs=[anyspec] * 2 + [pl.BlockSpec(memory_space=pltpu.SMEM)] + [vm] * 9 + [anyspec] * 4,
        out_specs=[anyspec] * 15 + [vm] * 4,
        scratch_shapes=[
            VMEM((3 * hid, width), bf16),
            VMEM((rows, width), bf16),
            VMEM((rows, width), bf16),
            VMEM((8, 128), f32),
            VMEM((units, 8, 128), f32),
            VMEM((rows, width), f32),
            VMEM((rows, width), bf16),
            VMEM((feat, rows), bf16),
            VMEM((feat, rows), bf16),
            VMEM((feat, rows), bf16),
            VMEM((feat, rows), bf16),
            VMEM((2 * units, 1, rows), f32),
            VMEM((2, half, width), bf16),
            VMEM((2, half, width), bf16),
            VMEM((half, width), f32),
            VMEM((rows, width), bf16),
            VMEM((hid, rows), bf16),
            VMEM((hid, rows), bf16),
            VMEM((2, 512, width), bf16),
            VMEM((half, width), bf16),
            VMEM((half, width), f32),
            VMEM((3, width, 128), bf16),
            VMEM((rows, width), f32),
            dma((7,)),
            dma((3,)),
            dma((3,)),
            dma((3,)),
            dma((3,)),
            dma((9, 5)),
            dma((9, 5)),
            dma((16,)),
            dma((2,)),
            dma((3,)),
            dma((3,)),
        ],
        compiler_params=pltpu.CompilerParams(
            collective_id=0, has_side_effects=True, vmem_limit_bytes=63 * MIB
        ),
        name="forward",
    )(*args)


def run_backward(args, gather, here, units, rows, width, n_time):
    half = rows // 2
    feat = units * 128
    anyspec = pl.BlockSpec(memory_space=pl.ANY)
    vm = pl.BlockSpec(memory_space=VMEM)
    dma = pltpu.SemaphoreType.DMA
    return pl.pallas_call(
        functools.partial(backward_kernel, gather),
        out_shape=(
            shape((here * rows, width), bf16),
            shape((units, 1, 2, 2, 2, 64, width), bf16),
            shape((here * rows, width), bf16),
            shape((2, 4, 384, width) if gather else (384, width), bf16),
            shape((n_time + 16, width), f32),
        ),
        in_specs=[vm] * 7 + [anyspec] * (len(args) - 7),
        out_specs=[anyspec] * 4 + [vm],
        scratch_shapes=[
            VMEM((4 * feat, width), bf16),
            VMEM((half, width), f32),
            VMEM((half, width), bf16),
            VMEM((half, width), f32),
            VMEM((rows, width), bf16),
            VMEM((half, width), f32),
            VMEM((rows, width), bf16),
            VMEM((feat, rows), bf16),
            VMEM((feat, rows), bf16),
            VMEM((feat, rows), bf16),
            VMEM((feat, rows), bf16),
            VMEM((feat, rows), bf16),
            VMEM((3 * feat, rows), bf16),
            VMEM((HEAD, rows), f32),
            VMEM((HEAD, rows), f32),
            VMEM((half, width), bf16),
            VMEM((half, width), bf16),
            VMEM((half, width), f32),
            VMEM((2, 1, 2, 2, 2, 64, width), bf16),
            VMEM((half, width), bf16),
            VMEM((16, width), f32),
            VMEM((24, width), f32),
            VMEM((2, units, 2, 2, 64, width), bf16),
            VMEM((2, units, 2, 2, 64, width), bf16),
            VMEM((2, units, 2, 64, width), bf16),
            VMEM((2, units, 1, 2, 64, width), bf16),
            VMEM((2, units, 1, 2, 64, width), bf16),
            VMEM((2, units, 1, 64, width), bf16),
            VMEM((units, 256, width), bf16),
            VMEM((2, 3, 256, width), bf16),
            VMEM((units, 128, width), bf16),
            VMEM((2, 3, 128, width), bf16),
            VMEM((384, width), bf16),
            VMEM((24, width // 2), f32),
            VMEM((4, 24, width // 2 + n_time), f32),
            VMEM((2, 48, width // 2 + n_time), f32),
            VMEM((2, 80, width // 2 + n_time), f32),
            dma((14,)),
            dma((2,)),
            dma((3,)),
            dma((3,)),
            dma((4, 1)),
            dma((7,)),
            dma((4,)),
            dma((7,)),
            dma((4,)),
            dma((2, units)),
            dma((2, 2, units)),
            dma((2, 2, units)),
            dma((2, units)),
            dma((2, 2, units)),
            dma((2, 2, units)),
            dma((2, 3)),
            dma((2, 3)),
            dma((2, 3)),
            dma((2, 3)),
            dma((8,)),
            dma((8,)),
            dma((8,)),
            dma((8,)),
            dma((7,)),
            dma((7,)),
        ],
        compiler_params=pltpu.CompilerParams(
            collective_id=1, has_side_effects=True, vmem_limit_bytes=63 * MIB
        ),
        name="backward",
    )(*args)


def run_deliver(parts, gin, lo, sums, n_time):
    rows, width = gin.shape
    steps = 8
    part = parts.shape[2] // 3
    hid = steps * part
    at = lambda i: (i, 0)
    return pl.pallas_call(
        deliver_kernel,
        grid=(steps,),
        out_shape=(
            shape((rows, width), f32),
            shape((rows, width), bf16),
            shape((n_time, width), f32),
            shape((3, width, 2 * part), f32),
            shape((2 * part, width), f32),
            shape((width, hid), f32),
            shape((hid, width), f32),
            *(shape((1, width), f32) for _ in range(5)),
            shape((3, 2 * part), f32),
            shape((1, hid), f32),
        ),
        in_specs=[
            pl.BlockSpec((1, 1, 3 * part, width), lambda i: (i // 4, i % 4, 0, 0)),
            pl.BlockSpec((rows // steps, width), at),
            pl.BlockSpec((rows // steps, width), at),
            pl.BlockSpec((n_time // steps, width), at),
            pl.BlockSpec((16, width), lambda i: (n_time // 16, 0)),
        ],
        out_specs=[
            pl.BlockSpec((rows // steps, width), at),
            pl.BlockSpec((rows // steps, width), at),
            pl.BlockSpec((n_time // steps, width), at),
            pl.BlockSpec((1, width, part), lambda i: (jnp.minimum(i % 4, 2), 0, i // 4)),
            pl.BlockSpec((part, width), lambda i: (i // 4, 0)),
            pl.BlockSpec((width, part), lambda i: (0, i)),
            pl.BlockSpec((part, width), at),
            *(pl.BlockSpec((1, width), lambda i: (0, 0)) for _ in range(5)),
            pl.BlockSpec((3, 2 * part), lambda i: (0, 0)),
            pl.BlockSpec((1, hid), lambda i: (0, 0)),
        ],
        compiler_params=pltpu.CompilerParams(vmem_limit_bytes=63 * MIB),
        name="deliver",
    )(parts, gin, lo, sums, sums)


def local(
    ndp, nmp, activations, noise_embed, lengths, time_weight, time_bias, attn_gain, qkv_weight, qkv_bias,
    out_weight, out_bias, mlp_gain, up_weight, up_bias, down_weight, down_bias, cotangent,
):
    width = activations.shape[1]
    here = activations.shape[0] // BUCKET
    assert 2 * here == nmp and qkv_weight.shape[2] == 256 and up_weight.shape[1] == 1024
    assert ndp % 8 == 0 and noise_embed.shape[0] == here * SLOTS
    n_time = time_weight.shape[0]
    def row(v):
        return v.reshape(1, width)

    (
        lo, mid, gfin, acc, gp, wup, stream, normed, qt, kt, vt, merged, lse, dwm, wqo, bias_rows, seg_col, trig, meta,
    ) = run_forward(
        (
            activations, cotangent, lengths, noise_embed, time_weight, row(time_bias), row(attn_gain),
            row(out_bias), row(mlp_gain), row(down_bias), qkv_bias, up_bias.reshape(8, 128),
            qkv_weight.transpose(1, 0, 2), out_weight, up_weight, down_weight,
        ),
        here, nmp, width,
    )
    gather = ndp == 8
    lo_all, _, gathered, parts, sums = run_backward(
        (
            meta, seg_col, trig, row(attn_gain), row(mlp_gain), bias_rows, lse, wqo, mid, gfin, acc, gp, wup, stream,
            normed, qt, kt, vt,
            merged, lo, dwm.reshape(nmp, 2, 2, 2, 2, 64, width),
        ),
        gather, here, nmp, BUCKET, width, n_time,
    )
    if not gather:
        groups = [[i + 8 * k for k in range(ndp // 8)] for i in range(8)]
        parts = lax.psum(parts, "dp", axis_index_groups=groups)
        sums = lax.psum(sums, "dp", axis_index_groups=groups)
        groups = [[8 * k + i for i in range(8)] for k in range(ndp // 8)]
        parts = lax.all_gather(parts, "dp", axis_index_groups=groups)
        parts = parts.reshape(4, 2, 384, width).transpose(1, 0, 2, 3)
    (
        grad_input, layer_output, grad_time_weight, grad_qkv, grad_out, grad_up, grad_down,
        grad_mlp_gain, grad_out_bias, grad_down_bias, grad_attn_gain, grad_time_bias, grad_qkv_bias, grad_up_bias,
    ) = run_deliver(parts, gathered, lo_all, sums, n_time)
    grad_qkv = grad_qkv.transpose(1, 0, 2)
    return (
        layer_output,
        grad_input,
        grad_time_weight,
        grad_time_bias.reshape(-1),
        grad_attn_gain.reshape(-1),
        grad_qkv,
        grad_qkv_bias,
        grad_out,
        grad_out_bias.reshape(-1),
        grad_mlp_gain.reshape(-1),
        grad_up,
        grad_up_bias.reshape(-1),
        grad_down,
        grad_down_bias.reshape(-1),
    )


def solution(mesh):
    in_specs = (
        P("dp", None),
        P("dp", None),
        P("dp"),
        P(),
        P(),
        P(),
        P(None, None, "mp"),
        P(None, "mp"),
        P("mp", None),
        P(),
        P(),
        P(None, "mp"),
        P("mp"),
        P("mp", None),
        P(),
        P("dp", None),
    )
    out_specs = (
        P("dp", None),
        P("dp", None),
        P(),
        P(),
        P(),
        P(None, None, "mp"),
        P(None, "mp"),
        P("mp", None),
        P(),
        P(),
        P(None, "mp"),
        P("mp"),
        P("mp", None),
        P(),
    )
    body = functools.partial(local, mesh.shape["dp"], mesh.shape["mp"])
    return jax.shard_map(body, mesh=mesh, in_specs=in_specs, out_specs=out_specs, check_vma=False)
```
